32 devices in a mesh: dp: 4 (over y, x), ctx: 8 (over z, core).
Axes of the slice: x: 2, y: 2, z: 4, core: 2. Of those that a mesh axis runs over, the one named last changes fastest.
Arguments:
- tokens: bfloat16 [8, 1024, 1024], P('dp', 'ctx'), may hold values from -6 to 6
- teacher: bfloat16 [8, 1024, 1024], P('dp', 'ctx'), may hold values from -6 to 6
- segments: int32 [8, 1024], P('dp'), may hold values from 0 to 13, as said below
- positions: int32 [8, 1024], P('dp', 'ctx'), may hold values from 0 to 639, as said below
- valid_mask: int32 [8, 1024], P('dp', 'ctx'), may hold values from 0 to 1, as said below
- norm_gain: bfloat16 [1024], P(('dp', 'ctx')), may hold values from 0.25 to 1.75
- norm_bias: bfloat16 [1024], P(('dp', 'ctx')), may hold values from -1.1953125 to 1.1953125
- qkv_weight: bfloat16 [1024, 3072], P(('dp', 'ctx')), may hold values from -0.1875 to 0.1875
- qkv_bias: bfloat16 [3072], P(('dp', 'ctx')), may hold values from -1.1953125 to 1.1953125
- proj_weight: bfloat16 [1024, 1024], P(('dp', 'ctx')), may hold values from -1 to 1
- proj_bias: bfloat16 [1024], P(('dp', 'ctx')), may hold values from -1.1953125 to 1.1953125
- up_weight: bfloat16 [1024, 4096], P(('dp', 'ctx')), may hold values from -0.1875 to 0.1875
- up_bias: bfloat16 [4096], P(('dp', 'ctx')), may hold values from -1.1953125 to 1.1953125
- down_weight: bfloat16 [4096, 1024], P(('dp', 'ctx')), may hold values from -0.09375 to 0.09375
- down_bias: bfloat16 [1024], P(('dp', 'ctx')), may hold values from -1.1953125 to 1.1953125
Outputs:
- layer_out: bfloat16 [8, 1024, 1024], P('dp', 'ctx')
- loss: float32 [], replicated
- input_grad: bfloat16 [8, 1024, 1024], P('dp', 'ctx')
- norm_gain_grad: float32 [1024], P(('dp', 'ctx'))
- norm_bias_grad: float32 [1024], P(('dp', 'ctx'))
- qkv_weight_grad: float32 [1024, 3072], P(('dp', 'ctx'))
- query_key_bias_grad: float32 [2048], P(('dp', 'ctx'))
- value_bias_grad: float32 [1024], P(('dp', 'ctx'))
- proj_weight_grad: float32 [1024, 1024], P(('dp', 'ctx'))
- proj_bias_grad: float32 [1024], P(('dp', 'ctx'))
- up_weight_grad: float32 [1024, 4096], P(('dp', 'ctx'))
- up_bias_grad: float32 [4096], P(('dp', 'ctx'))
- down_weight_grad: float32 [4096, 1024], P(('dp', 'ctx'))
- down_bias_grad: float32 [1024], P(('dp', 'ctx'))
The draws below stay inside these ranges and needn't reach their ends.
Inputs may be any that keep to these rules, and one draw needn't show every extreme that they name: `segments`: along each sequence the segment numbers start at 0 on its first token, rise by one at the first token of each next document and never fall. The first document of every sequence has exactly 640 tokens; every document but the last of a sequence has 30 tokens or more (the sequence's end may cut the last one short); in one sequence every document after the first, except perhaps its last, has exactly 30 tokens. `positions`: A token's position within its document: 0 at a document's first token, one more at each following token of the same document. `valid_mask`: the first token of every sequence is marked 1.
All inputs are finite; a program needn't handle non-finite values.
Results may differ from the reference program's by a relative error of at most 0.01.
Values may be sent and summed in bfloat16 or wider, within the bound.
No kernel may reach another device: no remote copies, remote signals or barrier semaphores. Data moves between devices by JAX's collectives and lax.ppermute only.
A program may use at most 256 MiB of HBM per device.

```python
import math
import jax
import jax.numpy as jnp
from jax import lax

D = 1024
HEADS = 16
FF = 4096
ROT = 16
LOCAL_TOK = 128
LENGTH = 1024
SEQS = 8
TOKENS = 8192


def document_layout(key):
    layout_key = jax.random.fold_in(key, 11)
    short_len = max(4, 60 * LENGTH // 2048)
    first_len = max(short_len + 1, LENGTH // 2 + LOCAL_TOK)
    other_top = max(short_len + 1, 800 * LENGTH // 2048)
    doc_slots = LENGTH // short_len + 2
    lengths = jax.random.randint(layout_key, (SEQS, doc_slots), short_len, other_top + 1, dtype=jnp.int32)
    slot_place = jnp.arange(doc_slots, dtype=jnp.int32)[None, :]
    seq_place = jnp.arange(SEQS, dtype=jnp.int32)[:, None]
    lengths = jnp.where(seq_place == 0, jnp.full_like(lengths, short_len), lengths)
    lengths = jnp.where(slot_place == 0, jnp.full_like(lengths, first_len), lengths).astype(jnp.int32)
    doc_ends = jnp.cumsum(lengths, axis=1).astype(jnp.int32)
    token_place = jnp.arange(LENGTH, dtype=jnp.int32)
    seg_ids = jnp.sum((doc_ends[:, None, :] <= token_place[None, :, None]).astype(jnp.int32), axis=2).astype(jnp.int32)
    doc_starts = doc_ends - lengths
    start_of = jnp.take_along_axis(doc_starts, seg_ids, axis=1)
    return (seg_ids, (token_place[None, :] - start_of).astype(jnp.int32))


def draw_segments(key, part):
    return document_layout(key)[0]


def draw_positions(key, part):
    return document_layout(key)[1]


def draw_valid_mask(key, part):
    mask_key = jax.random.fold_in(key, 23)
    token_place = jnp.arange(LENGTH, dtype=jnp.int32)[None, :]
    seq_place = jnp.arange(SEQS, dtype=jnp.int32)[:, None]
    ranking = seq_place * LENGTH + token_place
    threshold = 200 + 600 * ranking // (SEQS * LENGTH)
    rolls = jax.random.randint(mask_key, (SEQS, LENGTH), 0, 1000, dtype=jnp.int32)
    chosen = (rolls < threshold).astype(jnp.int32)
    return jnp.where(token_place == 0, jnp.ones_like(chosen), chosen).astype(jnp.int32)


def block_levels(own_key, shape, split, smallest, high):
    factor_of = 1.0
    for axis_at, parts in split:
        draws = jax.random.uniform(jax.random.fold_in(jax.random.fold_in(own_key, 6), axis_at), (parts,), jnp.float32, smallest / len(split), high / len(split))
        factor_of = factor_of * jnp.repeat(jnp.exp(draws), shape[axis_at] // parts).reshape((-1,) + (1,) * (len(shape) - 1 - axis_at))
    return factor_of


def centred(own_key, dims, width, reach, shards=(), kind=jnp.bfloat16):
    array = width * jax.random.normal(own_key, dims, jnp.float32)
    if shards:
        array = array * block_levels(own_key, dims, shards, -0.22, 0.18)
    return jnp.clip(array, -reach, reach).astype(kind)


def setup_inputs(seed: int = 0) -> dict:
    key_list = jax.random.split(jax.random.key(seed), 16)
    return {
        "tokens": centred(key_list[0], (SEQS, LENGTH, D), 1.0, 6.0, ((0, 4), (1, 8))),
        "teacher": centred(key_list[1], (SEQS, LENGTH, D), 1.0, 6.0, ((0, 4), (1, 8))),
        "segments": draw_segments(jax.random.fold_in(key_list[15], 71), 0),
        "positions": draw_positions(jax.random.fold_in(key_list[15], 71), 0),
        "valid_mask": draw_valid_mask(jax.random.fold_in(key_list[15], 71), 0),
        "norm_gain": jnp.clip(1.0 + 0.15 * jax.random.normal(key_list[5], (D,), jnp.float32), 0.25, 1.75).astype(jnp.bfloat16),
        "norm_bias": centred(key_list[6], (D,), 0.2, 1.1953125, ((0, 32),)),
        "qkv_weight": centred(key_list[7], (D, 3 * D), D ** -0.5, 0.1875, ((0, 32),)),
        "qkv_bias": centred(key_list[8], (3 * D,), 0.2, 1.1953125, ((0, 32),)),
        "proj_weight": centred(key_list[9], (D, D), (D // 32) ** -0.5, 1.0, ((0, 32),)),
        "proj_bias": centred(key_list[10], (D,), 0.2, 1.1953125, ((0, 32),)),
        "up_weight": centred(key_list[11], (D, FF), D ** -0.5, 0.1875, ((0, 32),)),
        "up_bias": centred(key_list[12], (FF,), 0.2, 1.1953125, ((0, 32),)),
        "down_weight": centred(key_list[13], (FF, D), FF ** -0.5, 0.09375, ((0, 32),)),
        "down_bias": centred(key_list[14], (D,), 0.2, 1.1953125, ((0, 32),)),
    }


@jax.custom_vjp
def low(v):
    return lax.optimization_barrier(v.astype(jnp.bfloat16)).astype(jnp.float32)

@jax.custom_vjp
def low_back(v):
    return v

def low_keep(v):
    return (low(v), None)

def low_pass(kept, grad):
    return (grad,)

def back_keep(v):
    return (v, None)

def back_low(kept, grad):
    return (low(grad),)
low.defvjp(low_keep, low_pass)
low_back.defvjp(back_keep, back_low)
HIGHEST_PREC = lax.Precision.HIGHEST
NEG_FILL = -1000000000.0

def rotary_tables(places, rot_dims):
    half_dims = rot_dims // 2
    freq_steps = jnp.arange(half_dims, dtype=jnp.float32)
    inverse = jnp.power(10000.0, -2.0 * freq_steps / rot_dims)
    angles = places.astype(jnp.float32)[:, None] * inverse[None, :]
    return (jnp.cos(angles)[:, None, :], jnp.sin(angles)[:, None, :])

def rotate(heads_in, cosine, sine_table, rot_dims):
    half_dims = rot_dims // 2
    first_half = heads_in[..., :half_dims]
    second_half = heads_in[..., half_dims:rot_dims]
    return jnp.concatenate([first_half * cosine - second_half * sine_table, second_half * cosine + first_half * sine_table, heads_in[..., rot_dims:]], axis=-1)

def layer_norm(rows_in, norm_gain, norm_bias):
    row_mean = lax.optimization_barrier(jnp.mean(rows_in, axis=-1, keepdims=True))
    centered = rows_in - row_mean
    variance = lax.optimization_barrier(jnp.mean(centered * centered, axis=-1, keepdims=True))
    return centered * lax.rsqrt(variance + 1e-05) * norm_gain + norm_bias

def attention(query_rows, key_rows, value_rows, seg_ids, score_scale):
    length = query_rows.shape[0]
    block_rows = math.gcd(length, 512)
    places = jnp.arange(length, dtype=jnp.int32)

    def one_block(block_start):
        query_blk = lax.dynamic_slice_in_dim(query_rows, block_start, block_rows, 0)
        query_place = block_start + jnp.arange(block_rows, dtype=jnp.int32)
        query_segs = lax.dynamic_slice_in_dim(seg_ids, block_start, block_rows, 0)
        allowed = (places[None, :] <= query_place[:, None]) & (seg_ids[None, :] == query_segs[:, None])
        raw_scores = jnp.einsum('qhd,khd->hqk', query_blk, key_rows, precision=HIGHEST_PREC)
        scores = low_back(raw_scores * score_scale)
        scores = jnp.where(allowed[None], scores, NEG_FILL)
        row_peak = lax.optimization_barrier(jnp.max(scores, axis=-1, keepdims=True))
        exp_scores = jnp.exp(scores - row_peak)
        probs = low(exp_scores / lax.optimization_barrier(jnp.sum(exp_scores, axis=-1, keepdims=True)))
        return jnp.einsum('hqk,khd->qhd', probs, value_rows, precision=HIGHEST_PREC)
    block_starts = (jnp.arange(length // block_rows, dtype=jnp.int32) * block_rows).astype(jnp.int32)
    blocks_out = lax.map(jax.checkpoint(one_block), block_starts)
    return blocks_out.reshape(length, -1)

def layer_forward(params, rows_in, teacher_rows, seg_ids, places, valid_rows):
    norm_gain, norm_bias, qkv_weight, qkv_bias, proj_weight, proj_bias, up_weight, up_bias, down_weight, down_bias = params
    length = rows_in.shape[0]
    head_size = D // HEADS
    score_scale = 1.0 / math.sqrt(head_size)
    normed = low(layer_norm(rows_in, norm_gain, norm_bias))
    qkv_full = low_back(jnp.dot(normed, qkv_weight, precision=HIGHEST_PREC) + qkv_bias)
    cosine, sine_table = rotary_tables(places, ROT)
    query_rows = low(rotate(qkv_full[:, :D].reshape(length, HEADS, head_size), cosine, sine_table, ROT))
    key_rows = low(rotate(qkv_full[:, D:2 * D].reshape(length, HEADS, head_size), cosine, sine_table, ROT))
    value_rows = low(qkv_full[:, 2 * D:].reshape(length, HEADS, head_size))
    mixed = low(low_back(attention(query_rows, key_rows, value_rows, seg_ids, score_scale)))
    up_full = low_back(jnp.dot(normed, up_weight, precision=HIGHEST_PREC) + up_bias)
    act_low = low(jax.nn.gelu(up_full, approximate=False))
    attn_part = jnp.dot(mixed, proj_weight, precision=HIGHEST_PREC) + proj_bias
    ffn_part = jnp.dot(act_low, down_weight, precision=HIGHEST_PREC) + down_bias
    branch = low_back(attn_part + ffn_part)
    outputs = rows_in + branch
    error = outputs - teacher_rows
    return (jnp.sum(valid_rows[:, None] * error * error), outputs)

def reference(tokens, teacher, segments, positions, valid_mask, norm_gain, norm_bias, qkv_weight, qkv_bias, proj_weight, proj_bias, up_weight, up_bias, down_weight, down_bias):
    params = tuple((weight.astype(jnp.float32) for weight in (norm_gain, norm_bias, qkv_weight, qkv_bias, proj_weight, proj_bias, up_weight, up_bias, down_weight, down_bias)))
    valid_all = valid_mask.astype(jnp.float32)
    valid_count = jnp.sum(valid_all)
    loss_seed = TOKENS / (2.0 * valid_count)

    def one_sequence(carried, sequence_in):
        grad_sum, square_sum = carried
        rows_in, teacher_rows, seg_ids, places, valid_rows = sequence_in

        def forward(params_in, inputs_in):
            return layer_forward(params_in, inputs_in, teacher_rows.astype(jnp.float32), seg_ids, places, valid_rows)
        seq_square, pullback, outputs = jax.vjp(forward, params, rows_in.astype(jnp.float32), has_aux=True)
        params_grad, inputs_grad = pullback(loss_seed.astype(seq_square.dtype))
        grad_sum = jax.tree.map(jnp.add, grad_sum, params_grad)
        return ((grad_sum, square_sum + seq_square), (outputs.astype(jnp.bfloat16), inputs_grad.astype(jnp.bfloat16)))
    start_state = (tuple((jnp.zeros_like(weight) for weight in params)), jnp.zeros((), jnp.float32))
    (grad_sum, square_sum), (layer_out, input_grad) = lax.scan(one_sequence, start_state, (tokens, teacher, segments, positions, valid_all))
    loss_value = square_sum / (valid_count * D)
    bias_grads = grad_sum[3]
    return (layer_out, loss_value, input_grad, grad_sum[0], grad_sum[1], grad_sum[2], bias_grads[:2 * D], bias_grads[2 * D:], grad_sum[4], grad_sum[5], grad_sum[6], grad_sum[7], grad_sum[8], grad_sum[9])
```

```python
import functools
import math

import jax
import jax.numpy as jnp
from jax import lax
from jax.experimental import pallas as pl
from jax.experimental.pallas import tpu as pltpu
from jax.sharding import PartitionSpec as P

HEADS = 16
ROT = 16
BLK = 128
NEG_FILL = -1000000000.0
F32 = jnp.float32
BF16 = jnp.bfloat16
VMEM_LIMIT = 56 * 1024 * 1024


def mm(a, b, dims=((1,), (0,))):
    return lax.dot_general(a, b, (dims, ((), ())), preferred_element_type=F32)


def block_spans(length, first_len):
    spans = []
    for start in range(0, length, BLK):
        low = 0 if start < first_len else first_len
        spans.append((start, low))
    return spans


def head_stack(rows, heads, size):
    lane = lax.broadcasted_iota(jnp.int32, rows.shape, 1) // size
    parts = [jnp.where(lane == h, rows, jnp.zeros_like(rows)) for h in range(heads)]
    return parts[0] if heads == 1 else jnp.concatenate(parts, axis=0)


def head_pick(stacked, heads, size):
    rows = stacked.shape[0] // heads
    out = stacked[:rows]
    lane = lax.broadcasted_iota(jnp.int32, out.shape, 1) // size
    for h in range(1, heads):
        out = jnp.where(lane == h, stacked[h * rows : (h + 1) * rows], out)
    return out


def turn(values, cosine, sine, size):
    half = ROT // 2
    width = values.shape[1]
    place = lax.broadcasted_iota(jnp.int32, values.shape, 1) % size
    partner = jnp.where(
        place < half,
        pltpu.roll(values, width - half, 1),
        pltpu.roll(values, half, 1),
    )
    return values * cosine + partner * sine


def span_mask(start, low, first_len, seg_col, seg_row, heads):
    stop = start + BLK
    shape = (BLK, stop - low)
    row = lax.broadcasted_iota(jnp.int32, shape, 0) + start
    col = lax.broadcasted_iota(jnp.int32, shape, 1) + low
    allowed = col <= row
    if low >= first_len:
        allowed = allowed & (seg_col[start:stop, :] == seg_row[:, low:stop])
    if heads > 1:
        allowed = jnp.concatenate([allowed.astype(jnp.int32)] * heads, axis=0) > 0
    return allowed


def attend_forward(
    first_len, heads, size, scale,
    x_ref, w_ref, b_ref, cos_ref, sin_ref, segc_ref, segr_ref,
    q_ref, k_ref, v_ref, o_ref, l_ref,
):
    length = x_ref.shape[1]
    width = heads * size
    step = min(256, length)
    for at in range(0, length, step):
        rows = slice(at, at + step)
        full = mm(x_ref[0, rows, :], w_ref[...]) + b_ref[...]
        cosine, sine = cos_ref[0, rows, :], sin_ref[0, rows, :]
        q_ref[0, rows, :] = (
            turn(full[:, :width], cosine, sine, size).astype(BF16) * jnp.asarray(scale, BF16)
        )
        k_ref[0, rows, :] = turn(full[:, width : 2 * width], cosine, sine, size).astype(BF16)
        v_ref[0, rows, :] = full[:, 2 * width :].astype(BF16)
    for start, low in block_spans(length, first_len):
        stop = start + BLK
        query = head_stack(q_ref[0, start:stop, :], heads, size)
        key, value = k_ref[0, low:stop, :], v_ref[0, low:stop, :]
        allowed = span_mask(start, low, first_len, segc_ref[0], segr_ref[0], heads)
        scores = jnp.where(allowed, mm(query, key, ((1,), (1,))), NEG_FILL)
        peak = jnp.max(scores, axis=1, keepdims=True)
        grown = jnp.exp(scores - peak)
        total = jnp.sum(grown, axis=1, keepdims=True)
        probs = (grown * (1.0 / total)).astype(BF16)
        mixed = mm(probs, value)
        o_ref[0, start:stop, :] = head_pick(mixed, heads, size).astype(BF16)
        stat = jnp.broadcast_to(peak + jnp.log(total), mixed.shape)
        l_ref[0, start:stop, :] = head_pick(stat, heads, size)


def attend_backward(
    first_len, heads, size, scale,
    q_ref, k_ref, v_ref, g_ref, l_ref, cos_ref, sin_ref, segc_ref, segr_ref,
    out_ref, dk_ref, dv_ref,
):
    length = q_ref.shape[1]
    width = heads * size
    dk_ref[...] = jnp.zeros_like(dk_ref)
    dv_ref[...] = jnp.zeros_like(dv_ref)
    for start, low in block_spans(length, first_len):
        stop = start + BLK
        query = head_stack(q_ref[0, start:stop, :], heads, size)
        grad = head_stack(g_ref[0, start:stop, :], heads, size)
        key, value = k_ref[0, low:stop, :], v_ref[0, low:stop, :]
        allowed = span_mask(start, low, first_len, segc_ref[0], segr_ref[0], heads)
        stat = l_ref[0, start:stop, :]
        stat = jnp.concatenate([stat[:, h * size : h * size + 1] for h in range(heads)], axis=0)
        scores = jnp.where(allowed, mm(query, key, ((1,), (1,))), NEG_FILL)
        probs = jnp.exp(scores - stat)
        prob_grad = mm(grad, value, ((1,), (1,)))
        delta = jnp.sum(probs * prob_grad, axis=1, keepdims=True)
        score_grad = (probs * (prob_grad - delta)).astype(BF16)
        dq = head_pick(mm(score_grad, key), heads, size) * scale
        cosine, sine = cos_ref[0, start:stop, :], sin_ref[0, start:stop, :]
        out_ref[0, start:stop, :width] = turn(dq, cosine, -sine, size).astype(BF16)
        dk_ref[low:stop, :] += mm(score_grad, query, ((0,), (0,)))
        dv_ref[low:stop, :] += mm(probs.astype(BF16), grad, ((0,), (0,)))
    out_ref[0, :, width : 2 * width] = turn(
        dk_ref[...], cos_ref[0], -sin_ref[0], size
    ).astype(BF16)
    out_ref[0, :, 2 * width :] = dv_ref[...].astype(BF16)


def seq_spec(*dims):
    return pl.BlockSpec((1,) + dims, lambda s: (s,) + (0,) * len(dims))


def whole_spec(*dims):
    return pl.BlockSpec(dims, lambda s: (0,) * len(dims))


def gather_dp(block, n_dp, me_dp):
    out = jnp.zeros((n_dp,) + block.shape, block.dtype)
    out = lax.dynamic_update_index_in_dim(out, block, me_dp, 0)
    for k in range(1, n_dp):
        pairs = [(i, i ^ k) for i in range(n_dp)]
        other = lax.ppermute(block, "dp", pairs)
        out = lax.dynamic_update_index_in_dim(out, other, me_dp ^ k, 0)
    return out.reshape((n_dp * block.shape[0],) + block.shape[1:])


def reduce_dp(terms, n_dp, me_dp):
    rows = terms.shape[0] // n_dp
    blocks = terms.reshape((n_dp, rows) + terms.shape[1:])
    total = lax.dynamic_index_in_dim(blocks, me_dp, 0, keepdims=False).astype(F32)
    low = blocks.astype(BF16)
    for k in range(1, n_dp):
        pairs = [(i, i ^ k) for i in range(n_dp)]
        block = lax.dynamic_index_in_dim(low, me_dp ^ k, 0, keepdims=False)
        total = total + lax.ppermute(block, "dp", pairs).astype(F32)
    return total


def body(
    n_dp, n_ctx,
    tokens, teacher, segments, positions, valid_mask,
    norm_gain, norm_bias, qkv_weight, qkv_bias, proj_weight, proj_bias,
    up_weight, up_bias, down_weight, down_bias,
):
    seqs, local_len, width = tokens.shape
    length = segments.shape[1]
    rows = seqs * local_len
    n_all = n_dp * n_ctx
    first_len = length // 2 + local_len
    heads = HEADS // n_ctx
    size = width // HEADS
    part = heads * size
    units = up_weight.shape[1] // n_ctx
    unit_rows = down_weight.shape[0]
    own = width // n_all
    scale = 1.0 / math.sqrt(size)
    me_dp = lax.axis_index("dp")
    me_ctx = lax.axis_index("ctx")
    both = ("dp", "ctx")

    tokens_all = lax.all_gather(tokens, "ctx", axis=1, tiled=True)

    valid_rows = valid_mask.reshape(rows).astype(F32)
    small = jnp.concatenate(
        [a.astype(F32) for a in (norm_gain, norm_bias, proj_bias, down_bias, qkv_bias, up_bias)]
        + [jnp.sum(valid_rows)[None]]
    )
    pad = -small.shape[0] % 128
    small = jnp.pad(small, (0, pad))
    small = lax.all_to_all(
        jnp.broadcast_to(small[None], (n_all, small.shape[0])), both, 0, 0, tiled=True
    )
    gain = small[:, :own].reshape(1, width)
    shift = small[:, own : 2 * own].reshape(1, width)
    out_bias = (small[:, 2 * own : 3 * own] + small[:, 3 * own : 4 * own]).reshape(1, width)
    at = 4 * own
    qkv_b = small[:, at : at + 3 * own].reshape(3, n_ctx, part)
    qkv_b = lax.dynamic_index_in_dim(qkv_b, me_ctx, 1, keepdims=False).reshape(1, 3 * part)
    at += 3 * own
    up_b = small[:, at : at + unit_rows].reshape(n_dp, n_ctx, unit_rows)
    up_b = lax.dynamic_index_in_dim(up_b, me_ctx, 1, keepdims=False).reshape(1, units)
    at += unit_rows
    valid_count = jnp.sum(small[:, at])

    qkv_cols = qkv_weight.reshape(own, 3, n_ctx, part).transpose(2, 0, 1, 3)
    up_cols = up_weight.reshape(own, n_dp, n_ctx, unit_rows).transpose(2, 0, 1, 3)
    cols = jnp.concatenate(
        [qkv_cols.reshape(n_ctx, own, 3 * part), up_cols.reshape(n_ctx, own, units)], axis=2
    )
    cols = lax.all_to_all(cols, "ctx", 0, 0, tiled=True).reshape(n_ctx * own, 3 * part + units)
    w_cols = gather_dp(cols, n_dp, me_dp)
    w_qkv, w_up = w_cols[:, : 3 * part], w_cols[:, 3 * part :]
    w_down = gather_dp(down_weight, n_dp, me_dp)
    to_plan = [(n_dp * j + i, i * n_ctx + j) for i in range(n_dp) for j in range(n_ctx)]
    from_plan = [(b, a) for a, b in to_plan]
    w_proj = gather_dp(lax.ppermute(proj_weight, both, to_plan), n_dp, me_dp)

    place = jnp.arange(length, dtype=jnp.int32)
    same = segments[:, :, None] == segments[:, None, :]
    before = place[None, None, :] < place[None, :, None]
    in_doc = jnp.sum((same & before).astype(F32), axis=2)
    half = ROT // 2
    lane = jnp.arange(part, dtype=jnp.int32) % size
    steps = jnp.arange(half, dtype=F32)
    inverse = jnp.power(10000.0, -2.0 * steps / ROT)
    lane_inverse = jnp.where(lane < ROT, inverse[lane % half], 0.0)
    angles = in_doc[:, :, None] * lane_inverse[None, None, :]
    cosine = jnp.cos(angles)
    sine = jnp.sin(angles) * jnp.where(lane < half, -1.0, 1.0)
    seg_col = segments[:, :, None]
    seg_row = segments[:, None, :]

    inputs_all = tokens_all.astype(F32)
    row_mean = jnp.mean(inputs_all, axis=-1, keepdims=True)
    centered = inputs_all - row_mean
    variance = jnp.mean(centered * centered, axis=-1, keepdims=True)
    normed = (centered * lax.rsqrt(variance + 1e-05) * gain + shift).astype(BF16)
    normed_rows = normed.reshape(seqs * length, width)

    params = pltpu.CompilerParams(vmem_limit_bytes=VMEM_LIMIT)
    head_shape = jax.ShapeDtypeStruct((seqs, length, part), BF16)
    query, key, value, mixed, stat = pl.pallas_call(
        functools.partial(attend_forward, first_len, heads, size, scale),
        grid=(seqs,),
        in_specs=[
            seq_spec(length, width),
            whole_spec(width, 3 * part),
            whole_spec(1, 3 * part),
            seq_spec(length, part),
            seq_spec(length, part),
            seq_spec(length, 1),
            seq_spec(1, length),
        ],
        out_specs=[seq_spec(length, part)] * 5,
        out_shape=[head_shape] * 4 + [jax.ShapeDtypeStruct((seqs, length, part), F32)],
        compiler_params=params,
        name="attend_forward",
    )(normed, w_qkv, qkv_b, cosine, sine, seg_col, seg_row)

    up = mm(normed_rows, w_up) + up_b
    cdf = 0.5 * (1.0 + lax.erf(up * math.sqrt(0.5)))
    act = (up * cdf).astype(BF16)
    gelu_slope = cdf + up * jnp.exp(-0.5 * up * up) * (1.0 / math.sqrt(2.0 * math.pi))
    mixed_rows = mixed.reshape(seqs * length, part)
    terms = mm(act, w_down) + mm(mixed_rows, w_proj)
    branch = lax.psum_scatter(
        terms.astype(BF16).reshape(seqs, length, width), "ctx", scatter_dimension=1, tiled=True
    )

    inputs = tokens.astype(F32)
    outputs = inputs + (branch.astype(F32) + out_bias)
    error = outputs - teacher.astype(F32)
    valid = valid_rows.reshape(seqs, local_len, 1)
    square = jnp.sum(valid * error * error)
    total_tokens = seqs * n_dp * length
    out_grad = (total_tokens / valid_count) * (valid * error)
    branch_low = out_grad.astype(BF16)
    branch_sum = jnp.sum(branch_low, axis=(0, 1), dtype=F32)
    layer_out = outputs.astype(BF16)

    grad_rows = lax.all_gather(branch_low, "ctx", axis=1, tiled=True).reshape(
        seqs * length, width
    )
    act_grad = mm(grad_rows, w_down, ((1,), (1,)))
    up_grad = (act_grad * gelu_slope).astype(BF16)
    mixed_grad = mm(grad_rows, w_proj, ((1,), (1,))).astype(BF16)
    qkv_grad = pl.pallas_call(
        functools.partial(attend_backward, first_len, heads, size, scale),
        grid=(seqs,),
        in_specs=[seq_spec(length, part)] * 7 + [seq_spec(length, 1), seq_spec(1, length)],
        out_specs=seq_spec(length, 3 * part),
        out_shape=jax.ShapeDtypeStruct((seqs, length, 3 * part), BF16),
        scratch_shapes=[pltpu.VMEM((length, part), F32), pltpu.VMEM((length, part), F32)],
        compiler_params=params,
        name="attend_backward",
    )(
        query, key, value, mixed_grad.reshape(seqs, length, part), stat,
        cosine, sine, seg_col, seg_row,
    ).reshape(seqs * length, 3 * part)
    back = mm(up_grad, w_up, ((1,), (1,))) + mm(qkv_grad, w_qkv, ((1,), (1,)))
    normed_grad = lax.psum_scatter(
        back.astype(BF16).reshape(seqs, length, width), "ctx", scatter_dimension=1, tiled=True
    ).astype(F32)

    first = ((0,), (0,))
    down_wgrad = reduce_dp(mm(act, grad_rows, first), n_dp, me_dp)
    proj_wgrad = reduce_dp(mm(mixed_rows, grad_rows, first), n_dp, me_dp)
    proj_wgrad = lax.ppermute(proj_wgrad.astype(BF16), both, from_plan).astype(F32)
    col_wgrad = jnp.concatenate(
        [mm(normed_rows, qkv_grad, first), mm(normed_rows, up_grad, first)], axis=1
    )
    col_wgrad = reduce_dp(col_wgrad, n_dp, me_dp).astype(BF16)
    col_wgrad = lax.all_to_all(
        col_wgrad.reshape(n_ctx, own, 3 * part + units), "ctx", 0, 0, tiled=True
    )
    qkv_wgrad = (
        col_wgrad[:, :, : 3 * part].reshape(n_ctx, own, 3, part).transpose(1, 2, 0, 3)
    ).reshape(own, 3 * width).astype(F32)
    up_wgrad = (
        col_wgrad[:, :, 3 * part :].reshape(n_ctx, own, n_dp, unit_rows).transpose(1, 2, 0, 3)
    ).reshape(own, n_ctx * units).astype(F32)

    row_mean = jnp.mean(inputs, axis=-1, keepdims=True)
    centered = inputs - row_mean
    variance = jnp.mean(centered * centered, axis=-1, keepdims=True)
    root = lax.rsqrt(variance + 1e-05)
    standard = centered * root
    gain_sum = jnp.sum(normed_grad * standard, axis=(0, 1))
    shift_sum = jnp.sum(normed_grad, axis=(0, 1))
    inner = normed_grad * gain
    input_part = root * (
        inner
        - jnp.mean(inner, axis=-1, keepdims=True)
        - standard * jnp.mean(inner * standard, axis=-1, keepdims=True)
    )
    input_grad = (out_grad + input_part).astype(BF16)

    qkv_bsum = jnp.sum(qkv_grad, axis=0, dtype=F32).reshape(3, 1, part)
    qkv_bsum = lax.dynamic_update_slice(
        jnp.zeros((3, n_ctx, part), F32), qkv_bsum, (0, me_ctx, 0)
    )
    up_bsum = jnp.sum(up_grad, axis=0, dtype=F32).reshape(n_dp, 1, unit_rows)
    up_bsum = lax.dynamic_update_slice(
        jnp.zeros((n_dp, n_ctx, unit_rows), F32), up_bsum, (0, me_ctx, 0)
    )
    sums = jnp.concatenate(
        [
            gain_sum.reshape(n_all, own),
            shift_sum.reshape(n_all, own),
            branch_sum.reshape(n_all, own),
            qkv_bsum[2].reshape(n_all, own),
            qkv_bsum[:2].reshape(n_all, 2 * own),
            up_bsum.reshape(n_all, unit_rows),
            jnp.broadcast_to(square, (n_all, 1)),
        ],
        axis=1,
    )
    sums = jnp.pad(sums, ((0, 0), (0, -sums.shape[1] % 128)))
    sums = jnp.sum(lax.all_to_all(sums, both, 0, 0, tiled=True), axis=0)
    gain_grad, shift_grad, bias_grad, value_bgrad = (
        sums[k * own : (k + 1) * own] for k in range(4)
    )
    qk_bgrad = sums[4 * own : 6 * own]
    up_bgrad = sums[6 * own : 6 * own + unit_rows]
    loss = sums[6 * own + unit_rows] / (valid_count * width)
    return (
        layer_out, loss, input_grad, gain_grad, shift_grad, qkv_wgrad, qk_bgrad, value_bgrad,
        proj_wgrad, bias_grad, up_wgrad, up_bgrad, down_wgrad, bias_grad,
    )


def solution(mesh):
    n_dp, n_ctx = mesh.shape["dp"], mesh.shape["ctx"]
    seq, flat = P("dp", "ctx", None), P(("dp", "ctx"))
    mat = P(("dp", "ctx"), None)
    in_specs = (
        seq, seq, P("dp", None), P("dp", "ctx"), P("dp", "ctx"),
        flat, flat, mat, flat, mat, flat, mat, flat, mat, flat,
    )
    out_specs = (seq, P(), seq, flat, flat, mat, flat, flat, mat, flat, mat, flat, mat, flat)
    return jax.shard_map(
        functools.partial(body, n_dp, n_ctx),
        mesh=mesh, in_specs=in_specs, out_specs=out_specs, check_vma=False,
    )
```

```python
import functools
import math

import jax
import jax.numpy as jnp
from jax import lax
from jax.experimental import pallas as pl
from jax.experimental.pallas import tpu as pltpu
from jax.sharding import PartitionSpec as P

HEADS = 16
ROT = 16
BLK = 128
NEG_FILL = -1000000000.0
F32 = jnp.float32
BF16 = jnp.bfloat16
PARAMS = pltpu.CompilerParams(vmem_limit_bytes=56 * 1024 * 1024)
COPIES = 128
STEP = 512
LAST = ((1,), (1,))
FIRST = ((0,), (0,))


def mm(a, b, dims=((1,), (0,))):
    return lax.dot_general(a, b, (dims, ((), ())), preferred_element_type=F32)


def block_spans(length, first_len):
    return [(at, 0 if at < first_len else first_len) for at in range(0, length, BLK)]


def head_stack(rows, heads, size):
    lane = lax.broadcasted_iota(jnp.int32, rows.shape, 1) // size
    parts = [jnp.where(lane == h, rows, jnp.zeros_like(rows)) for h in range(heads)]
    return parts[0] if heads == 1 else jnp.concatenate(parts, axis=0)


def head_pick(stacked, heads, size):
    rows = stacked.shape[0] // heads
    out = stacked[:rows]
    lane = lax.broadcasted_iota(jnp.int32, out.shape, 1) // size
    for h in range(1, heads):
        out = jnp.where(lane == h, stacked[h * rows : (h + 1) * rows], out)
    return out


def turn(values, cosine, sine, size):
    half = ROT // 2
    width = values.shape[1]
    place = lax.broadcasted_iota(jnp.int32, values.shape, 1) % size
    partner = jnp.where(
        place < half,
        pltpu.roll(values, width - half, 1),
        pltpu.roll(values, half, 1),
    )
    return values * cosine + partner * sine


def span_mask(start, low, first_len, seg_row, heads):
    stop = start + BLK
    shape = (heads * BLK, stop - low)
    row = lax.rem(lax.broadcasted_iota(jnp.int32, shape, 0), BLK) + start
    col = lax.broadcasted_iota(jnp.int32, shape, 1) + low
    allowed = col <= row
    if low >= first_len:
        turned = jnp.transpose(jnp.broadcast_to(seg_row[:, start:stop], (BLK, BLK)))[:, :1]
        turned = jnp.concatenate([turned] * heads, axis=0)
        allowed = allowed & (turned == seg_row[:, low:stop])
    return allowed


def standardize(rows):
    centered = rows - jnp.mean(rows, axis=-1, keepdims=True)
    variance = jnp.mean(centered * centered, axis=-1, keepdims=True)
    root = lax.rsqrt(variance + 1e-05)
    return centered * root, root


class Copier:
    def __init__(self, sems):
        self.sems, self.used = sems, 0

    def start(self, source, target):
        copy = pltpu.make_async_copy(source, target, self.sems.at[self.used])
        self.used += 1
        copy.start()
        return copy

    def rows(self, pairs, at, step):
        return [self.start(a.at[at : at + step], b.at[at : at + step]) for a, b in pairs]


def view_columns(refs, part, units):
    if len(refs) == 2:
        return refs
    return refs[0].at[:, pl.ds(0, 3 * part)], refs[0].at[:, pl.ds(3 * part, units)]


def wait_all(copies):
    for copy in copies:
        copy.wait()


def forward_kernel(
    first_len, heads, size, scale, length, step,
    gain, shift, bqkv, bup, seg_row, x_in, cos_in, sin_in, wdown_in, wproj_in, *refs,
):
    (x, cosine, sine, wdown, wproj,
     normed, q, k, v, act, slope, mixed, stat, terms, sems) = refs[-15:]
    split = (len(refs) - 24) // 2
    w_in, w = refs[:split], refs[split + 9 : 2 * split + 9]
    (n_out, q_out, k_out, v_out, act_out, slope_out, mixed_out, stat_out, terms_out) = refs[
        split : split + 9
    ]
    copier = Copier(sems)
    part = heads * size
    wqkv, wup = view_columns(w, part, act.shape[1])
    total = x.shape[0]
    starts = range(0, total, step)
    tables = ((cos_in, cosine), (sin_in, sine))
    x_copies = {0: copier.rows([(x_in, x)], 0, step)}
    w_copies = [copier.start(a, b) for a, b in zip(w_in, w)]
    t_copies = {0: copier.rows(tables, 0, step)}
    for at in starts[1:]:
        x_copies[at] = copier.rows([(x_in, x)], at, step)
        t_copies[at] = copier.rows(tables, at, step)
    w_copies += [copier.start(wdown_in, wdown), copier.start(wproj_in, wproj)]
    out = []
    for seq in range(total // length):
        origin = seq * length
        for at in range(origin, origin + length, step):
            rows = slice(at, at + step)
            wait_all(x_copies[at])
            standard, _ = standardize(x[rows, :].astype(F32))
            low = (standard * gain[...] + shift[...]).astype(BF16)
            normed[rows, :] = low
            out += copier.rows([(normed, n_out)], at, step)
            if at == 0:
                wait_all(w_copies[:split])
            full = mm(low, wqkv[...]) + bqkv[...]
            wait_all(t_copies[at])
            cos_rows, sin_rows = cosine[rows, :], sine[rows, :]
            q[rows, :] = turn(full[:, :part], cos_rows, sin_rows, size).astype(
                BF16
            ) * jnp.asarray(scale, BF16)
            k[rows, :] = turn(full[:, part : 2 * part], cos_rows, sin_rows, size).astype(BF16)
            v[rows, :] = full[:, 2 * part :].astype(BF16)
            out += copier.rows(((q, q_out), (k, k_out), (v, v_out)), at, step)
            up = mm(low, wup[...]) + bup[...]
            cdf = 0.5 * (1.0 + lax.erf(up * math.sqrt(0.5)))
            act[rows, :] = (up * cdf).astype(BF16)
            slope[rows, :] = cdf + up * jnp.exp(-0.5 * up * up) * (
                1.0 / math.sqrt(2.0 * math.pi)
            )
            out += copier.rows(((act, act_out), (slope, slope_out)), at, step)
        for start, low in block_spans(length, first_len):
            rows, cols = slice(origin + start, origin + start + BLK), slice(
                origin + low, origin + start + BLK
            )
            query = head_stack(q[rows, :], heads, size)
            allowed = span_mask(start, low, first_len, seg_row[seq : seq + 1, :], heads)
            scores = jnp.where(allowed, mm(query, k[cols, :], LAST), NEG_FILL)
            peak = jnp.max(scores, axis=1, keepdims=True)
            grown = jnp.exp(scores - peak)
            summed = jnp.sum(grown, axis=1, keepdims=True)
            probs = (grown * (1.0 / summed)).astype(BF16)
            result = mm(probs, v[cols, :])
            mixed[rows, :] = head_pick(result, heads, size).astype(BF16)
            stat[rows, :] = head_pick(
                jnp.broadcast_to(peak + jnp.log(summed), result.shape), heads, size
            )
        out += copier.rows(((mixed, mixed_out), (stat, stat_out)), origin, length)
        if seq == 0:
            wait_all(w_copies[split:])
        for at in range(origin, origin + length, step):
            rows = slice(at, at + step)
            terms[rows, :] = (mm(act[rows, :], wdown[...]) + mm(mixed[rows, :], wproj[...])).astype(
                BF16
            )
            out += copier.rows([(terms, terms_out)], at, step)
    wait_all(out)


def backward_kernel(
    first_len, heads, size, scale, length, step,
    seg_row,
    g_in, slope_in, q_in, k_in, v_in, stat_in, cos_in, sin_in, wdown_in, wproj_in, *refs,
):
    (g, slope, q, k, v, stat, cosine, sine, wdown, wproj,
     mg, ug, qg, dk, dv, back, sems) = refs[-17:]
    split = (len(refs) - 20) // 2
    w_in, w = refs[:split], refs[split + 3 : 2 * split + 3]
    ug_out, qg_out, back_out = refs[split : split + 3]
    copier = Copier(sems)
    width = heads * size
    wqkv, wup = view_columns(w, width, ug.shape[1])
    total = g.shape[0]
    starts = range(0, total, step)
    loads = ((g_in, g), (slope_in, slope))
    saved = (
        (q_in, q), (k_in, k), (v_in, v), (stat_in, stat), (cos_in, cosine), (sin_in, sine)
    )
    g_copies = {0: copier.rows(loads[:1], 0, step)}
    w_copies = [copier.start(wdown_in, wdown)]
    g_copies[0] += copier.rows(loads[1:], 0, step)
    w_copies.append(copier.start(wproj_in, wproj))
    s_copies = {}
    for at in starts[1:]:
        g_copies[at] = copier.rows(loads, at, step)
        if (at + step) % length == 0:
            origin = at + step - length
            s_copies[origin] = copier.rows(saved, origin, length)
            if origin == 0:
                w_copies += [copier.start(a, b) for a, b in zip(w_in, w)]
    out = []
    for seq in range(total // length):
        origin = seq * length
        for at in range(origin, origin + length, step):
            rows = slice(at, at + step)
            wait_all(g_copies[at])
            if at == 0:
                wait_all(w_copies[:2])
            grad = g[rows, :]
            ug[rows, :] = (mm(grad, wdown[...], LAST) * slope[rows, :]).astype(BF16)
            out += copier.rows([(ug, ug_out)], at, step)
            mg[rows, :] = mm(grad, wproj[...], LAST).astype(BF16)
        dk[...] = jnp.zeros_like(dk)
        dv[...] = jnp.zeros_like(dv)
        wait_all(s_copies[origin])
        for start, low in block_spans(length, first_len):
            stop = start + BLK
            rows, cols = slice(origin + start, origin + stop), slice(origin + low, origin + stop)
            query = head_stack(q[rows, :], heads, size)
            grad = head_stack(mg[rows, :], heads, size)
            key, value = k[cols, :], v[cols, :]
            allowed = span_mask(start, low, first_len, seg_row[seq : seq + 1, :], heads)
            peak = stat[rows, :]
            peak = jnp.concatenate(
                [peak[:, h * size : h * size + 1] for h in range(heads)], axis=0
            )
            scores = jnp.where(allowed, mm(query, key, LAST), NEG_FILL)
            probs = jnp.exp(scores - peak)
            prob_grad = mm(grad, value, LAST)
            delta = jnp.sum(probs * prob_grad, axis=1, keepdims=True)
            score_grad = (probs * (prob_grad - delta)).astype(BF16)
            dq = head_pick(mm(score_grad, key), heads, size) * scale
            qg[rows, :width] = turn(dq, cosine[rows, :], -sine[rows, :], size).astype(BF16)
            dk[low:stop, :] += mm(score_grad, query, FIRST)
            dv[low:stop, :] += mm(probs.astype(BF16), grad, FIRST)
        rows = slice(origin, origin + length)
        qg[rows, width : 2 * width] = turn(
            dk[...], cosine[rows, :], -sine[rows, :], size
        ).astype(BF16)
        qg[rows, 2 * width :] = dv[...].astype(BF16)
        out += copier.rows([(qg, qg_out)], origin, length)
        if seq == 0:
            wait_all(w_copies[2:])
        for at in range(origin, origin + length, step):
            rows = slice(at, at + step)
            back[rows, :] = (
                mm(ug[rows, :], wup[...], LAST) + mm(qg[rows, :], wqkv[...], LAST)
            ).astype(BF16)
            out += copier.rows([(back, back_out)], at, step)
    wait_all(out)


def column_kernel(cut, order, n, qg, ug, *outs):
    outs, sums = outs[:-1], outs[-1]
    rows, split = outs[0].shape[0], qg.shape[1]
    ones = jnp.ones((8, n.shape[0]), BF16)
    sums[:, :split] = mm(ones, qg[...])
    sums[:, split:] = mm(ones, ug[...])
    for k in list(range(1, len(outs))) + [0]:
        if cut:
            block = n[:, pl.ds(pl.multiple_of(order[k] * rows, rows), rows)]
        else:
            block = n[...]
        outs[k][:, :split] = mm(block, qg[...], FIRST).astype(outs[k].dtype)
        outs[k][:, split:] = mm(block, ug[...], FIRST).astype(outs[k].dtype)


def down_kernel(act, mixed, g, dw, pw):
    dw[...] = mm(act[...], g[...], FIRST).astype(BF16)
    pw[...] = mm(mixed[...], g[...], FIRST).astype(BF16)


def sums_kernel(x, back, gain_sum, shift_sum):
    @pl.when(pl.program_id(0) == 0)
    def _():
        for ref in (gain_sum, shift_sum):
            ref[...] = jnp.zeros_like(ref)

    standard, _ = standardize(x[...].astype(F32))
    terms = back[...].astype(F32)
    gain_sum[...] += jnp.sum(terms * standard, axis=0, keepdims=True)
    shift_sum[...] += jnp.sum(terms, axis=0, keepdims=True)


def loss_kernel(branch, x, teacher, valid, bias, factor, out, grad, low, column, square):
    full = x[...].astype(F32) + (branch[...].astype(F32) + bias[...])
    out[...] = full.astype(BF16)
    error = valid[...] * (full - teacher[...].astype(F32))
    square[...] = jnp.sum(jnp.sum(error * error, axis=0, keepdims=True), axis=1, keepdims=True)
    scaled = factor[...] * error
    grad[...] = scaled
    rounded = scaled.astype(BF16)
    low[...] = rounded
    column[...] = jnp.sum(rounded.astype(F32), axis=0, keepdims=True)


def norm_back_kernel(ng, x, og, gain, out):
    standard, root = standardize(x[...].astype(F32))
    inner = ng[...].astype(F32) * gain[...]
    out[...] = (
        og[...]
        + root
        * (
            inner
            - jnp.mean(inner, axis=-1, keepdims=True)
            - standard * jnp.mean(inner * standard, axis=-1, keepdims=True)
        )
    ).astype(BF16)


def head_of(local, ctx, heads, n_ctx, paired):
    if not paired:
        return ctx * heads + local
    return (heads * (ctx % 2) + local) * (n_ctx // 2) + ctx // 2


def pack_columns(heads, size, paired, units, n_dp, n_ctx, qkv_ref, up_ref, valid_ref, *refs):
    vectors, out_ref = refs[:-1], refs[-1]
    part = heads * size
    width, unit_rows = n_ctx * part, units // n_dp
    count = jnp.sum(jnp.sum(valid_ref[...].astype(F32), axis=1, keepdims=True), axis=0, keepdims=True)
    high = jnp.floor(count * (1.0 / 128.0))
    small = [
        jnp.pad(ref[...].astype(F32).reshape(1, ref.shape[0]), ((0, 0), (0, 128 - ref.shape[0])))
        for ref in vectors
    ]
    small += [jnp.broadcast_to(a, (1, 128)) for a in (high, count - 128.0 * high)]
    small = jnp.concatenate(small, axis=0).astype(BF16)
    small = jnp.concatenate([small, jnp.zeros((out_ref.shape[1] - 8, 128), BF16)], axis=0)
    for j in range(n_ctx):
        out_ref[j, :, 3 * part + units :] = small
        for p in range(3):
            at = [p * width + head_of(h, j, heads, n_ctx, paired) * size for h in range(heads)]
            out_ref[j, :, p * part : (p + 1) * part] = jnp.concatenate(
                [qkv_ref[:, a : a + size] for a in at], axis=1
            )
        for i in range(n_dp):
            at = (i * n_ctx + j) * unit_rows
            out_ref[j, :, 3 * part + i * unit_rows : 3 * part + (i + 1) * unit_rows] = up_ref[
                :, at : at + unit_rows
            ]


def unpack_columns(heads, size, paired, units, n_dp, n_ctx, in_ref, qkv_ref, up_ref):
    part = heads * size
    width, unit_rows = n_ctx * part, units // n_dp
    held = {
        head_of(h, j, heads, n_ctx, paired): (j, h) for j in range(n_ctx) for h in range(heads)
    }
    for p in range(3):
        for first in range(0, n_ctx * heads, heads):
            pieces = []
            for head in range(first, first + heads):
                j, h = held[head]
                pieces.append(in_ref[j, :, p * part : (p + 1) * part][:, h * size : (h + 1) * size])
            qkv_ref[:, p * width + first * size : p * width + (first + heads) * size] = (
                jnp.concatenate(pieces, axis=1).astype(F32)
            )
    for j in range(n_ctx):
        for i in range(n_dp):
            at = (i * n_ctx + j) * unit_rows
            up_ref[:, at : at + unit_rows] = in_ref[
                j, :, 3 * part + i * unit_rows : 3 * part + (i + 1) * unit_rows
            ].astype(F32)


def shape_of(dims, dtype):
    return jax.ShapeDtypeStruct(dims, dtype)


def row_spec(rows, *dims):
    return pl.BlockSpec((rows,) + dims, lambda s: (s,) + (0,) * len(dims))


def whole_spec(*dims):
    return pl.BlockSpec(dims, lambda s: (0,) * len(dims))


HBM = pl.BlockSpec(memory_space=pl.ANY)
LOCAL = pl.BlockSpec(memory_space=pltpu.VMEM)
SCALAR = pl.BlockSpec(memory_space=pltpu.SMEM)


def kernel_call(kernel, name, in_specs, out, scratch=(), flops=0, moved=0, grid=None):
    return pl.pallas_call(
        kernel,
        in_specs=in_specs,
        out_specs=[spec for spec, _ in out],
        out_shape=[shape for _, shape in out],
        scratch_shapes=list(scratch),
        compiler_params=PARAMS,
        cost_estimate=pl.CostEstimate(flops=flops, bytes_accessed=moved, transcendentals=0),
        name=name,
        **({"grid": grid} if grid else {}),
    )


def gather_dp(block, n_dp, me_dp):
    out = jnp.zeros((n_dp,) + block.shape, block.dtype)
    out = lax.dynamic_update_index_in_dim(out, block, me_dp, 0)
    for k in range(1, n_dp):
        pairs = [(i, i ^ k) for i in range(n_dp)]
        other = lax.ppermute(block, "dp", pairs)
        out = lax.dynamic_update_index_in_dim(out, other, me_dp ^ k, 0)
    return out.reshape((n_dp * block.shape[0],) + block.shape[1:])


def exchange_dp(terms, n_dp):
    total = terms[0]
    for k in range(1, n_dp):
        pairs = [(i, i ^ k) for i in range(n_dp)]
        total = total + lax.ppermute(terms[k], "dp", pairs).astype(F32)
    return total


def reduce_dp(terms, n_dp, me_dp):
    rows = terms.shape[0] // n_dp
    blocks = terms.reshape((n_dp, rows) + terms.shape[1:])
    total = lax.dynamic_index_in_dim(blocks, me_dp, 0, keepdims=False).astype(F32)
    for k in range(1, n_dp):
        pairs = [(i, i ^ k) for i in range(n_dp)]
        block = lax.dynamic_index_in_dim(blocks, me_dp ^ k, 0, keepdims=False)
        total = total + lax.ppermute(block, "dp", pairs).astype(F32)
    return total


def body(
    n_dp, n_ctx,
    tokens, teacher, segments, positions, valid_mask,
    norm_gain, norm_bias, qkv_weight, qkv_bias, proj_weight, proj_bias,
    up_weight, up_bias, down_weight, down_bias,
):
    seqs, local_len, width = tokens.shape
    length = segments.shape[1]
    rows = seqs * local_len
    all_rows = seqs * length
    n_all = n_dp * n_ctx
    first_len = length // 2 + local_len
    heads = HEADS // n_ctx
    size = width // HEADS
    part = heads * size
    hidden = up_weight.shape[1]
    units = hidden // n_ctx
    unit_rows = down_weight.shape[0]
    own = width // n_all
    scale = 1.0 / math.sqrt(size)
    me_dp = lax.axis_index("dp")
    me_ctx = lax.axis_index("ctx")
    both = ("dp", "ctx")
    aligned = part % 128 == 0 and unit_rows % 128 == 0 and own % 16 == 0
    paired = aligned and 2 * own == size and 2 * heads == n_dp
    me_core, me_chip = me_ctx % 2, me_ctx // 2
    swap = [(j, j ^ 1) for j in range(n_ctx)]

    to_plan = [(n_dp * j + i, i * n_ctx + j) for i in range(n_dp) for j in range(n_ctx)]
    from_plan = [(b, a) for a, b in to_plan]
    valid = valid_mask.astype(F32).reshape(rows, 1)
    vectors = [norm_gain, norm_bias, proj_bias, down_bias, qkv_bias, up_bias]
    extra = 128 * max(1, 8 // own)
    total_cols = 3 * part + units + extra
    if aligned:
        cols = pl.pallas_call(
            functools.partial(pack_columns, heads, size, paired, units, n_dp, n_ctx),
            out_shape=shape_of((n_ctx, own, total_cols), BF16),
            compiler_params=PARAMS,
            name="pack_columns",
        )(qkv_weight, up_weight, valid_mask, *vectors)
    else:
        count = jnp.sum(valid_mask)
        small = jnp.stack(
            [jnp.pad(a, (0, 128 - a.shape[0])) for a in vectors]
            + [jnp.broadcast_to(a.astype(BF16), (128,)) for a in (count // 128, count % 128)]
        ).reshape(8 * 128)
        small = jnp.pad(small, (0, own * extra - 8 * 128)).reshape(own, extra)
        qkv_cols = qkv_weight.reshape(own, 3, n_ctx, part).transpose(2, 0, 1, 3)
        up_cols = up_weight.reshape(own, n_dp, n_ctx, unit_rows).transpose(2, 0, 1, 3)
        cols = jnp.concatenate(
            [
                qkv_cols.reshape(n_ctx, own, 3 * part), up_cols.reshape(n_ctx, own, units),
                jnp.broadcast_to(small[None], (n_ctx, own, extra)),
            ],
            axis=2,
        )
    cols, down_weight, proj_weight = lax.optimization_barrier((cols, down_weight, proj_weight))
    x_rows = lax.all_gather(tokens, "ctx", axis=1, tiled=True).reshape(all_rows, width)
    cols = lax.all_to_all(cols, "ctx", 0, 0, tiled=True).reshape(n_ctx * own, total_cols)
    cols, segments = lax.optimization_barrier((cols, segments))
    w_cols = gather_dp(cols, n_dp, me_dp)
    small = w_cols[:, 3 * part + units :].reshape(n_all, own * extra)[:, : 8 * 128]
    small = small.reshape(n_all, 8, 128).astype(F32)
    gain = small[:, 0, :own].reshape(1, width)
    shift = small[:, 1, :own].reshape(1, width)
    out_bias = (small[:, 2, :own] + small[:, 3, :own]).reshape(1, width)
    qkv_b = small[:, 4, : 3 * own]
    if paired:
        qkv_b = lax.dynamic_slice(
            qkv_b.reshape(3, 2, heads, n_ctx // 2, size), (0, me_core, 0, me_chip, 0),
            (3, 1, heads, 1, size),
        )
    else:
        qkv_b = lax.dynamic_index_in_dim(qkv_b.reshape(3, n_ctx, part), me_ctx, 1)
    qkv_b = qkv_b.reshape(1, 3 * part)
    up_b = small[:, 5, :unit_rows].reshape(n_dp, n_ctx, unit_rows)
    up_b = lax.dynamic_index_in_dim(up_b, me_ctx, 1, keepdims=False).reshape(1, units)
    valid_count = 128.0 * jnp.sum(small[:, 6, 0]) + jnp.sum(small[:, 7, 0])
    sliced = (3 * part) % 128 == 0 and units % 128 == 0
    if sliced:
        w_split = [w_cols]
    else:
        w_split = [w_cols[:, : 3 * part], w_cols[:, 3 * part : 3 * part + units]]
    token = jnp.arange(length, dtype=jnp.int32)
    half = ROT // 2
    lane = jnp.arange(part, dtype=jnp.int32) % size
    steps = jnp.arange(half, dtype=F32)
    inverse = jnp.power(10000.0, -2.0 * steps / ROT)
    lane_inverse = jnp.where(lane < ROT, inverse[lane % half], 0.0)
    same = segments[:, :, None] == segments[:, None, :]
    before = token[None, None, :] < token[None, :, None]
    in_doc = jnp.sum((same & before).astype(F32), axis=2)
    angles = in_doc.reshape(all_rows, 1) * lane_inverse[None, :]
    cosine = jnp.cos(angles)
    sine = jnp.sin(angles) * jnp.where(lane < half, -1.0, 1.0)

    w_down = gather_dp(down_weight, n_dp, me_dp)
    if paired:
        halves = gather_dp(proj_weight, n_dp, me_dp).reshape(2, heads, own, width)
        keep = lax.dynamic_index_in_dim(halves, me_core, 0, keepdims=False)
        got = lax.ppermute(
            lax.dynamic_index_in_dim(halves, 1 - me_core, 0, keepdims=False), "ctx", swap
        )
        w_proj = jnp.stack(
            [jnp.where(me_core == 0, keep, got), jnp.where(me_core == 0, got, keep)], axis=1
        ).reshape(part, width)
    else:
        w_proj = gather_dp(lax.ppermute(proj_weight, both, to_plan), n_dp, me_dp)

    def wide(columns, dtype=BF16):
        return pltpu.VMEM((all_rows, columns), dtype)

    def store(columns, dtype=BF16):
        return (HBM, shape_of((all_rows, columns), dtype))

    w_scratch = [pltpu.VMEM(a.shape, BF16) for a in w_split]
    weights = [pltpu.VMEM((units, width), BF16), pltpu.VMEM((part, width), BF16)]
    sems = pltpu.SemaphoreType.DMA((COPIES,))
    normed, query, key, value, act, slope, mixed, stat, terms = kernel_call(
        functools.partial(forward_kernel, first_len, heads, size, scale, length, STEP),
        "forward_kernel",
        [LOCAL] * 5 + [HBM] * (5 + len(w_split)),
        [
            store(width), store(part), store(part), store(part), store(units), store(units, F32),
            store(part), store(part, F32), store(width),
        ],
        [
            *w_scratch, wide(width), wide(part, F32), wide(part, F32), *weights,
            wide(width), wide(part), wide(part), wide(part), wide(units), wide(units, F32),
            wide(part), wide(part, F32), wide(width), sems,
        ],
        flops=10 * 10**9, moved=2 * 10**7,
    )(
        gain, shift, qkv_b, up_b, segments, x_rows, cosine, sine, w_down, w_proj, *w_split
    )
    branch = lax.psum_scatter(
        terms.reshape(seqs, length, width), "ctx", scatter_dimension=1, tiled=True
    ).reshape(rows, width)

    total_tokens = seqs * n_dp * length
    factor = (total_tokens / valid_count).reshape(1, 1)
    tokens_rows = tokens.reshape(rows, width)
    own_block = (rows, width)
    layer_out, out_grad, low, column, square = kernel_call(
        loss_kernel, "loss_kernel", [LOCAL] * 6,
        [
            (LOCAL, shape_of(own_block, BF16)), (LOCAL, shape_of(own_block, F32)),
            (LOCAL, shape_of(own_block, BF16)), (LOCAL, shape_of((1, width), F32)),
            (LOCAL, shape_of((1, 1), F32)),
        ],
        flops=10**6, moved=3 * 10**6,
    )(branch, tokens_rows, teacher.reshape(rows, width), valid, out_bias, factor)

    grads = lax.all_gather(
        low.reshape(tokens.shape), "ctx", axis=1, tiled=True
    ).reshape(all_rows, width)
    up_grad, qkv_grad, back = kernel_call(
        functools.partial(backward_kernel, first_len, heads, size, scale, length, STEP),
        "backward_kernel",
        [LOCAL] + [HBM] * (10 + len(w_split)),
        [store(units), store(3 * part), store(width)],
        [
            *w_scratch, wide(width), wide(units, F32), wide(part), wide(part), wide(part),
            wide(part, F32), wide(part, F32), wide(part, F32), *weights, wide(part), wide(units), wide(3 * part),
            pltpu.VMEM((length, part), F32), pltpu.VMEM((length, part), F32), wide(width), sems,
        ],
        flops=12 * 10**9, moved=2 * 10**7,
    )(
        segments, grads, slope, query, key, value, stat, cosine, sine, w_down, w_proj, *w_split
    )
    normed_grad = lax.psum_scatter(
        back.reshape(seqs, length, width), "ctx", scatter_dimension=1, tiled=True
    ).reshape(rows, width)

    order = jnp.stack([me_dp ^ k for k in range(n_dp)]).astype(jnp.int32)
    cut = (width // n_dp) % 128 == 0
    block = (width // n_dp if cut else width, 3 * part + units)
    *col_terms, col_sums = kernel_call(
        functools.partial(column_kernel, cut), "column_kernel",
        [SCALAR] + [LOCAL] * 3,
        [(LOCAL, shape_of(block, BF16 if k else F32)) for k in range(n_dp if cut else 1)]
        + [(LOCAL, shape_of((8, block[1]), F32))],
        flops=4 * 10**9, moved=10**7,
    )(order, normed, qkv_grad, up_grad)
    col_terms, x_rows = lax.optimization_barrier((col_terms, x_rows))
    if cut:
        col_wgrad = exchange_dp(col_terms, n_dp).astype(BF16)
    else:
        col_wgrad = reduce_dp(col_terms[0].astype(BF16), n_dp, me_dp).astype(BF16)
    sum_rows = 512
    gain_sum, shift_sum = kernel_call(
        sums_kernel, "sums_kernel",
        [row_spec(sum_rows, width)] * 2,
        [(whole_spec(1, width), shape_of((1, width), F32))] * 2,
        flops=10**6, moved=10**5, grid=(all_rows // sum_rows,),
    )(x_rows, back)
    qkv_bsum, up_bsum = col_sums[:1, : 3 * part], col_sums[:1, 3 * part :]
    if paired:
        qkv_bsum = lax.dynamic_update_slice(
            jnp.zeros((3, 2, heads, n_ctx // 2, size), F32),
            qkv_bsum.reshape(3, 1, heads, 1, size), (0, me_core, 0, me_chip, 0),
        )
    else:
        qkv_bsum = lax.dynamic_update_slice(
            jnp.zeros((3, n_ctx, part), F32), qkv_bsum.reshape(3, 1, part), (0, me_ctx, 0)
        )
    up_bsum = lax.dynamic_update_slice(
        jnp.zeros((n_dp, n_ctx, unit_rows), F32), up_bsum.reshape(n_dp, 1, unit_rows),
        (0, me_ctx, 0),
    )
    parts = [
        gain_sum.reshape(n_all, own), shift_sum.reshape(n_all, own),
        column.reshape(n_all, own), qkv_bsum[2].reshape(n_all, own),
        qkv_bsum[:2].reshape(n_all, 2 * own), up_bsum.reshape(n_all, unit_rows),
        jnp.broadcast_to(square, (n_all, 1)),
    ]
    sums = jnp.concatenate(parts, axis=1)
    sums = jnp.pad(sums, ((0, 0), (0, -sums.shape[1] % 128)))
    sums = lax.all_to_all(sums, both, 0, 0, tiled=True)
    col_wgrad, sums = lax.optimization_barrier((col_wgrad, sums))
    col_wgrad, act = lax.optimization_barrier((col_wgrad, act))
    col_wgrad = lax.all_to_all(
        col_wgrad.reshape(n_ctx, own, 3 * part + units), "ctx", 0, 0, tiled=True
    )
    sums = jnp.sum(sums, axis=0)
    gain_grad, shift_grad, bias_grad, value_bgrad = (
        sums[k * own : (k + 1) * own] for k in range(4)
    )
    qk_bgrad = sums[4 * own : 6 * own]
    up_bgrad = sums[6 * own : 6 * own + unit_rows]
    loss = sums[6 * own + unit_rows] / (valid_count * width)

    down_wgrad, proj_wgrad = kernel_call(
        down_kernel, "down_kernel", [LOCAL] * 3,
        [(LOCAL, shape_of((units, width), BF16)), (LOCAL, shape_of((part, width), BF16))],
        flops=10**6, moved=10**5,
    )(act, mixed, grads)
    down_wgrad = reduce_dp(down_wgrad, n_dp, me_dp)
    if paired:
        halves = proj_wgrad.reshape(heads, 2, own, width)
        keep = lax.dynamic_index_in_dim(halves, me_core, 1, keepdims=False)
        got = lax.ppermute(
            lax.dynamic_index_in_dim(halves, 1 - me_core, 1, keepdims=False), "ctx", swap
        )
        proj_wgrad = jnp.concatenate(
            [jnp.where(me_core == 0, keep, got), jnp.where(me_core == 0, got, keep)], axis=0
        ).reshape(n_dp * own, width)
        proj_wgrad = reduce_dp(proj_wgrad, n_dp, me_dp)
    else:
        proj_wgrad = reduce_dp(proj_wgrad, n_dp, me_dp)
        proj_wgrad = lax.ppermute(proj_wgrad.astype(BF16), both, from_plan).astype(F32)

    (input_grad,) = kernel_call(
        norm_back_kernel, "norm_back_kernel", [LOCAL] * 4, [(LOCAL, shape_of(own_block, BF16))],
        flops=10**6, moved=3 * 10**6,
    )(normed_grad, tokens_rows, out_grad, gain)
    input_grad, col_wgrad = lax.optimization_barrier((input_grad, col_wgrad))
    if aligned:
        qkv_wgrad, up_wgrad = pl.pallas_call(
            functools.partial(unpack_columns, heads, size, paired, units, n_dp, n_ctx),
            out_shape=[shape_of((own, 3 * width), F32), shape_of((own, hidden), F32)],
            compiler_params=PARAMS,
            name="unpack_columns",
        )(col_wgrad)
    else:
        qkv_wgrad = (
            col_wgrad[:, :, : 3 * part].reshape(n_ctx, own, 3, part).transpose(1, 2, 0, 3)
        ).reshape(own, 3 * width).astype(F32)
        up_wgrad = (
            col_wgrad[:, :, 3 * part :].reshape(n_ctx, own, n_dp, unit_rows).transpose(1, 2, 0, 3)
        ).reshape(own, hidden).astype(F32)

    return (
        layer_out.reshape(tokens.shape), loss, input_grad.reshape(tokens.shape), gain_grad,
        shift_grad, qkv_wgrad, qk_bgrad, value_bgrad, proj_wgrad, bias_grad, up_wgrad, up_bgrad,
        down_wgrad, bias_grad,
    )


def solution(mesh):
    n_dp, n_ctx = mesh.shape["dp"], mesh.shape["ctx"]
    seq, flat = P("dp", "ctx", None), P(("dp", "ctx"))
    mat = P(("dp", "ctx"), None)
    in_specs = (
        seq, seq, P("dp", None), P("dp", "ctx"), P("dp", "ctx"),
        flat, flat, mat, flat, mat, flat, mat, flat, mat, flat,
    )
    out_specs = (seq, P(), seq, flat, flat, mat, flat, flat, mat, flat, mat, flat, mat, flat)
    return jax.shard_map(
        functools.partial(body, n_dp, n_ctx),
        mesh=mesh, in_specs=in_specs, out_specs=out_specs, check_vma=False,
    )
```

```python
import functools
import math

import jax
import jax.numpy as jnp
from jax import lax
from jax.experimental import pallas as pl
from jax.experimental.pallas import tpu as pltpu
from jax.sharding import PartitionSpec as P

HEADS = 16
ROT = 16
BLK = 128
NEG_FILL = -1000000000.0
F32 = jnp.float32
BF16 = jnp.bfloat16
PARAMS = pltpu.CompilerParams(vmem_limit_bytes=56 * 1024 * 1024)
COPIES = 128
STEP = 512
LAST = ((1,), (1,))
FIRST = ((0,), (0,))


def mm(a, b, dims=((1,), (0,))):
    return lax.dot_general(a, b, (dims, ((), ())), preferred_element_type=F32)


def block_spans(length, first_len):
    return [(at, 0 if at < first_len else first_len) for at in range(0, length, BLK)]


def head_stack(rows, heads, size):
    lane = lax.broadcasted_iota(jnp.int32, rows.shape, 1) // size
    parts = [jnp.where(lane == h, rows, jnp.zeros_like(rows)) for h in range(heads)]
    return parts[0] if heads == 1 else jnp.concatenate(parts, axis=0)


def head_pick(stacked, heads, size):
    rows = stacked.shape[0] // heads
    out = stacked[:rows]
    lane = lax.broadcasted_iota(jnp.int32, out.shape, 1) // size
    for h in range(1, heads):
        out = jnp.where(lane == h, stacked[h * rows : (h + 1) * rows], out)
    return out


def turn(values, cosine, sine, size):
    half = ROT // 2
    width = values.shape[1]
    place = lax.broadcasted_iota(jnp.int32, values.shape, 1) % size
    partner = jnp.where(
        place < half,
        pltpu.roll(values, width - half, 1),
        pltpu.roll(values, half, 1),
    )
    return values * cosine + partner * sine


def span_mask(start, low, first_len, seg_row, heads):
    stop = start + BLK
    shape = (heads * BLK, stop - low)
    row = lax.rem(lax.broadcasted_iota(jnp.int32, shape, 0), BLK) + start
    col = lax.broadcasted_iota(jnp.int32, shape, 1) + low
    allowed = col <= row
    if low >= first_len:
        turned = jnp.transpose(jnp.broadcast_to(seg_row[:, start:stop], (BLK, BLK)))[:, :1]
        turned = jnp.concatenate([turned] * heads, axis=0)
        allowed = allowed & (turned == seg_row[:, low:stop])
    return allowed


def standardize(rows):
    centered = rows - jnp.mean(rows, axis=-1, keepdims=True)
    variance = jnp.mean(centered * centered, axis=-1, keepdims=True)
    root = lax.rsqrt(variance + 1e-05)
    return centered * root, root


class Copier:
    def __init__(self, sems):
        self.sems, self.used = sems, 0

    def start(self, source, target):
        copy = pltpu.make_async_copy(source, target, self.sems.at[self.used])
        self.used += 1
        copy.start()
        return copy

    def rows(self, pairs, at, step):
        return [self.start(a.at[at : at + step], b.at[at : at + step]) for a, b in pairs]


def view_columns(refs, part, units):
    if len(refs) == 2:
        return refs
    return refs[0].at[:, pl.ds(0, 3 * part)], refs[0].at[:, pl.ds(3 * part, units)]


def wait_all(copies):
    for copy in copies:
        copy.wait()


def forward_kernel(
    first_len, heads, size, scale, length, step,
    gain, shift, bqkv, bup, seg_row, x_in, cos_in, sin_in, wdown_in, wproj_in, *refs,
):
    (x, cosine, sine, wdown, wproj,
     normed, q, k, v, act, slope, mixed, stat, terms, sems) = refs[-15:]
    split = (len(refs) - 24) // 2
    w_in, w = refs[:split], refs[split + 9 : 2 * split + 9]
    (n_out, q_out, k_out, v_out, act_out, slope_out, mixed_out, stat_out, terms_out) = refs[
        split : split + 9
    ]
    copier = Copier(sems)
    part = heads * size
    wqkv, wup = view_columns(w, part, act.shape[1])
    total = x.shape[0]
    starts = range(0, total, step)
    tables = ((cos_in, cosine), (sin_in, sine))
    x_copies = {0: copier.rows([(x_in, x)], 0, step)}
    w_copies = [copier.start(a, b) for a, b in zip(w_in, w)]
    t_copies = {0: copier.rows(tables, 0, step)}
    for at in starts[1:]:
        x_copies[at] = copier.rows([(x_in, x)], at, step)
        t_copies[at] = copier.rows(tables, at, step)
    w_copies += [copier.start(wdown_in, wdown), copier.start(wproj_in, wproj)]
    out = []
    for seq in range(total // length):
        origin = seq * length
        for at in range(origin, origin + length, step):
            rows = slice(at, at + step)
            wait_all(x_copies[at])
            standard, _ = standardize(x[rows, :].astype(F32))
            low = (standard * gain[...] + shift[...]).astype(BF16)
            normed[rows, :] = low
            out += copier.rows([(normed, n_out)], at, step)
            if at == 0:
                wait_all(w_copies[:split])
            full = mm(low, wqkv[...]) + bqkv[...]
            wait_all(t_copies[at])
            cos_rows, sin_rows = cosine[rows, :], sine[rows, :]
            q[rows, :] = turn(full[:, :part], cos_rows, sin_rows, size).astype(
                BF16
            ) * jnp.asarray(scale, BF16)
            k[rows, :] = turn(full[:, part : 2 * part], cos_rows, sin_rows, size).astype(BF16)
            v[rows, :] = full[:, 2 * part :].astype(BF16)
            out += copier.rows(((q, q_out), (k, k_out), (v, v_out)), at, step)
            up = mm(low, wup[...]) + bup[...]
            cdf = 0.5 * (1.0 + lax.erf(up * math.sqrt(0.5)))
            act[rows, :] = (up * cdf).astype(BF16)
            slope[rows, :] = (
                cdf + up * jnp.exp(-0.5 * up * up) * (1.0 / math.sqrt(2.0 * math.pi))
            ).astype(BF16)
            out += copier.rows(((act, act_out), (slope, slope_out)), at, step)
        for start, low in block_spans(length, first_len):
            rows, cols = slice(origin + start, origin + start + BLK), slice(
                origin + low, origin + start + BLK
            )
            query = head_stack(q[rows, :], heads, size)
            allowed = span_mask(start, low, first_len, seg_row[seq : seq + 1, :], heads)
            scores = jnp.where(allowed, mm(query, k[cols, :], LAST), NEG_FILL)
            peak = jnp.max(scores, axis=1, keepdims=True)
            grown = jnp.exp(scores - peak)
            summed = jnp.sum(grown, axis=1, keepdims=True)
            probs = (grown * (1.0 / summed)).astype(BF16)
            result = mm(probs, v[cols, :])
            mixed[rows, :] = head_pick(result, heads, size).astype(BF16)
            stat[rows, :] = head_pick(
                jnp.broadcast_to(peak + jnp.log(summed), result.shape), heads, size
            )
        out += copier.rows(((mixed, mixed_out), (stat, stat_out)), origin, length)
        if seq == 0:
            wait_all(w_copies[split:])
        for at in range(origin, origin + length, step):
            rows = slice(at, at + step)
            terms[rows, :] = (mm(act[rows, :], wdown[...]) + mm(mixed[rows, :], wproj[...])).astype(
                BF16
            )
            out += copier.rows([(terms, terms_out)], at, step)
    wait_all(out)


def backward_kernel(
    first_len, heads, size, scale, length, step, cut,
    order, seg_row, g_in, slope_in, q_in, k_in, v_in, stat_in, cos_in, sin_in, x_in, n_in,
    act_in, mixed_in, wdown_in, wproj_in, *refs,
):
    (g, slope, q, k, v, stat, cosine, sine, x, normed, act, mixed, wdown, wproj,
     mg, ug, qg, dk, dv, sems) = refs[-20:]
    split = 1 if refs[0].shape[1] > 3 * heads * size else 2
    w_in, refs = refs[:split], refs[split:-20]
    back_out, gain_sum, shift_sum, up_sum, qkv_sum, pw = refs[:6]
    outs, w = refs[6 : len(refs) - split], refs[len(refs) - split :]
    col_out, down_out = outs[: len(outs) // 2], outs[len(outs) // 2 :]
    for ref in (gain_sum, shift_sum, up_sum, qkv_sum):
        ref[...] = jnp.zeros_like(ref)
    copier = Copier(sems)
    width = heads * size
    wqkv, wup = view_columns(w, width, ug.shape[1])
    total = g.shape[0]
    loads = ((g_in, g), (slope_in, slope))
    saved = (
        (q_in, q), (k_in, k), (v_in, v), (stat_in, stat), (cos_in, cosine), (sin_in, sine)
    )
    g_copies, s_copies, x_copies = {}, {}, {}
    for at in range(0, total, step):
        g_copies[at] = copier.rows(loads[:1], at, step)
        if at == 0:
            w_copies = [copier.start(wdown_in, wdown)]
        g_copies[at] += copier.rows(loads[1:], at, step)
        if at == 0:
            w_copies.append(copier.start(wproj_in, wproj))
        if (at + step) % length == 0:
            origin = at + step - length
            s_copies[origin] = copier.rows(saved, origin, length)
            if origin == 0:
                w_copies += [copier.start(a, b) for a, b in zip(w_in, w)]
            x_copies[origin] = copier.rows([(x_in, x)], origin, length)
    late = [copier.start(a, b) for a, b in ((act_in, act), (mixed_in, mixed), (n_in, normed))]
    out = []
    for seq in range(total // length):
        origin = seq * length
        for at in range(origin, origin + length, step):
            rows = slice(at, at + step)
            wait_all(g_copies[at])
            if at == 0:
                wait_all(w_copies[:2])
            grad = g[rows, :]
            up_grad = (mm(grad, wdown[...], LAST) * slope[rows, :].astype(F32)).astype(BF16)
            ug[rows, :] = up_grad
            up_sum[...] += jnp.sum(up_grad.astype(F32), axis=0, keepdims=True)
            mg[rows, :] = mm(grad, wproj[...], LAST).astype(BF16)
        dk[...] = jnp.zeros_like(dk)
        dv[...] = jnp.zeros_like(dv)
        wait_all(s_copies[origin])
        for start, low in block_spans(length, first_len):
            stop = start + BLK
            rows, cols = slice(origin + start, origin + stop), slice(origin + low, origin + stop)
            query = head_stack(q[rows, :], heads, size)
            grad = head_stack(mg[rows, :], heads, size)
            key, value = k[cols, :], v[cols, :]
            allowed = span_mask(start, low, first_len, seg_row[seq : seq + 1, :], heads)
            peak = stat[rows, :]
            peak = jnp.concatenate(
                [peak[:, h * size : h * size + 1] for h in range(heads)], axis=0
            )
            scores = jnp.where(allowed, mm(query, key, LAST), NEG_FILL)
            probs = jnp.exp(scores - peak)
            prob_grad = mm(grad, value, LAST)
            delta = jnp.sum(probs * prob_grad, axis=1, keepdims=True)
            score_grad = (probs * (prob_grad - delta)).astype(BF16)
            dq = head_pick(mm(score_grad, key), heads, size) * scale
            qg[rows, :width] = turn(dq, cosine[rows, :], -sine[rows, :], size).astype(BF16)
            dk[low:stop, :] += mm(score_grad, query, FIRST)
            dv[low:stop, :] += mm(probs.astype(BF16), grad, FIRST)
        rows = slice(origin, origin + length)
        qg[rows, width : 2 * width] = turn(
            dk[...], cosine[rows, :], -sine[rows, :], size
        ).astype(BF16)
        qg[rows, 2 * width :] = dv[...].astype(BF16)
        wait_all(x_copies[origin])
        if seq == 0:
            wait_all(w_copies[2:])
        for at in range(origin, origin + length, step):
            rows = slice(at, at + step)
            terms = mm(ug[rows, :], wup[...], LAST) + mm(qg[rows, :], wqkv[...], LAST)
            standard, _ = standardize(x[rows, :].astype(F32))
            x[rows, :] = terms.astype(BF16)
            out += copier.rows([(x, back_out)], at, step)
            gain_sum[...] += jnp.sum(terms * standard, axis=0, keepdims=True)
            shift_sum[...] += jnp.sum(terms, axis=0, keepdims=True)
            qkv_sum[...] += jnp.sum(qg[rows, :].astype(F32), axis=0, keepdims=True)
    wait_all(late)
    for left, rights, parts in ((act, (g,), down_out), (normed, (qg, ug), col_out)):
        rows = parts[0].shape[0]
        for i, part in enumerate(parts):
            block = left[...]
            if cut:
                block = left[:, pl.ds(pl.multiple_of(order[i] * rows, rows), rows)]
            column = 0
            for right in rights:
                stop = column + right.shape[1]
                part[:, column:stop] = mm(block, right[...], FIRST).astype(part.dtype)
                column = stop
    pw[...] = mm(mixed[...], g[...], FIRST).astype(BF16)
    wait_all(out)


def loss_kernel(branch, x, teacher, valid, bias, factor, out, grad, low, column, square):
    full = x[...].astype(F32) + (branch[...].astype(F32) + bias[...])
    out[...] = full.astype(BF16)
    error = valid[...] * (full - teacher[...].astype(F32))
    square[...] = jnp.sum(jnp.sum(error * error, axis=0, keepdims=True), axis=1, keepdims=True)
    scaled = factor[...] * error
    grad[...] = scaled
    rounded = scaled.astype(BF16)
    low[...] = rounded
    column[...] = jnp.sum(rounded.astype(F32), axis=0, keepdims=True)


def norm_back_kernel(ng, x, og, gain, out):
    standard, root = standardize(x[...].astype(F32))
    inner = ng[...].astype(F32) * gain[...]
    out[...] = (
        og[...]
        + root
        * (
            inner
            - jnp.mean(inner, axis=-1, keepdims=True)
            - standard * jnp.mean(inner * standard, axis=-1, keepdims=True)
        )
    ).astype(BF16)


def head_of(local, ctx, heads, n_ctx, paired):
    if not paired:
        return ctx * heads + local
    return (heads * (ctx % 2) + local) * (n_ctx // 2) + ctx // 2


def pack_columns(heads, size, paired, units, n_dp, n_ctx, qkv_ref, up_ref, valid_ref, *refs):
    vectors, out_ref = refs[:-1], refs[-1]
    part = heads * size
    width, unit_rows = n_ctx * part, units // n_dp
    count = jnp.sum(jnp.sum(valid_ref[...].astype(F32), axis=1, keepdims=True), axis=0, keepdims=True)
    high = jnp.floor(count * (1.0 / 128.0))
    small = [
        jnp.pad(ref[...].astype(F32).reshape(1, ref.shape[0]), ((0, 0), (0, 128 - ref.shape[0])))
        for ref in vectors
    ]
    small += [jnp.broadcast_to(a, (1, 128)) for a in (high, count - 128.0 * high)]
    small = jnp.concatenate(small, axis=0).astype(BF16)
    small = jnp.concatenate([small, jnp.zeros((out_ref.shape[1] - 8, 128), BF16)], axis=0)
    for j in range(n_ctx):
        out_ref[j, :, 3 * part + units :] = small
        for p in range(3):
            at = [p * width + head_of(h, j, heads, n_ctx, paired) * size for h in range(heads)]
            out_ref[j, :, p * part : (p + 1) * part] = jnp.concatenate(
                [qkv_ref[:, a : a + size] for a in at], axis=1
            )
        for i in range(n_dp):
            at = (i * n_ctx + j) * unit_rows
            out_ref[j, :, 3 * part + i * unit_rows : 3 * part + (i + 1) * unit_rows] = up_ref[
                :, at : at + unit_rows
            ]


def unpack_columns(heads, size, paired, units, n_dp, n_ctx, in_ref, qkv_ref, up_ref):
    part = heads * size
    width, unit_rows = n_ctx * part, units // n_dp
    held = {
        head_of(h, j, heads, n_ctx, paired): (j, h) for j in range(n_ctx) for h in range(heads)
    }
    for p in range(3):
        for first in range(0, n_ctx * heads, heads):
            pieces = []
            for head in range(first, first + heads):
                j, h = held[head]
                pieces.append(in_ref[j, :, p * part : (p + 1) * part][:, h * size : (h + 1) * size])
            qkv_ref[:, p * width + first * size : p * width + (first + heads) * size] = (
                jnp.concatenate(pieces, axis=1).astype(F32)
            )
    for j in range(n_ctx):
        for i in range(n_dp):
            at = (i * n_ctx + j) * unit_rows
            up_ref[:, at : at + unit_rows] = in_ref[
                j, :, 3 * part + i * unit_rows : 3 * part + (i + 1) * unit_rows
            ].astype(F32)


def shape_of(dims, dtype):
    return jax.ShapeDtypeStruct(dims, dtype)


def row_spec(rows, *dims):
    return pl.BlockSpec((rows,) + dims, lambda s: (s,) + (0,) * len(dims))


def whole_spec(*dims):
    return pl.BlockSpec(dims, lambda s: (0,) * len(dims))


HBM = pl.BlockSpec(memory_space=pl.ANY)
LOCAL = pl.BlockSpec(memory_space=pltpu.VMEM)
SCALAR = pl.BlockSpec(memory_space=pltpu.SMEM)


def kernel_call(kernel, name, in_specs, out, scratch=(), flops=0, moved=0, grid=None):
    return pl.pallas_call(
        kernel,
        in_specs=in_specs,
        out_specs=[spec for spec, _ in out],
        out_shape=[shape for _, shape in out],
        scratch_shapes=list(scratch),
        compiler_params=PARAMS,
        cost_estimate=pl.CostEstimate(flops=flops, bytes_accessed=moved, transcendentals=0),
        name=name,
        **({"grid": grid} if grid else {}),
    )


def gather_dp(block, n_dp, me_dp):
    out = jnp.zeros((n_dp,) + block.shape, block.dtype)
    out = lax.dynamic_update_index_in_dim(out, block, me_dp, 0)
    for k in range(1, n_dp):
        pairs = [(i, i ^ k) for i in range(n_dp)]
        other = lax.ppermute(block, "dp", pairs)
        out = lax.dynamic_update_index_in_dim(out, other, me_dp ^ k, 0)
    return out.reshape((n_dp * block.shape[0],) + block.shape[1:])


def exchange_dp(terms, n_dp):
    total = terms[0]
    for k in range(1, n_dp):
        pairs = [(i, i ^ k) for i in range(n_dp)]
        total = total + lax.ppermute(terms[k], "dp", pairs).astype(F32)
    return total


def reduce_blocks(terms, cut, n_dp, me_dp):
    if cut:
        return exchange_dp(terms, n_dp)
    return reduce_dp(terms[0], n_dp, me_dp)


def reduce_dp(terms, n_dp, me_dp):
    rows = terms.shape[0] // n_dp
    blocks = terms.reshape((n_dp, rows) + terms.shape[1:])
    total = lax.dynamic_index_in_dim(blocks, me_dp, 0, keepdims=False).astype(F32)
    for k in range(1, n_dp):
        pairs = [(i, i ^ k) for i in range(n_dp)]
        block = lax.dynamic_index_in_dim(blocks, me_dp ^ k, 0, keepdims=False)
        total = total + lax.ppermute(block, "dp", pairs).astype(F32)
    return total


def body(
    n_dp, n_ctx,
    tokens, teacher, segments, positions, valid_mask,
    norm_gain, norm_bias, qkv_weight, qkv_bias, proj_weight, proj_bias,
    up_weight, up_bias, down_weight, down_bias,
):
    seqs, local_len, width = tokens.shape
    length = segments.shape[1]
    rows = seqs * local_len
    all_rows = seqs * length
    n_all = n_dp * n_ctx
    first_len = length // 2 + local_len
    heads = HEADS // n_ctx
    size = width // HEADS
    part = heads * size
    hidden = up_weight.shape[1]
    units = hidden // n_ctx
    unit_rows = down_weight.shape[0]
    own = width // n_all
    scale = 1.0 / math.sqrt(size)
    me_dp = lax.axis_index("dp")
    me_ctx = lax.axis_index("ctx")
    both = ("dp", "ctx")
    aligned = part % 128 == 0 and unit_rows % 128 == 0 and own % 16 == 0
    paired = aligned and 2 * own == size and 2 * heads == n_dp
    me_core, me_chip = me_ctx % 2, me_ctx // 2
    swap = [(j, j ^ 1) for j in range(n_ctx)]

    to_plan = [(n_dp * j + i, i * n_ctx + j) for i in range(n_dp) for j in range(n_ctx)]
    from_plan = [(b, a) for a, b in to_plan]
    valid = valid_mask.astype(F32).reshape(rows, 1)
    vectors = [norm_gain, norm_bias, proj_bias, down_bias, qkv_bias, up_bias]
    extra = 128 * max(1, 8 // own)
    total_cols = 3 * part + units + extra
    if aligned:
        cols = pl.pallas_call(
            functools.partial(pack_columns, heads, size, paired, units, n_dp, n_ctx),
            out_shape=shape_of((n_ctx, own, total_cols), BF16),
            compiler_params=PARAMS,
            name="pack_columns",
        )(qkv_weight, up_weight, valid_mask, *vectors)
    else:
        count = jnp.sum(valid_mask)
        small = jnp.stack(
            [jnp.pad(a, (0, 128 - a.shape[0])) for a in vectors]
            + [jnp.broadcast_to(a.astype(BF16), (128,)) for a in (count // 128, count % 128)]
        ).reshape(8 * 128)
        small = jnp.pad(small, (0, own * extra - 8 * 128)).reshape(own, extra)
        qkv_cols = qkv_weight.reshape(own, 3, n_ctx, part).transpose(2, 0, 1, 3)
        up_cols = up_weight.reshape(own, n_dp, n_ctx, unit_rows).transpose(2, 0, 1, 3)
        cols = jnp.concatenate(
            [
                qkv_cols.reshape(n_ctx, own, 3 * part), up_cols.reshape(n_ctx, own, units),
                jnp.broadcast_to(small[None], (n_ctx, own, extra)),
            ],
            axis=2,
        )
    tied = jnp.concatenate([down_weight, proj_weight], axis=0) if paired else down_weight
    cols, tied = lax.optimization_barrier((cols, tied))
    x_rows = lax.all_gather(tokens, "ctx", axis=1, tiled=True).reshape(all_rows, width)
    cols = lax.all_to_all(cols, "ctx", 0, 0, tiled=True).reshape(n_ctx * own, total_cols)
    cols, segments = lax.optimization_barrier((cols, segments))
    w_cols = gather_dp(cols, n_dp, me_dp)
    small = w_cols[:, 3 * part + units :].reshape(n_all, own * extra)[:, : 8 * 128]
    small = small.reshape(n_all, 8, 128).astype(F32)
    gain = small[:, 0, :own].reshape(1, width)
    shift = small[:, 1, :own].reshape(1, width)
    out_bias = (small[:, 2, :own] + small[:, 3, :own]).reshape(1, width)
    qkv_b = small[:, 4, : 3 * own]
    if paired:
        qkv_b = lax.dynamic_slice(
            qkv_b.reshape(3, 2, heads, n_ctx // 2, size), (0, me_core, 0, me_chip, 0),
            (3, 1, heads, 1, size),
        )
    else:
        qkv_b = lax.dynamic_index_in_dim(qkv_b.reshape(3, n_ctx, part), me_ctx, 1)
    qkv_b = qkv_b.reshape(1, 3 * part)
    up_b = small[:, 5, :unit_rows].reshape(n_dp, n_ctx, unit_rows)
    up_b = lax.dynamic_index_in_dim(up_b, me_ctx, 1, keepdims=False).reshape(1, units)
    valid_count = 128.0 * jnp.sum(small[:, 6, 0]) + jnp.sum(small[:, 7, 0])
    sliced = (3 * part) % 128 == 0 and units % 128 == 0
    if sliced:
        w_split = [w_cols]
    else:
        w_split = [w_cols[:, : 3 * part], w_cols[:, 3 * part : 3 * part + units]]
    token = jnp.arange(length, dtype=jnp.int32)
    half = ROT // 2
    lane = jnp.arange(part, dtype=jnp.int32) % size
    steps = jnp.arange(half, dtype=F32)
    inverse = jnp.power(10000.0, -2.0 * steps / ROT)
    lane_inverse = jnp.where(lane < ROT, inverse[lane % half], 0.0)
    same = segments[:, :, None] == segments[:, None, :]
    before = token[None, None, :] < token[None, :, None]
    in_doc = jnp.sum((same & before).astype(F32), axis=2)
    angles = in_doc.reshape(all_rows, 1) * lane_inverse[None, :]
    cosine = jnp.cos(angles)
    sine = jnp.sin(angles) * jnp.where(lane < half, -1.0, 1.0)

    tied = gather_dp(tied, n_dp, me_dp).reshape(n_dp, -1, width)
    w_down = tied[:, :unit_rows].reshape(units, width)
    if paired:
        halves = tied[:, unit_rows:].reshape(2, heads, own, width)
        keep = lax.dynamic_index_in_dim(halves, me_core, 0, keepdims=False)
        got = lax.ppermute(
            lax.dynamic_index_in_dim(halves, 1 - me_core, 0, keepdims=False), "ctx", swap
        )
        w_proj = jnp.stack(
            [jnp.where(me_core == 0, keep, got), jnp.where(me_core == 0, got, keep)], axis=1
        ).reshape(part, width)
    else:
        w_proj = gather_dp(lax.ppermute(proj_weight, both, to_plan), n_dp, me_dp)

    def wide(columns, dtype=BF16):
        return pltpu.VMEM((all_rows, columns), dtype)

    def store(columns, dtype=BF16):
        return (HBM, shape_of((all_rows, columns), dtype))

    w_scratch = [pltpu.VMEM(a.shape, BF16) for a in w_split]
    weights = [pltpu.VMEM((units, width), BF16), pltpu.VMEM((part, width), BF16)]
    sems = pltpu.SemaphoreType.DMA((COPIES,))
    normed, query, key, value, act, slope, mixed, stat, terms = kernel_call(
        functools.partial(forward_kernel, first_len, heads, size, scale, length, STEP),
        "forward_kernel",
        [LOCAL] * 5 + [HBM] * (5 + len(w_split)),
        [
            store(width), store(part), store(part), store(part), store(units), store(units),
            store(part), store(part, F32), store(width),
        ],
        [
            *w_scratch, wide(width), wide(part, F32), wide(part, F32), *weights,
            wide(width), wide(part), wide(part), wide(part), wide(units), wide(units),
            wide(part), wide(part, F32), wide(width), sems,
        ],
        flops=10 * 10**9, moved=2 * 10**7,
    )(
        gain, shift, qkv_b, up_b, segments, x_rows, cosine, sine, w_down, w_proj, *w_split
    )
    branch = lax.psum_scatter(
        terms.reshape(seqs, length, width), "ctx", scatter_dimension=1, tiled=True
    ).reshape(rows, width)

    total_tokens = seqs * n_dp * length
    factor = (total_tokens / valid_count).reshape(1, 1)
    tokens_rows = tokens.reshape(rows, width)
    own_block = (rows, width)
    layer_out, out_grad, low, column, square = kernel_call(
        loss_kernel, "loss_kernel", [LOCAL] * 6,
        [
            (LOCAL, shape_of(own_block, BF16)), (LOCAL, shape_of(own_block, F32)),
            (LOCAL, shape_of(own_block, BF16)), (LOCAL, shape_of((1, width), F32)),
            (LOCAL, shape_of((1, 1), F32)),
        ],
        flops=10**6, moved=3 * 10**6,
    )(branch, tokens_rows, teacher.reshape(rows, width), valid, out_bias, factor)

    grads = lax.all_gather(
        low.reshape(tokens.shape), "ctx", axis=1, tiled=True
    ).reshape(all_rows, width)
    order = jnp.stack([me_dp ^ k for k in range(n_dp)]).astype(jnp.int32)
    cut = (width // n_dp) % 128 == 0 and unit_rows % 128 == 0

    def blocks_of(rows_out, columns):
        if not cut:
            return [(LOCAL, shape_of((rows_out, columns), BF16))]
        block = (rows_out // n_dp, columns)
        return [(LOCAL, shape_of(block, BF16 if k else F32)) for k in range(n_dp)]

    back, gain_sum, shift_sum, up_bsum, qkv_bsum, proj_wgrad, *terms = kernel_call(
        functools.partial(backward_kernel, first_len, heads, size, scale, length, STEP, cut),
        "backward_kernel",
        [SCALAR, LOCAL] + [HBM] * (14 + len(w_split)),
        [
            store(width),
            *[(LOCAL, shape_of((1, a), F32)) for a in (width, width, units, 3 * part)],
            (LOCAL, shape_of((part, width), BF16)), *blocks_of(width, 3 * part + units),
            *blocks_of(units, width),
        ],
        [
            *w_scratch, wide(width), wide(units), wide(part), wide(part), wide(part),
            wide(part, F32), wide(part, F32), wide(part, F32), wide(width), wide(width),
            wide(units), wide(part), *weights, wide(part), wide(units), wide(3 * part), pltpu.VMEM((length, part), F32),
            pltpu.VMEM((length, part), F32), sems,
        ],
        flops=12 * 10**9, moved=2 * 10**7,
    )(
        order, segments, grads, slope, query, key, value, stat, cosine, sine, x_rows, normed,
        act, mixed, w_down, w_proj, *w_split,
    )
    col_terms, down_terms = terms[: len(terms) // 2], terms[len(terms) // 2 :]
    normed_grad = lax.psum_scatter(
        back.reshape(seqs, length, width), "ctx", scatter_dimension=1, tiled=True
    ).reshape(rows, width)

    col_wgrad = reduce_blocks(col_terms, cut, n_dp, me_dp).astype(BF16)

    if paired:
        qkv_bsum = lax.dynamic_update_slice(
            jnp.zeros((3, 2, heads, n_ctx // 2, size), F32),
            qkv_bsum.reshape(3, 1, heads, 1, size), (0, me_core, 0, me_chip, 0),
        )
    else:
        qkv_bsum = lax.dynamic_update_slice(
            jnp.zeros((3, n_ctx, part), F32), qkv_bsum.reshape(3, 1, part), (0, me_ctx, 0)
        )
    up_bsum = lax.dynamic_update_slice(
        jnp.zeros((n_dp, n_ctx, unit_rows), F32), up_bsum.reshape(n_dp, 1, unit_rows),
        (0, me_ctx, 0),
    )
    parts = [
        gain_sum.reshape(n_all, own), shift_sum.reshape(n_all, own),
        column.reshape(n_all, own), qkv_bsum[2].reshape(n_all, own),
        qkv_bsum[:2].reshape(n_all, 2 * own), up_bsum.reshape(n_all, unit_rows),
        jnp.broadcast_to(square, (n_all, 1)),
    ]
    sums = jnp.concatenate(parts, axis=1)
    sums = jnp.pad(sums, ((0, 0), (0, -sums.shape[1] % 128)))
    sums = lax.all_to_all(sums, both, 0, 0, tiled=True)
    col_wgrad, sums = lax.optimization_barrier((col_wgrad, sums))
    col_wgrad = lax.all_to_all(
        col_wgrad.reshape(n_ctx, own, 3 * part + units), "ctx", 0, 0, tiled=True
    )
    sums = jnp.sum(sums, axis=0)
    gain_grad, shift_grad, bias_grad, value_bgrad = (
        sums[k * own : (k + 1) * own] for k in range(4)
    )
    qk_bgrad = sums[4 * own : 6 * own]
    up_bgrad = sums[6 * own : 6 * own + unit_rows]
    loss = sums[6 * own + unit_rows] / (valid_count * width)

    down_wgrad = reduce_blocks(down_terms, cut, n_dp, me_dp)
    if paired:
        halves = proj_wgrad.reshape(heads, 2, own, width)
        keep = lax.dynamic_index_in_dim(halves, me_core, 1, keepdims=False)
        got = lax.ppermute(
            lax.dynamic_index_in_dim(halves, 1 - me_core, 1, keepdims=False), "ctx", swap
        )
        proj_wgrad = jnp.concatenate(
            [jnp.where(me_core == 0, keep, got), jnp.where(me_core == 0, got, keep)], axis=0
        ).reshape(n_dp * own, width)
        proj_wgrad = reduce_dp(proj_wgrad, n_dp, me_dp)
    else:
        proj_wgrad = reduce_dp(proj_wgrad, n_dp, me_dp)
        proj_wgrad = lax.ppermute(proj_wgrad.astype(BF16), both, from_plan).astype(F32)

    (input_grad,) = kernel_call(
        norm_back_kernel, "norm_back_kernel", [LOCAL] * 4, [(LOCAL, shape_of(own_block, BF16))],
        flops=10**6, moved=3 * 10**6,
    )(normed_grad, tokens_rows, out_grad, gain)
    if aligned:
        qkv_wgrad, up_wgrad = pl.pallas_call(
            functools.partial(unpack_columns, heads, size, paired, units, n_dp, n_ctx),
            out_shape=[shape_of((own, 3 * width), F32), shape_of((own, hidden), F32)],
            compiler_params=PARAMS,
            name="unpack_columns",
        )(col_wgrad)
    else:
        qkv_wgrad = (
            col_wgrad[:, :, : 3 * part].reshape(n_ctx, own, 3, part).transpose(1, 2, 0, 3)
        ).reshape(own, 3 * width).astype(F32)
        up_wgrad = (
            col_wgrad[:, :, 3 * part :].reshape(n_ctx, own, n_dp, unit_rows).transpose(1, 2, 0, 3)
        ).reshape(own, hidden).astype(F32)

    return (
        layer_out.reshape(tokens.shape), loss, input_grad.reshape(tokens.shape), gain_grad,
        shift_grad, qkv_wgrad, qk_bgrad, value_bgrad, proj_wgrad, bias_grad, up_wgrad, up_bgrad,
        down_wgrad, bias_grad,
    )


def solution(mesh):
    n_dp, n_ctx = mesh.shape["dp"], mesh.shape["ctx"]
    seq, flat = P("dp", "ctx", None), P(("dp", "ctx"))
    mat = P(("dp", "ctx"), None)
    in_specs = (
        seq, seq, P("dp", None), P("dp", "ctx"), P("dp", "ctx"),
        flat, flat, mat, flat, mat, flat, mat, flat, mat, flat,
    )
    out_specs = (seq, P(), seq, flat, flat, mat, flat, flat, mat, flat, mat, flat, mat, flat)
    return jax.shard_map(
        functools.partial(body, n_dp, n_ctx),
        mesh=mesh, in_specs=in_specs, out_specs=out_specs, check_vma=False,
    )
```

```python
import functools
import math

import jax
import jax.numpy as jnp
from jax import lax
from jax.experimental import pallas as pl
from jax.experimental.pallas import tpu as pltpu
from jax.sharding import PartitionSpec as P

HEADS = 16
ROT = 16
BLK = 128
NEG_FILL = -1000000000.0
F32 = jnp.float32
BF16 = jnp.bfloat16
PARAMS = pltpu.CompilerParams(vmem_limit_bytes=56 * 1024 * 1024)
COPIES = 128
STEP = 512
TOGETHER = 2
LAST = ((1,), (1,))
FIRST = ((0,), (0,))


def mm(a, b, dims=((1,), (0,))):
    return lax.dot_general(a, b, (dims, ((), ())), preferred_element_type=F32)


def block_spans(length, first_len):
    return [(at, 0 if at < first_len else first_len) for at in range(0, length, BLK)]


def head_stack(rows, heads, size):
    lane = lax.broadcasted_iota(jnp.int32, rows.shape, 1) // size
    parts = [jnp.where(lane == h, rows, jnp.zeros_like(rows)) for h in range(heads)]
    return parts[0] if heads == 1 else jnp.concatenate(parts, axis=0)


def head_pick(stacked, heads, size):
    rows = stacked.shape[0] // heads
    out = stacked[:rows]
    lane = lax.broadcasted_iota(jnp.int32, out.shape, 1) // size
    for h in range(1, heads):
        out = jnp.where(lane == h, stacked[h * rows : (h + 1) * rows], out)
    return out


def turn(values, cosine, sine, size):
    half = ROT // 2
    width = values.shape[1]
    place = lax.broadcasted_iota(jnp.int32, values.shape, 1) % size
    partner = jnp.where(
        place < half,
        pltpu.roll(values, width - half, 1),
        pltpu.roll(values, half, 1),
    )
    return values * cosine + partner * sine


def mask_scores(scores, start, low, first_len, seg_row, heads):
    shape = (heads * BLK, BLK)
    row = lax.rem(lax.broadcasted_iota(jnp.int32, shape, 0), BLK)
    causal = lax.broadcasted_iota(jnp.int32, shape, 1) <= row
    if low < first_len:
        last = jnp.where(causal, scores[:, start - low :], NEG_FILL)
        return last if start == low else jnp.concatenate([scores[:, : start - low], last], axis=1)
    own = jnp.transpose(jnp.broadcast_to(seg_row[:, start : start + BLK], (BLK, BLK)))
    own = jnp.concatenate([own] * heads, axis=0)
    parts = []
    for at in range(low, start + BLK, BLK):
        allowed = own == seg_row[:, at : at + BLK]
        if at == start:
            allowed = allowed & causal
        parts.append(jnp.where(allowed, scores[:, at - low : at - low + BLK], NEG_FILL))
    return jnp.concatenate(parts, axis=1)


def in_step(chains):
    chains = list(chains)
    while chains:
        chains = [chain for chain in chains if next(chain, "over") != "over"]


def grouped(items, count):
    return [items[at : at + count] for at in range(0, len(items), count)]


def standardize(rows):
    centered = rows - jnp.mean(rows, axis=-1, keepdims=True)
    variance = jnp.mean(centered * centered, axis=-1, keepdims=True)
    root = lax.rsqrt(variance + 1e-05)
    return centered * root, root


class Copier:
    def __init__(self, sems):
        self.sems, self.used = sems, 0

    def start(self, source, target):
        copy = pltpu.make_async_copy(source, target, self.sems.at[self.used])
        self.used += 1
        copy.start()
        return copy

    def rows(self, pairs, at, step):
        return [self.start(a.at[at : at + step], b.at[at : at + step]) for a, b in pairs]


def view_columns(refs, part, units):
    if len(refs) == 2:
        return refs
    return refs[0].at[:, pl.ds(0, 3 * part)], refs[0].at[:, pl.ds(3 * part, units)]


def wait_all(copies):
    for copy in copies:
        copy.wait()


def forward_kernel(
    first_len, heads, size, scale, length, step,
    gain, shift, bqkv, bup, seg_row, x_in, cos_in, sin_in, wdown_in, wproj_in, *refs,
):
    (x, cosine, sine, wdown, wproj,
     normed, q, k, v, act, slope, mixed, stat, terms, sems) = refs[-15:]
    split = (len(refs) - 24) // 2
    w_in, w = refs[:split], refs[split + 9 : 2 * split + 9]
    (n_out, q_out, k_out, v_out, act_out, slope_out, mixed_out, stat_out, terms_out) = refs[
        split : split + 9
    ]
    copier = Copier(sems)
    part = heads * size
    wqkv, wup = view_columns(w, part, act.shape[1])
    total = x.shape[0]
    starts = range(0, total, step)
    tables = ((cos_in, cosine), (sin_in, sine))
    x_copies = {0: copier.rows([(x_in, x)], 0, step)}
    w_copies = [copier.start(a, b) for a, b in zip(w_in, w)]
    t_copies = {0: copier.rows(tables, 0, step)}
    for at in starts[1:]:
        x_copies[at] = copier.rows([(x_in, x)], at, step)
        t_copies[at] = copier.rows(tables, at, step)
    w_copies += [copier.start(wdown_in, wdown), copier.start(wproj_in, wproj)]
    out = []
    seqs = total // length
    for origin in range(0, total, length):
        for at in range(origin, origin + length, step):
            rows = slice(at, at + step)
            wait_all(x_copies[at])
            standard, _ = standardize(x[rows, :].astype(F32))
            low = (standard * gain[...] + shift[...]).astype(BF16)
            normed[rows, :] = low
            out += copier.rows([(normed, n_out)], at, step)
            if at == 0:
                wait_all(w_copies[:split])
            full = mm(low, wqkv[...]) + bqkv[...]
            wait_all(t_copies[at])
            cos_rows, sin_rows = cosine[rows, :], sine[rows, :]
            q[rows, :] = turn(full[:, :part], cos_rows, sin_rows, size).astype(
                BF16
            ) * jnp.asarray(scale, BF16)
            k[rows, :] = turn(full[:, part : 2 * part], cos_rows, sin_rows, size).astype(BF16)
            v[rows, :] = full[:, 2 * part :].astype(BF16)
            out += copier.rows(((q, q_out), (k, k_out), (v, v_out)), at, step)
            up = mm(low, wup[...]) + bup[...]
            cdf = 0.5 * (1.0 + lax.erf(up * math.sqrt(0.5)))
            act[rows, :] = (up * cdf).astype(BF16)
            slope[rows, :] = (
                cdf + up * jnp.exp(-0.5 * up * up) * (1.0 / math.sqrt(2.0 * math.pi))
            ).astype(BF16)
            out += copier.rows(((act, act_out), (slope, slope_out)), at, step)

    def attend(seq, start, low):
        origin = seq * length
        rows = slice(origin + start, origin + start + BLK)
        cols = slice(origin + low, origin + start + BLK)
        query = head_stack(q[rows, :], heads, size)
        yield
        scores = mm(query, k[cols, :], LAST)
        yield
        scores = mask_scores(scores, start, low, first_len, seg_row[seq : seq + 1, :], heads)
        peak = jnp.max(scores, axis=1, keepdims=True)
        yield
        grown = jnp.exp(scores - peak)
        summed = jnp.sum(grown, axis=1, keepdims=True)
        yield
        probs = (grown * (1.0 / summed)).astype(BF16)
        yield
        result = mm(probs, v[cols, :])
        yield
        mixed[rows, :] = head_pick(result, heads, size).astype(BF16)
        stat[rows, :] = head_pick(
            jnp.broadcast_to(peak + jnp.log(summed), result.shape), heads, size
        )

    for spans in grouped(block_spans(length, first_len), TOGETHER):
        in_step(attend(seq, start, low) for start, low in spans for seq in range(seqs))
    out += copier.rows(((mixed, mixed_out), (stat, stat_out)), 0, total)
    wait_all(w_copies[split:])
    for at in range(0, total, step):
        rows = slice(at, at + step)
        terms[rows, :] = (mm(act[rows, :], wdown[...]) + mm(mixed[rows, :], wproj[...])).astype(
            BF16
        )
        out += copier.rows([(terms, terms_out)], at, step)
    wait_all(out)


def backward_kernel(
    first_len, heads, size, scale, length, step, cut,
    order, seg_row, g_in, slope_in, q_in, k_in, v_in, stat_in, cos_in, sin_in, x_in, n_in,
    wdown_in, wproj_in, *refs,
):
    (g, slope, q, k, v, stat, cosine, sine, x, normed, wdown, wproj,
     mg, ug, qg, dk, dv, sems) = refs[-18:]
    split = 1 if refs[0].shape[1] > 3 * heads * size else 2
    w_in, refs = refs[:split], refs[split:-18]
    back_out, gain_sum, shift_sum, up_sum, qkv_sum = refs[:5]
    col_out, w = refs[5 : len(refs) - split], refs[len(refs) - split :]
    for ref in (gain_sum, shift_sum, up_sum, qkv_sum):
        ref[...] = jnp.zeros_like(ref)
    copier = Copier(sems)
    width = heads * size
    wqkv, wup = view_columns(w, width, ug.shape[1])
    total = g.shape[0]
    loads = ((g_in, g), (slope_in, slope))
    saved = (
        (q_in, q), (k_in, k), (v_in, v), (stat_in, stat), (cos_in, cosine), (sin_in, sine)
    )
    g_copies, s_copies, x_copies = {}, {}, {}
    for at in range(0, total, step):
        g_copies[at] = copier.rows(loads[:1], at, step)
        if at == 0:
            w_copies = [copier.start(wdown_in, wdown)]
        g_copies[at] += copier.rows(loads[1:], at, step)
        if at == 0:
            w_copies.append(copier.start(wproj_in, wproj))
        if (at + step) % length == 0:
            origin = at + step - length
            s_copies[origin] = copier.rows(saved, origin, length)
            if origin == 0:
                w_copies += [copier.start(a, b) for a, b in zip(w_in, w)]
            x_copies[origin] = copier.rows([(x_in, x)], origin, length)
    late = [copier.start(n_in, normed)]
    out = []
    for seq in range(total // length):
        origin = seq * length
        for at in range(origin, origin + length, step):
            rows = slice(at, at + step)
            wait_all(g_copies[at])
            if at == 0:
                wait_all(w_copies[:2])
            grad = g[rows, :]
            up_grad = (mm(grad, wdown[...], LAST) * slope[rows, :].astype(F32)).astype(BF16)
            ug[rows, :] = up_grad
            up_sum[...] += jnp.sum(up_grad.astype(F32), axis=0, keepdims=True)
            mg[rows, :] = mm(grad, wproj[...], LAST).astype(BF16)
    dk[...] = jnp.zeros_like(dk)
    dv[...] = jnp.zeros_like(dv)
    for origin in s_copies:
        wait_all(s_copies[origin])

    def attend(seq, start, low):
        origin = seq * length
        stop = start + BLK
        rows, cols = slice(origin + start, origin + stop), slice(origin + low, origin + stop)
        query = head_stack(q[rows, :], heads, size)
        grad = head_stack(mg[rows, :], heads, size)
        key, value = k[cols, :], v[cols, :]
        yield
        scores = mm(query, key, LAST)
        yield
        prob_grad = mm(grad, value, LAST)
        yield
        peak = stat[rows, :]
        peak = jnp.concatenate([peak[:, h * size : h * size + 1] for h in range(heads)], axis=0)
        scores = mask_scores(scores, start, low, first_len, seg_row[seq : seq + 1, :], heads)
        probs = jnp.exp(scores - peak)
        yield
        delta = jnp.sum(probs * prob_grad, axis=1, keepdims=True)
        yield
        score_grad = (probs * (prob_grad - delta)).astype(BF16)
        yield
        dq = mm(score_grad, key)
        yield
        dk[cols, :] += mm(score_grad, query, FIRST)
        yield
        dv[cols, :] += mm(probs.astype(BF16), grad, FIRST)
        yield
        dq = head_pick(dq, heads, size) * scale
        qg[rows, :width] = turn(dq, cosine[rows, :], -sine[rows, :], size).astype(BF16)

    for spans in grouped(block_spans(length, first_len), 1):
        in_step(
            attend(seq, start, low) for start, low in spans for seq in range(total // length)
        )
    for at in range(0, total, step):
        rows = slice(at, at + step)
        qg[rows, width : 2 * width] = turn(
            dk[rows, :], cosine[rows, :], -sine[rows, :], size
        ).astype(BF16)
        qg[rows, 2 * width :] = dv[rows, :].astype(BF16)
    for origin in x_copies:
        wait_all(x_copies[origin])
    wait_all(w_copies[2:])
    for at in range(0, total, step):
        rows = slice(at, at + step)
        terms = mm(ug[rows, :], wup[...], LAST) + mm(qg[rows, :], wqkv[...], LAST)
        standard, _ = standardize(x[rows, :].astype(F32))
        x[rows, :] = terms.astype(BF16)
        out += copier.rows([(x, back_out)], at, step)
        gain_sum[...] += jnp.sum(terms * standard, axis=0, keepdims=True)
        shift_sum[...] += jnp.sum(terms, axis=0, keepdims=True)
        qkv_sum[...] += jnp.sum(qg[rows, :].astype(F32), axis=0, keepdims=True)
    wait_all(late)
    weight_blocks(cut, order, normed, (qg, ug), col_out)
    wait_all(out)


def weight_blocks(cut, order, left, rights, outs):
    rows = outs[0].shape[0]
    for i, part in enumerate(outs):
        block = left[...]
        if cut:
            block = left[:, pl.ds(pl.multiple_of(order[i] * rows, rows), rows)]
        column = 0
        for right in rights:
            stop = column + right.shape[1]
            part[:, column:stop] = mm(block, right[...], FIRST).astype(part.dtype)
            column = stop


def down_kernel(cut, order, act, mixed, g, pw, *outs):
    weight_blocks(cut, order, act, (g,), outs)
    pw[...] = mm(mixed[...], g[...], FIRST).astype(BF16)


def loss_kernel(branch, x, teacher, valid, bias, factor, out, grad, low, column, square):
    full = x[...].astype(F32) + (branch[...].astype(F32) + bias[...])
    out[...] = full.astype(BF16)
    error = valid[...] * (full - teacher[...].astype(F32))
    square[...] = jnp.sum(jnp.sum(error * error, axis=0, keepdims=True), axis=1, keepdims=True)
    scaled = factor[...] * error
    grad[...] = scaled
    rounded = scaled.astype(BF16)
    low[...] = rounded
    column[...] = jnp.sum(rounded.astype(F32), axis=0, keepdims=True)


def norm_back_kernel(ng, x, og, gain, out):
    standard, root = standardize(x[...].astype(F32))
    inner = ng[...].astype(F32) * gain[...]
    out[...] = (
        og[...]
        + root
        * (
            inner
            - jnp.mean(inner, axis=-1, keepdims=True)
            - standard * jnp.mean(inner * standard, axis=-1, keepdims=True)
        )
    ).astype(BF16)


def head_of(local, ctx, heads, n_ctx, paired):
    if not paired:
        return ctx * heads + local
    return (heads * (ctx % 2) + local) * (n_ctx // 2) + ctx // 2


def pack_columns(heads, size, paired, units, n_dp, n_ctx, qkv_ref, up_ref, valid_ref, *refs):
    vectors, out_ref, small_ref = refs[:-2], refs[-2], refs[-1]
    part = heads * size
    width, unit_rows = n_ctx * part, units // n_dp
    count = jnp.sum(jnp.sum(valid_ref[...].astype(F32), axis=1, keepdims=True), axis=0, keepdims=True)
    high = jnp.floor(count * (1.0 / 128.0))
    small = [
        jnp.pad(ref[...].astype(F32).reshape(1, ref.shape[0]), ((0, 0), (0, 128 - ref.shape[0])))
        for ref in vectors
    ]
    small += [jnp.broadcast_to(a, (1, 128)) for a in (high, count - 128.0 * high)]
    small = jnp.concatenate(small, axis=0).astype(BF16)
    for j in range(small_ref.shape[0]):
        small_ref[j] = small
    for j in range(n_ctx):
        for p in range(3):
            at = [p * width + head_of(h, j, heads, n_ctx, paired) * size for h in range(heads)]
            out_ref[j, :, p * part : (p + 1) * part] = jnp.concatenate(
                [qkv_ref[:, a : a + size] for a in at], axis=1
            )
        for i in range(n_dp):
            at = (i * n_ctx + j) * unit_rows
            out_ref[j, :, 3 * part + i * unit_rows : 3 * part + (i + 1) * unit_rows] = up_ref[
                :, at : at + unit_rows
            ]


def unpack_columns(heads, size, paired, units, n_dp, n_ctx, in_ref, qkv_ref, up_ref):
    part = heads * size
    width, unit_rows = n_ctx * part, units // n_dp
    held = {
        head_of(h, j, heads, n_ctx, paired): (j, h) for j in range(n_ctx) for h in range(heads)
    }
    for p in range(3):
        for first in range(0, n_ctx * heads, heads):
            pieces = []
            for head in range(first, first + heads):
                j, h = held[head]
                pieces.append(in_ref[j, :, p * part : (p + 1) * part][:, h * size : (h + 1) * size])
            qkv_ref[:, p * width + first * size : p * width + (first + heads) * size] = (
                jnp.concatenate(pieces, axis=1).astype(F32)
            )
    for j in range(n_ctx):
        for i in range(n_dp):
            at = (i * n_ctx + j) * unit_rows
            up_ref[:, at : at + unit_rows] = in_ref[
                j, :, 3 * part + i * unit_rows : 3 * part + (i + 1) * unit_rows
            ].astype(F32)


def shape_of(dims, dtype):
    return jax.ShapeDtypeStruct(dims, dtype)


def row_spec(rows, *dims):
    return pl.BlockSpec((rows,) + dims, lambda s: (s,) + (0,) * len(dims))


def whole_spec(*dims):
    return pl.BlockSpec(dims, lambda s: (0,) * len(dims))


HBM = pl.BlockSpec(memory_space=pl.ANY)
LOCAL = pl.BlockSpec(memory_space=pltpu.VMEM)
SCALAR = pl.BlockSpec(memory_space=pltpu.SMEM)


def kernel_call(kernel, name, in_specs, out, scratch=(), flops=0, moved=0, grid=None):
    return pl.pallas_call(
        kernel,
        in_specs=in_specs,
        out_specs=[spec for spec, _ in out],
        out_shape=[shape for _, shape in out],
        scratch_shapes=list(scratch),
        compiler_params=PARAMS,
        cost_estimate=pl.CostEstimate(flops=flops, bytes_accessed=moved, transcendentals=0),
        name=name,
        **({"grid": grid} if grid else {}),
    )


def gather_dp(block, n_dp, me_dp):
    out = jnp.zeros((n_dp,) + block.shape, block.dtype)
    out = lax.dynamic_update_index_in_dim(out, block, me_dp, 0)
    for k in range(1, n_dp):
        pairs = [(i, i ^ k) for i in range(n_dp)]
        other = lax.ppermute(block, "dp", pairs)
        out = lax.dynamic_update_index_in_dim(out, other, me_dp ^ k, 0)
    return out.reshape((n_dp * block.shape[0],) + block.shape[1:])


def reduce_blocks(terms, cut, n_dp, me_dp, later=None):
    if not cut:
        return reduce_dp(terms[0], n_dp, me_dp), later
    parts = [
        lax.ppermute(terms[k], "dp", [(i, i ^ k) for i in range(n_dp)]) for k in range(1, n_dp)
    ]
    if later is not None:
        parts[0], later = lax.optimization_barrier((parts[0], later))
    total = terms[0]
    for part in parts:
        total = total + part.astype(F32)
    return total, later


def reduce_dp(terms, n_dp, me_dp):
    rows = terms.shape[0] // n_dp
    blocks = terms.reshape((n_dp, rows) + terms.shape[1:])
    total = lax.dynamic_index_in_dim(blocks, me_dp, 0, keepdims=False).astype(F32)
    for k in range(1, n_dp):
        pairs = [(i, i ^ k) for i in range(n_dp)]
        block = lax.dynamic_index_in_dim(blocks, me_dp ^ k, 0, keepdims=False)
        total = total + lax.ppermute(block, "dp", pairs).astype(F32)
    return total


def body(
    n_dp, n_ctx,
    tokens, teacher, segments, positions, valid_mask,
    norm_gain, norm_bias, qkv_weight, qkv_bias, proj_weight, proj_bias,
    up_weight, up_bias, down_weight, down_bias,
):
    seqs, local_len, width = tokens.shape
    length = segments.shape[1]
    rows = seqs * local_len
    all_rows = seqs * length
    n_all = n_dp * n_ctx
    first_len = length // 2 + local_len
    heads = HEADS // n_ctx
    size = width // HEADS
    part = heads * size
    hidden = up_weight.shape[1]
    units = hidden // n_ctx
    unit_rows = down_weight.shape[0]
    own = width // n_all
    scale = 1.0 / math.sqrt(size)
    me_dp = lax.axis_index("dp")
    me_ctx = lax.axis_index("ctx")
    both = ("dp", "ctx")
    aligned = part % 128 == 0 and unit_rows % 128 == 0 and own % 16 == 0
    paired = aligned and 2 * own == size and 2 * heads == n_dp
    me_core, me_chip = me_ctx % 2, me_ctx // 2
    swap = [(j, j ^ 1) for j in range(n_ctx)]

    to_plan = [(n_dp * j + i, i * n_ctx + j) for i in range(n_dp) for j in range(n_ctx)]
    from_plan = [(b, a) for a, b in to_plan]
    valid = valid_mask.astype(F32).reshape(rows, 1)
    vectors = [norm_gain, norm_bias, proj_bias, down_bias, qkv_bias, up_bias]
    total_cols = 3 * part + units
    if aligned:
        cols, small = pl.pallas_call(
            functools.partial(pack_columns, heads, size, paired, units, n_dp, n_ctx),
            out_shape=[
                shape_of((n_ctx, own, total_cols), BF16), shape_of((n_all, 8, 128), BF16)
            ],
            compiler_params=PARAMS,
            name="pack_columns",
        )(qkv_weight, up_weight, valid_mask, *vectors)
    else:
        count = jnp.sum(valid_mask)
        small = jnp.stack(
            [jnp.pad(a, (0, 128 - a.shape[0])) for a in vectors]
            + [jnp.broadcast_to(a.astype(BF16), (128,)) for a in (count // 128, count % 128)]
        )
        small = jnp.broadcast_to(small[None], (n_all, 8, 128))
        qkv_cols = qkv_weight.reshape(own, 3, n_ctx, part).transpose(2, 0, 1, 3)
        up_cols = up_weight.reshape(own, n_dp, n_ctx, unit_rows).transpose(2, 0, 1, 3)
        cols = jnp.concatenate(
            [
                qkv_cols.reshape(n_ctx, own, 3 * part), up_cols.reshape(n_ctx, own, units),
            ],
            axis=2,
        )
    tied = jnp.concatenate([down_weight, proj_weight], axis=0) if paired else down_weight
    cols, tied = lax.optimization_barrier((cols, tied))
    x_rows = lax.all_gather(tokens, "ctx", axis=1, tiled=True).reshape(all_rows, width)
    cols = lax.all_to_all(cols, "ctx", 0, 0, tiled=True).reshape(n_ctx * own, total_cols)
    cols, segments, small = lax.optimization_barrier((cols, segments, small))
    w_cols = gather_dp(cols, n_dp, me_dp)
    small = lax.all_to_all(small, both, 0, 0, tiled=True).astype(F32)
    gain = small[:, 0, :own].reshape(1, width)
    shift = small[:, 1, :own].reshape(1, width)
    out_bias = (small[:, 2, :own] + small[:, 3, :own]).reshape(1, width)
    qkv_b = small[:, 4, : 3 * own]
    if paired:
        qkv_b = lax.dynamic_slice(
            qkv_b.reshape(3, 2, heads, n_ctx // 2, size), (0, me_core, 0, me_chip, 0),
            (3, 1, heads, 1, size),
        )
    else:
        qkv_b = lax.dynamic_index_in_dim(qkv_b.reshape(3, n_ctx, part), me_ctx, 1)
    qkv_b = qkv_b.reshape(1, 3 * part)
    up_b = small[:, 5, :unit_rows].reshape(n_dp, n_ctx, unit_rows)
    up_b = lax.dynamic_index_in_dim(up_b, me_ctx, 1, keepdims=False).reshape(1, units)
    valid_count = 128.0 * jnp.sum(small[:, 6, 0]) + jnp.sum(small[:, 7, 0])
    sliced = (3 * part) % 128 == 0 and units % 128 == 0
    if sliced:
        w_split = [w_cols]
    else:
        w_split = [w_cols[:, : 3 * part], w_cols[:, 3 * part : 3 * part + units]]
    token = jnp.arange(length, dtype=jnp.int32)
    half = ROT // 2
    lane = jnp.arange(part, dtype=jnp.int32) % size
    steps = jnp.arange(half, dtype=F32)
    inverse = jnp.power(10000.0, -2.0 * steps / ROT)
    lane_inverse = jnp.where(lane < ROT, inverse[lane % half], 0.0)
    same = segments[:, :, None] == segments[:, None, :]
    before = token[None, None, :] < token[None, :, None]
    in_doc = jnp.sum((same & before).astype(F32), axis=2)
    angles = in_doc.reshape(all_rows, 1) * lane_inverse[None, :]
    cosine = jnp.cos(angles)
    sine = jnp.sin(angles) * jnp.where(lane < half, -1.0, 1.0)

    tied = gather_dp(tied, n_dp, me_dp).reshape(n_dp, -1, width)
    w_down = tied[:, :unit_rows].reshape(units, width)
    if paired:
        halves = tied[:, unit_rows:].reshape(2, heads, own, width)
        keep = lax.dynamic_index_in_dim(halves, me_core, 0, keepdims=False)
        got = lax.ppermute(
            lax.dynamic_index_in_dim(halves, 1 - me_core, 0, keepdims=False), "ctx", swap
        )
        w_proj = jnp.stack(
            [jnp.where(me_core == 0, keep, got), jnp.where(me_core == 0, got, keep)], axis=1
        ).reshape(part, width)
    else:
        w_proj = gather_dp(lax.ppermute(proj_weight, both, to_plan), n_dp, me_dp)

    def wide(columns, dtype=BF16):
        return pltpu.VMEM((all_rows, columns), dtype)

    def store(columns, dtype=BF16):
        return (HBM, shape_of((all_rows, columns), dtype))

    w_scratch = [pltpu.VMEM(a.shape, BF16) for a in w_split]
    weights = [pltpu.VMEM((units, width), BF16), pltpu.VMEM((part, width), BF16)]
    sems = pltpu.SemaphoreType.DMA((COPIES,))
    normed, query, key, value, act, slope, mixed, stat, terms = kernel_call(
        functools.partial(forward_kernel, first_len, heads, size, scale, length, STEP),
        "forward_kernel",
        [LOCAL] * 5 + [HBM] * (5 + len(w_split)),
        [
            store(width), store(part), store(part), store(part), store(units), store(units),
            store(part), store(part, F32), store(width),
        ],
        [
            *w_scratch, wide(width), wide(part, F32), wide(part, F32), *weights,
            wide(width), wide(part), wide(part), wide(part), wide(units), wide(units),
            wide(part), wide(part, F32), wide(width), sems,
        ],
        flops=10 * 10**9, moved=2 * 10**7,
    )(
        gain, shift, qkv_b, up_b, segments, x_rows, cosine, sine, w_down, w_proj, *w_split
    )
    branch = lax.psum_scatter(
        terms.reshape(seqs, length, width), "ctx", scatter_dimension=1, tiled=True
    ).reshape(rows, width)

    total_tokens = seqs * n_dp * length
    factor = (total_tokens / valid_count).reshape(1, 1)
    tokens_rows = tokens.reshape(rows, width)
    own_block = (rows, width)
    layer_out, out_grad, low, column, square = kernel_call(
        loss_kernel, "loss_kernel", [LOCAL] * 6,
        [
            (LOCAL, shape_of(own_block, BF16)), (LOCAL, shape_of(own_block, F32)),
            (LOCAL, shape_of(own_block, BF16)), (LOCAL, shape_of((1, width), F32)),
            (LOCAL, shape_of((1, 1), F32)),
        ],
        flops=10**6, moved=3 * 10**6,
    )(branch, tokens_rows, teacher.reshape(rows, width), valid, out_bias, factor)

    grads = lax.all_gather(
        low.reshape(tokens.shape), "ctx", axis=1, tiled=True
    ).reshape(all_rows, width)
    order = jnp.stack([me_dp ^ k for k in range(n_dp)]).astype(jnp.int32)
    cut = (width // n_dp) % 128 == 0 and unit_rows % 128 == 0

    def blocks_of(rows_out, columns):
        if not cut:
            return [(LOCAL, shape_of((rows_out, columns), BF16))]
        block = (rows_out // n_dp, columns)
        return [(LOCAL, shape_of(block, BF16 if k else F32)) for k in range(n_dp)]

    back, gain_sum, shift_sum, up_bsum, qkv_bsum, *col_terms = kernel_call(
        functools.partial(backward_kernel, first_len, heads, size, scale, length, STEP, cut),
        "backward_kernel",
        [SCALAR, LOCAL] + [HBM] * (12 + len(w_split)),
        [
            store(width),
            *[(LOCAL, shape_of((1, a), F32)) for a in (width, width, units, 3 * part)],
            *blocks_of(width, 3 * part + units),
        ],
        [
            *w_scratch, wide(width), wide(units), wide(part), wide(part), wide(part),
            wide(part, F32), wide(part, F32), wide(part, F32), wide(width), wide(width),
            *weights, wide(part), wide(units), wide(3 * part), wide(part, F32),
            wide(part, F32), sems,
        ],
        flops=12 * 10**9, moved=2 * 10**7,
    )(
        order, segments, grads, slope, query, key, value, stat, cosine, sine, x_rows, normed,
        w_down, w_proj, *w_split,
    )
    normed_grad = lax.psum_scatter(
        back.reshape(seqs, length, width), "ctx", scatter_dimension=1, tiled=True
    ).reshape(rows, width)

    col_wgrad, act = reduce_blocks(col_terms, cut, n_dp, me_dp, act)
    col_wgrad = col_wgrad.astype(BF16)

    if paired:
        qkv_bsum = lax.dynamic_update_slice(
            jnp.zeros((3, 2, heads, n_ctx // 2, size), F32),
            qkv_bsum.reshape(3, 1, heads, 1, size), (0, me_core, 0, me_chip, 0),
        )
    else:
        qkv_bsum = lax.dynamic_update_slice(
            jnp.zeros((3, n_ctx, part), F32), qkv_bsum.reshape(3, 1, part), (0, me_ctx, 0)
        )
    up_bsum = lax.dynamic_update_slice(
        jnp.zeros((n_dp, n_ctx, unit_rows), F32), up_bsum.reshape(n_dp, 1, unit_rows),
        (0, me_ctx, 0),
    )
    parts = [
        gain_sum.reshape(n_all, own), shift_sum.reshape(n_all, own),
        column.reshape(n_all, own), qkv_bsum[2].reshape(n_all, own),
        qkv_bsum[:2].reshape(n_all, 2 * own), up_bsum.reshape(n_all, unit_rows),
        jnp.broadcast_to(square, (n_all, 1)),
    ]
    sums = jnp.concatenate(parts, axis=1)
    sums = jnp.pad(sums, ((0, 0), (0, -sums.shape[1] % 128)))
    sums, act = lax.optimization_barrier((sums, act))
    sums = lax.all_to_all(sums, both, 0, 0, tiled=True)
    col_wgrad, sums = lax.optimization_barrier((col_wgrad, sums))
    col_wgrad = lax.all_to_all(
        col_wgrad.reshape(n_ctx, own, 3 * part + units), "ctx", 0, 0, tiled=True
    )
    sums = jnp.sum(sums, axis=0)
    gain_grad, shift_grad, bias_grad, value_bgrad = (
        sums[k * own : (k + 1) * own] for k in range(4)
    )
    qk_bgrad = sums[4 * own : 6 * own]
    up_bgrad = sums[6 * own : 6 * own + unit_rows]
    loss = sums[6 * own + unit_rows] / (valid_count * width)

    proj_wgrad, *down_terms = kernel_call(
        functools.partial(down_kernel, cut), "down_kernel", [SCALAR] + [LOCAL] * 3,
        [(LOCAL, shape_of((part, width), BF16)), *blocks_of(units, width)],
        flops=10**6, moved=10**5,
    )(order, act, mixed, grads)
    down_wgrad, _ = reduce_blocks(down_terms, cut, n_dp, me_dp)
    if paired:
        halves = proj_wgrad.reshape(heads, 2, own, width)
        keep = lax.dynamic_index_in_dim(halves, me_core, 1, keepdims=False)
        got = lax.ppermute(
            lax.dynamic_index_in_dim(halves, 1 - me_core, 1, keepdims=False), "ctx", swap
        )
        proj_wgrad = jnp.concatenate(
            [jnp.where(me_core == 0, keep, got), jnp.where(me_core == 0, got, keep)], axis=0
        ).reshape(n_dp * own, width)
        proj_wgrad = reduce_dp(proj_wgrad, n_dp, me_dp)
    else:
        proj_wgrad = reduce_dp(proj_wgrad, n_dp, me_dp)
        proj_wgrad = lax.ppermute(proj_wgrad.astype(BF16), both, from_plan).astype(F32)

    (input_grad,) = kernel_call(
        norm_back_kernel, "norm_back_kernel", [LOCAL] * 4, [(LOCAL, shape_of(own_block, BF16))],
        flops=10**6, moved=3 * 10**6,
    )(normed_grad, tokens_rows, out_grad, gain)
    if aligned:
        qkv_wgrad, up_wgrad = pl.pallas_call(
            functools.partial(unpack_columns, heads, size, paired, units, n_dp, n_ctx),
            out_shape=[shape_of((own, 3 * width), F32), shape_of((own, hidden), F32)],
            compiler_params=PARAMS,
            name="unpack_columns",
        )(col_wgrad)
    else:
        qkv_wgrad = (
            col_wgrad[:, :, : 3 * part].reshape(n_ctx, own, 3, part).transpose(1, 2, 0, 3)
        ).reshape(own, 3 * width).astype(F32)
        up_wgrad = (
            col_wgrad[:, :, 3 * part :].reshape(n_ctx, own, n_dp, unit_rows).transpose(1, 2, 0, 3)
        ).reshape(own, hidden).astype(F32)

    return (
        layer_out.reshape(tokens.shape), loss, input_grad.reshape(tokens.shape), gain_grad,
        shift_grad, qkv_wgrad, qk_bgrad, value_bgrad, proj_wgrad, bias_grad, up_wgrad, up_bgrad,
        down_wgrad, bias_grad,
    )


def solution(mesh):
    n_dp, n_ctx = mesh.shape["dp"], mesh.shape["ctx"]
    seq, flat = P("dp", "ctx", None), P(("dp", "ctx"))
    mat = P(("dp", "ctx"), None)
    in_specs = (
        seq, seq, P("dp", None), P("dp", "ctx"), P("dp", "ctx"),
        flat, flat, mat, flat, mat, flat, mat, flat, mat, flat,
    )
    out_specs = (seq, P(), seq, flat, flat, mat, flat, flat, mat, flat, mat, flat, mat, flat)
    return jax.shard_map(
        functools.partial(body, n_dp, n_ctx),
        mesh=mesh, in_specs=in_specs, out_specs=out_specs, check_vma=False,
    )
```

```python
import functools
import math

import jax
import jax.numpy as jnp
from jax import lax
from jax.experimental import pallas as pl
from jax.experimental.pallas import tpu as pltpu
from jax.sharding import PartitionSpec as P

HEADS = 16
ROT = 16
BLK = 128
NEG_FILL = -1000000000.0
F32 = jnp.float32
BF16 = jnp.bfloat16
PARAMS = pltpu.CompilerParams(vmem_limit_bytes=56 * 1024 * 1024)
COPIES = 128
STEP = 512
TOGETHER = 4
LAST = ((1,), (1,))
FIRST = ((0,), (0,))


def mm(a, b, dims=((1,), (0,))):
    return lax.dot_general(a, b, (dims, ((), ())), preferred_element_type=F32)


def block_spans(length, first_len):
    return [(at, 0 if at < first_len else first_len) for at in range(0, length, BLK)]


def head_stack(rows, heads, size):
    lane = lax.broadcasted_iota(jnp.int32, rows.shape, 1) // size
    parts = [jnp.where(lane == h, rows, jnp.zeros_like(rows)) for h in range(heads)]
    return parts[0] if heads == 1 else jnp.concatenate(parts, axis=0)


def head_pick(stacked, heads, size):
    rows = stacked.shape[0] // heads
    out = stacked[:rows]
    lane = lax.broadcasted_iota(jnp.int32, out.shape, 1) // size
    for h in range(1, heads):
        out = jnp.where(lane == h, stacked[h * rows : (h + 1) * rows], out)
    return out


def turn(values, cosine, sine, size):
    half = ROT // 2
    width = values.shape[1]
    place = lax.broadcasted_iota(jnp.int32, values.shape, 1) % size
    partner = jnp.where(
        place < half,
        pltpu.roll(values, width - half, 1),
        pltpu.roll(values, half, 1),
    )
    return values * cosine + partner * sine


def mask_scores(scores, start, low, first_len, seg_row, heads):
    shape = (heads * BLK, BLK)
    row = lax.rem(lax.broadcasted_iota(jnp.int32, shape, 0), BLK)
    causal = lax.broadcasted_iota(jnp.int32, shape, 1) <= row
    if low < first_len:
        last = jnp.where(causal, scores[:, start - low :], NEG_FILL)
        return last if start == low else jnp.concatenate([scores[:, : start - low], last], axis=1)
    own = jnp.transpose(jnp.broadcast_to(seg_row[:, start : start + BLK], (BLK, BLK)))
    own = jnp.concatenate([own] * heads, axis=0)
    parts = []
    for at in range(low, start + BLK, BLK):
        allowed = own == seg_row[:, at : at + BLK]
        if at == start:
            allowed = allowed & causal
        parts.append(jnp.where(allowed, scores[:, at - low : at - low + BLK], NEG_FILL))
    return jnp.concatenate(parts, axis=1)


def in_step(chains):
    chains = list(chains)
    while chains:
        chains = [chain for chain in chains if next(chain, "over") != "over"]


def grouped(items, count):
    return [items[at : at + count] for at in range(0, len(items), count)]


def standardize(rows):
    centered = rows - jnp.mean(rows, axis=-1, keepdims=True)
    variance = jnp.mean(centered * centered, axis=-1, keepdims=True)
    root = lax.rsqrt(variance + 1e-05)
    return centered * root, root


class Copier:
    def __init__(self, sems):
        self.sems, self.used = sems, 0

    def start(self, source, target):
        copy = pltpu.make_async_copy(source, target, self.sems.at[self.used])
        self.used += 1
        copy.start()
        return copy

    def rows(self, pairs, at, step):
        return [self.start(a.at[at : at + step], b.at[at : at + step]) for a, b in pairs]


def fetch_columns(copier, order, sources, targets):
    if len(targets) == 2:
        return [copier.start(a, b) for a, b in zip(sources, targets)]
    rows = sources[0].shape[0]
    return [
        copier.start(a, targets[0].at[pl.ds(pl.multiple_of(order[k] * rows, rows), rows)])
        for k, a in enumerate(sources)
    ]


def view_columns(refs, part, units):
    if len(refs) == 2:
        return refs
    return refs[0].at[:, pl.ds(0, 3 * part)], refs[0].at[:, pl.ds(3 * part, units)]


def wait_all(copies):
    for copy in copies:
        copy.wait()


def forward_kernel(
    first_len, heads, size, scale, length, step, split,
    order, gain, shift, bqkv, bup, seg_row, x_in, cos_in, sin_in, wdown_in, wproj_in, *refs,
):
    (x, cosine, sine, wdown, wproj,
     normed, q, k, v, act, slope, mixed, stat, terms, sems) = refs[-15:]
    w_in, w = refs[:split], refs[split + 9 : -15]
    (n_out, q_out, k_out, v_out, act_out, slope_out, mixed_out, stat_out, terms_out) = refs[
        split : split + 9
    ]
    copier = Copier(sems)
    part = heads * size
    wqkv, wup = view_columns(w, part, act.shape[1])
    total = x.shape[0]
    starts = range(0, total, step)
    tables = ((cos_in, cosine), (sin_in, sine))
    x_copies = {0: copier.rows([(x_in, x)], 0, step)}
    w_copies = fetch_columns(copier, order, w_in, w)
    t_copies = {0: copier.rows(tables, 0, step)}
    for at in starts[1:]:
        x_copies[at] = copier.rows([(x_in, x)], at, step)
        t_copies[at] = copier.rows(tables, at, step)
    w_copies += [copier.start(wdown_in, wdown), copier.start(wproj_in, wproj)]
    out = []
    seqs = total // length
    for origin in range(0, total, length):
        for at in range(origin, origin + length, step):
            rows = slice(at, at + step)
            wait_all(x_copies[at])
            standard, _ = standardize(x[rows, :].astype(F32))
            low = (standard * gain[...] + shift[...]).astype(BF16)
            normed[rows, :] = low
            out += copier.rows([(normed, n_out)], at, step)
            if at == 0:
                wait_all(w_copies[:split])
            full = mm(low, wqkv[...]) + bqkv[...]
            wait_all(t_copies[at])
            cos_rows, sin_rows = cosine[rows, :], sine[rows, :]
            q[rows, :] = turn(full[:, :part], cos_rows, sin_rows, size).astype(
                BF16
            ) * jnp.asarray(scale, BF16)
            k[rows, :] = turn(full[:, part : 2 * part], cos_rows, sin_rows, size).astype(BF16)
            v[rows, :] = full[:, 2 * part :].astype(BF16)
            out += copier.rows(((q, q_out), (k, k_out), (v, v_out)), at, step)
            up = mm(low, wup[...]) + bup[...]
            cdf = 0.5 * (1.0 + lax.erf(up * math.sqrt(0.5)))
            act[rows, :] = (up * cdf).astype(BF16)
            slope[rows, :] = (
                cdf + up * jnp.exp(-0.5 * up * up) * (1.0 / math.sqrt(2.0 * math.pi))
            ).astype(BF16)
            out += copier.rows(((act, act_out), (slope, slope_out)), at, step)

    def attend(seq, start, low):
        origin = seq * length
        rows = slice(origin + start, origin + start + BLK)
        cols = slice(origin + low, origin + start + BLK)
        query = head_stack(q[rows, :], heads, size)
        yield
        scores = mm(query, k[cols, :], LAST)
        yield
        scores = mask_scores(scores, start, low, first_len, seg_row[seq : seq + 1, :], heads)
        peak = jnp.max(scores, axis=1, keepdims=True)
        yield
        grown = jnp.exp(scores - peak)
        summed = jnp.sum(grown, axis=1, keepdims=True)
        yield
        probs = (grown * (1.0 / summed)).astype(BF16)
        yield
        result = mm(probs, v[cols, :])
        yield
        mixed[rows, :] = head_pick(result, heads, size).astype(BF16)
        stat[rows, :] = head_pick(
            jnp.broadcast_to(peak + jnp.log(summed), result.shape), heads, size
        )

    for spans in grouped(block_spans(length, first_len), TOGETHER):
        in_step(attend(seq, start, low) for start, low in spans for seq in range(seqs))
    out += copier.rows(((mixed, mixed_out), (stat, stat_out)), 0, total)
    wait_all(w_copies[split:])
    for at in range(0, total, step):
        rows = slice(at, at + step)
        terms[rows, :] = (mm(act[rows, :], wdown[...]) + mm(mixed[rows, :], wproj[...])).astype(
            BF16
        )
        out += copier.rows([(terms, terms_out)], at, step)
    wait_all(out)


def backward_kernel(
    first_len, heads, size, scale, length, step, cut, split,
    order, seg_row, g_in, slope_in, q_in, k_in, v_in, stat_in, cos_in, sin_in, x_in, n_in,
    wdown_in, wproj_in, *refs,
):
    (g, slope, q, k, v, stat, cosine, sine, x, normed, wdown, wproj,
     mg, ug, qg, dk, dv, sems) = refs[-18:]
    w_in, refs = refs[:split], refs[split:-18]
    back_out, gain_sum, shift_sum, up_sum, qkv_sum = refs[:5]
    held = 2 if split == 2 else 1
    col_out, w = refs[5 : len(refs) - held], refs[len(refs) - held :]
    for ref in (gain_sum, shift_sum, up_sum, qkv_sum):
        ref[...] = jnp.zeros_like(ref)
    copier = Copier(sems)
    width = heads * size
    wqkv, wup = view_columns(w, width, ug.shape[1])
    total = g.shape[0]
    loads = ((g_in, g), (slope_in, slope))
    saved = (
        (q_in, q), (k_in, k), (v_in, v), (stat_in, stat), (cos_in, cosine), (sin_in, sine)
    )
    g_copies, s_copies, x_copies = {}, {}, {}
    for at in range(0, total, step):
        g_copies[at] = copier.rows(loads[:1], at, step)
        if at == 0:
            w_copies = [copier.start(wdown_in, wdown)]
        g_copies[at] += copier.rows(loads[1:], at, step)
        if at == 0:
            w_copies.append(copier.start(wproj_in, wproj))
        if (at + step) % length == 0:
            origin = at + step - length
            s_copies[origin] = copier.rows(saved, origin, length)
            if origin == 0:
                w_copies += fetch_columns(copier, order, w_in, w)
            x_copies[origin] = copier.rows([(x_in, x)], origin, length)
    late = [copier.start(n_in, normed)]
    out = []
    for seq in range(total // length):
        origin = seq * length
        for at in range(origin, origin + length, step):
            rows = slice(at, at + step)
            wait_all(g_copies[at])
            if at == 0:
                wait_all(w_copies[:2])
            grad = g[rows, :]
            up_grad = (mm(grad, wdown[...], LAST) * slope[rows, :].astype(F32)).astype(BF16)
            ug[rows, :] = up_grad
            up_sum[...] += jnp.sum(up_grad.astype(F32), axis=0, keepdims=True)
            mg[rows, :] = mm(grad, wproj[...], LAST).astype(BF16)
    dk[...] = jnp.zeros_like(dk)
    dv[...] = jnp.zeros_like(dv)
    for origin in s_copies:
        wait_all(s_copies[origin])

    def attend(seq, start, low):
        origin = seq * length
        stop = start + BLK
        rows, cols = slice(origin + start, origin + stop), slice(origin + low, origin + stop)
        query = head_stack(q[rows, :], heads, size)
        grad = head_stack(mg[rows, :], heads, size)
        key, value = k[cols, :], v[cols, :]
        yield
        scores = mm(query, key, LAST)
        yield
        prob_grad = mm(grad, value, LAST)
        yield
        peak = stat[rows, :]
        peak = jnp.concatenate([peak[:, h * size : h * size + 1] for h in range(heads)], axis=0)
        scores = mask_scores(scores, start, low, first_len, seg_row[seq : seq + 1, :], heads)
        probs = jnp.exp(scores - peak)
        yield
        delta = jnp.sum(probs * prob_grad, axis=1, keepdims=True)
        yield
        score_grad = (probs * (prob_grad - delta)).astype(BF16)
        yield
        dq = mm(score_grad, key)
        yield
        dk[cols, :] += mm(score_grad, query, FIRST)
        yield
        dv[cols, :] += mm(probs.astype(BF16), grad, FIRST)
        yield
        dq = head_pick(dq, heads, size) * scale
        qg[rows, :width] = turn(dq, cosine[rows, :], -sine[rows, :], size).astype(BF16)

    for spans in grouped(block_spans(length, first_len), 1):
        in_step(
            attend(seq, start, low) for start, low in spans for seq in range(total // length)
        )
    for at in range(0, total, step):
        rows = slice(at, at + step)
        qg[rows, width : 2 * width] = turn(
            dk[rows, :], cosine[rows, :], -sine[rows, :], size
        ).astype(BF16)
        qg[rows, 2 * width :] = dv[rows, :].astype(BF16)
    for origin in x_copies:
        wait_all(x_copies[origin])
    wait_all(w_copies[2:])
    for at in range(0, total, step):
        rows = slice(at, at + step)
        terms = mm(ug[rows, :], wup[...], LAST) + mm(qg[rows, :], wqkv[...], LAST)
        standard, _ = standardize(x[rows, :].astype(F32))
        x[rows, :] = terms.astype(BF16)
        out += copier.rows([(x, back_out)], at, step)
        gain_sum[...] += jnp.sum(terms * standard, axis=0, keepdims=True)
        shift_sum[...] += jnp.sum(terms, axis=0, keepdims=True)
        qkv_sum[...] += jnp.sum(qg[rows, :].astype(F32), axis=0, keepdims=True)
    wait_all(late)
    weight_blocks(cut, order, normed, (qg, ug), col_out)
    wait_all(out)


def weight_blocks(cut, order, left, rights, outs):
    rows = outs[0].shape[0]
    for i, part in enumerate(outs):
        block = left[...]
        if cut:
            block = left[:, pl.ds(pl.multiple_of(order[i] * rows, rows), rows)]
        column = 0
        for right in rights:
            stop = column + right.shape[1]
            part[:, column:stop] = mm(block, right[...], FIRST).astype(part.dtype)
            column = stop


def down_kernel(cut, order, act, mixed, g, pw, *outs):
    weight_blocks(cut, order, act, (g,), outs)
    pw[...] = mm(mixed[...], g[...], FIRST).astype(BF16)


def loss_terms(branch, x, teacher, valid, bias, factor):
    full = x[...].astype(F32) + (branch[...].astype(F32) + bias[...])
    error = valid[...] * (full - teacher[...].astype(F32))
    return full, error, factor[...] * error


def loss_kernel(branch, x, teacher, valid, bias, factor, low):
    low[...] = loss_terms(branch, x, teacher, valid, bias, factor)[2].astype(BF16)


def output_kernel(branch, x, teacher, valid, bias, factor, out, grad, column, square):
    full, error, scaled = loss_terms(branch, x, teacher, valid, bias, factor)
    out[...] = full.astype(BF16)
    grad[...] = scaled
    square[...] = jnp.sum(jnp.sum(error * error, axis=0, keepdims=True), axis=1, keepdims=True)
    column[...] = jnp.sum(scaled.astype(BF16).astype(F32), axis=0, keepdims=True)


def norm_back_kernel(ng, x, og, gain, out):
    standard, root = standardize(x[...].astype(F32))
    inner = ng[...].astype(F32) * gain[...]
    out[...] = (
        og[...]
        + root
        * (
            inner
            - jnp.mean(inner, axis=-1, keepdims=True)
            - standard * jnp.mean(inner * standard, axis=-1, keepdims=True)
        )
    ).astype(BF16)


def head_of(local, ctx, heads, n_ctx, paired):
    if not paired:
        return ctx * heads + local
    return (heads * (ctx % 2) + local) * (n_ctx // 2) + ctx // 2


def pack_columns(heads, size, paired, units, n_dp, n_ctx, qkv_ref, up_ref, valid_ref, *refs):
    vectors, out_ref, small_ref = refs[:-2], refs[-2], refs[-1]
    part = heads * size
    width, unit_rows = n_ctx * part, units // n_dp
    count = jnp.sum(jnp.sum(valid_ref[...].astype(F32), axis=1, keepdims=True), axis=0, keepdims=True)
    high = jnp.floor(count * (1.0 / 128.0))
    small = [
        jnp.pad(ref[...].astype(F32).reshape(1, ref.shape[0]), ((0, 0), (0, 128 - ref.shape[0])))
        for ref in vectors
    ]
    small += [jnp.broadcast_to(a, (1, 128)) for a in (high, count - 128.0 * high)]
    small = jnp.concatenate(small, axis=0).astype(BF16)
    for j in range(small_ref.shape[0]):
        small_ref[j] = small
    for j in range(n_ctx):
        for p in range(3):
            at = [p * width + head_of(h, j, heads, n_ctx, paired) * size for h in range(heads)]
            out_ref[j, :, p * part : (p + 1) * part] = jnp.concatenate(
                [qkv_ref[:, a : a + size] for a in at], axis=1
            )
        for i in range(n_dp):
            at = (i * n_ctx + j) * unit_rows
            out_ref[j, :, 3 * part + i * unit_rows : 3 * part + (i + 1) * unit_rows] = up_ref[
                :, at : at + unit_rows
            ]


def unpack_columns(heads, size, paired, units, n_dp, n_ctx, in_ref, qkv_ref, up_ref):
    part = heads * size
    width, unit_rows = n_ctx * part, units // n_dp
    held = {
        head_of(h, j, heads, n_ctx, paired): (j, h) for j in range(n_ctx) for h in range(heads)
    }
    for p in range(3):
        for first in range(0, n_ctx * heads, heads):
            pieces = []
            for head in range(first, first + heads):
                j, h = held[head]
                pieces.append(in_ref[j, :, p * part : (p + 1) * part][:, h * size : (h + 1) * size])
            qkv_ref[:, p * width + first * size : p * width + (first + heads) * size] = (
                jnp.concatenate(pieces, axis=1).astype(F32)
            )
    for j in range(n_ctx):
        for i in range(n_dp):
            at = (i * n_ctx + j) * unit_rows
            up_ref[:, at : at + unit_rows] = in_ref[
                j, :, 3 * part + i * unit_rows : 3 * part + (i + 1) * unit_rows
            ].astype(F32)


def shape_of(dims, dtype):
    return jax.ShapeDtypeStruct(dims, dtype)


def row_spec(rows, *dims):
    return pl.BlockSpec((rows,) + dims, lambda s: (s,) + (0,) * len(dims))


def whole_spec(*dims):
    return pl.BlockSpec(dims, lambda s: (0,) * len(dims))


HBM = pl.BlockSpec(memory_space=pl.ANY)
LOCAL = pl.BlockSpec(memory_space=pltpu.VMEM)
SCALAR = pl.BlockSpec(memory_space=pltpu.SMEM)


def kernel_call(kernel, name, in_specs, out, scratch=(), flops=0, moved=0, grid=None):
    return pl.pallas_call(
        kernel,
        in_specs=in_specs,
        out_specs=[spec for spec, _ in out],
        out_shape=[shape for _, shape in out],
        scratch_shapes=list(scratch),
        compiler_params=PARAMS,
        cost_estimate=pl.CostEstimate(flops=flops, bytes_accessed=moved, transcendentals=0),
        name=name,
        **({"grid": grid} if grid else {}),
    )


def gather_dp(block, n_dp, me_dp):
    out = jnp.zeros((n_dp,) + block.shape, block.dtype)
    out = lax.dynamic_update_index_in_dim(out, block, me_dp, 0)
    for k in range(1, n_dp):
        pairs = [(i, i ^ k) for i in range(n_dp)]
        other = lax.ppermute(block, "dp", pairs)
        out = lax.dynamic_update_index_in_dim(out, other, me_dp ^ k, 0)
    return out.reshape((n_dp * block.shape[0],) + block.shape[1:])


def reduce_blocks(terms, cut, n_dp, me_dp, later=None):
    if not cut:
        return reduce_dp(terms[0], n_dp, me_dp), later
    parts = [
        lax.ppermute(terms[k], "dp", [(i, i ^ k) for i in range(n_dp)]) for k in range(1, n_dp)
    ]
    if later is not None:
        parts[0], later = lax.optimization_barrier((parts[0], later))
    total = terms[0]
    for part in parts:
        total = total + part.astype(F32)
    return total, later


def reduce_dp(terms, n_dp, me_dp):
    rows = terms.shape[0] // n_dp
    blocks = terms.reshape((n_dp, rows) + terms.shape[1:])
    total = lax.dynamic_index_in_dim(blocks, me_dp, 0, keepdims=False).astype(F32)
    for k in range(1, n_dp):
        pairs = [(i, i ^ k) for i in range(n_dp)]
        block = lax.dynamic_index_in_dim(blocks, me_dp ^ k, 0, keepdims=False)
        total = total + lax.ppermute(block, "dp", pairs).astype(F32)
    return total


def body(
    n_dp, n_ctx,
    tokens, teacher, segments, positions, valid_mask,
    norm_gain, norm_bias, qkv_weight, qkv_bias, proj_weight, proj_bias,
    up_weight, up_bias, down_weight, down_bias,
):
    seqs, local_len, width = tokens.shape
    length = segments.shape[1]
    rows = seqs * local_len
    all_rows = seqs * length
    n_all = n_dp * n_ctx
    first_len = length // 2 + local_len
    heads = HEADS // n_ctx
    size = width // HEADS
    part = heads * size
    hidden = up_weight.shape[1]
    units = hidden // n_ctx
    unit_rows = down_weight.shape[0]
    own = width // n_all
    scale = 1.0 / math.sqrt(size)
    me_dp = lax.axis_index("dp")
    me_ctx = lax.axis_index("ctx")
    both = ("dp", "ctx")
    aligned = part % 128 == 0 and unit_rows % 128 == 0 and own % 16 == 0
    paired = aligned and 2 * own == size and 2 * heads == n_dp
    me_core, me_chip = me_ctx % 2, me_ctx // 2
    swap = [(j, j ^ 1) for j in range(n_ctx)]

    to_plan = [(n_dp * j + i, i * n_ctx + j) for i in range(n_dp) for j in range(n_ctx)]
    from_plan = [(b, a) for a, b in to_plan]
    valid = valid_mask.astype(F32).reshape(rows, 1)
    vectors = [norm_gain, norm_bias, proj_bias, down_bias, qkv_bias, up_bias]
    total_cols = 3 * part + units
    if aligned:
        cols, small = pl.pallas_call(
            functools.partial(pack_columns, heads, size, paired, units, n_dp, n_ctx),
            out_shape=[
                shape_of((n_ctx, own, total_cols), BF16), shape_of((n_all, 8, 128), BF16)
            ],
            compiler_params=PARAMS,
            name="pack_columns",
        )(qkv_weight, up_weight, valid_mask, *vectors)
    else:
        count = jnp.sum(valid_mask)
        small = jnp.stack(
            [jnp.pad(a, (0, 128 - a.shape[0])) for a in vectors]
            + [jnp.broadcast_to(a.astype(BF16), (128,)) for a in (count // 128, count % 128)]
        )
        small = jnp.broadcast_to(small[None], (n_all, 8, 128))
        qkv_cols = qkv_weight.reshape(own, 3, n_ctx, part).transpose(2, 0, 1, 3)
        up_cols = up_weight.reshape(own, n_dp, n_ctx, unit_rows).transpose(2, 0, 1, 3)
        cols = jnp.concatenate(
            [
                qkv_cols.reshape(n_ctx, own, 3 * part), up_cols.reshape(n_ctx, own, units),
            ],
            axis=2,
        )
    tied = jnp.concatenate([down_weight, proj_weight], axis=0) if paired else down_weight
    cols, tied = lax.optimization_barrier((cols, tied))
    x_rows = lax.all_gather(tokens, "ctx", axis=1, tiled=True).reshape(all_rows, width)
    cols = lax.all_to_all(cols, "ctx", 0, 0, tiled=True).reshape(n_ctx * own, total_cols)
    cols, segments, small = lax.optimization_barrier((cols, segments, small))
    small = lax.all_to_all(small, both, 0, 0, tiled=True).astype(F32)
    gain = small[:, 0, :own].reshape(1, width)
    shift = small[:, 1, :own].reshape(1, width)
    out_bias = (small[:, 2, :own] + small[:, 3, :own]).reshape(1, width)
    qkv_b = small[:, 4, : 3 * own]
    if paired:
        qkv_b = lax.dynamic_slice(
            qkv_b.reshape(3, 2, heads, n_ctx // 2, size), (0, me_core, 0, me_chip, 0),
            (3, 1, heads, 1, size),
        )
    else:
        qkv_b = lax.dynamic_index_in_dim(qkv_b.reshape(3, n_ctx, part), me_ctx, 1)
    qkv_b = qkv_b.reshape(1, 3 * part)
    up_b = small[:, 5, :unit_rows].reshape(n_dp, n_ctx, unit_rows)
    up_b = lax.dynamic_index_in_dim(up_b, me_ctx, 1, keepdims=False).reshape(1, units)
    valid_count = 128.0 * jnp.sum(small[:, 6, 0]) + jnp.sum(small[:, 7, 0])
    sliced = (3 * part) % 128 == 0 and units % 128 == 0
    order = jnp.stack([me_dp ^ k for k in range(n_dp)]).astype(jnp.int32)
    if sliced and n_dp > 2:
        w_split = [cols] + [
            lax.ppermute(cols, "dp", [(i, i ^ k) for i in range(n_dp)]) for k in range(1, n_dp)
        ]
        w_scratch = [pltpu.VMEM((width, total_cols), BF16)]
    else:
        w_cols = gather_dp(cols, n_dp, me_dp)
        w_split = [w_cols[:, : 3 * part], w_cols[:, 3 * part : 3 * part + units]]
        w_scratch = [pltpu.VMEM(a.shape, BF16) for a in w_split]
    token = jnp.arange(length, dtype=jnp.int32)
    half = ROT // 2
    lane = jnp.arange(part, dtype=jnp.int32) % size
    steps = jnp.arange(half, dtype=F32)
    inverse = jnp.power(10000.0, -2.0 * steps / ROT)
    lane_inverse = jnp.where(lane < ROT, inverse[lane % half], 0.0)
    same = segments[:, :, None] == segments[:, None, :]
    before = token[None, None, :] < token[None, :, None]
    in_doc = jnp.sum((same & before).astype(F32), axis=2)
    angles = in_doc.reshape(all_rows, 1) * lane_inverse[None, :]
    cosine = jnp.cos(angles)
    sine = jnp.sin(angles) * jnp.where(lane < half, -1.0, 1.0)

    tied = gather_dp(tied, n_dp, me_dp).reshape(n_dp, -1, width)
    w_down = tied[:, :unit_rows].reshape(units, width)
    if paired:
        halves = tied[:, unit_rows:].reshape(2, heads, own, width)
        keep = lax.dynamic_index_in_dim(halves, me_core, 0, keepdims=False)
        got = lax.ppermute(
            lax.dynamic_index_in_dim(halves, 1 - me_core, 0, keepdims=False), "ctx", swap
        )
        w_proj = jnp.stack(
            [jnp.where(me_core == 0, keep, got), jnp.where(me_core == 0, got, keep)], axis=1
        ).reshape(part, width)
    else:
        w_proj = gather_dp(lax.ppermute(proj_weight, both, to_plan), n_dp, me_dp)

    def wide(columns, dtype=BF16):
        return pltpu.VMEM((all_rows, columns), dtype)

    def store(columns, dtype=BF16):
        return (HBM, shape_of((all_rows, columns), dtype))

    weights = [pltpu.VMEM((units, width), BF16), pltpu.VMEM((part, width), BF16)]
    sems = pltpu.SemaphoreType.DMA((COPIES,))
    normed, query, key, value, act, slope, mixed, stat, terms = kernel_call(
        functools.partial(
            forward_kernel, first_len, heads, size, scale, length, STEP, len(w_split)
        ),
        "forward_kernel",
        [SCALAR] + [LOCAL] * 5 + [HBM] * (5 + len(w_split)),
        [
            store(width), store(part), store(part), store(part), store(units), store(units),
            store(part), store(part, F32), store(width),
        ],
        [
            *w_scratch, wide(width), wide(part, F32), wide(part, F32), *weights,
            wide(width), wide(part), wide(part), wide(part), wide(units), wide(units),
            wide(part), wide(part, F32), wide(width), sems,
        ],
        flops=10 * 10**9, moved=2 * 10**7,
    )(
        order, gain, shift, qkv_b, up_b, segments, x_rows, cosine, sine, w_down, w_proj, *w_split
    )
    branch = lax.psum_scatter(
        terms.reshape(seqs, length, width), "ctx", scatter_dimension=1, tiled=True
    ).reshape(rows, width)

    total_tokens = seqs * n_dp * length
    factor = (total_tokens / valid_count).reshape(1, 1)
    tokens_rows = tokens.reshape(rows, width)
    own_block = (rows, width)
    loss_in = (branch, tokens_rows, teacher.reshape(rows, width), valid, out_bias, factor)
    (low,) = kernel_call(
        loss_kernel, "loss_kernel", [LOCAL] * 6, [(LOCAL, shape_of(own_block, BF16))],
        flops=10**6, moved=2 * 10**6,
    )(*loss_in)
    low, *loss_in = lax.optimization_barrier((low, *loss_in))
    layer_out, out_grad, column, square = kernel_call(
        output_kernel, "output_kernel", [LOCAL] * 6,
        [
            (LOCAL, shape_of(own_block, BF16)), (LOCAL, shape_of(own_block, F32)),
            (LOCAL, shape_of((1, width), F32)), (LOCAL, shape_of((1, 1), F32)),
        ],
        flops=10**6, moved=3 * 10**6,
    )(*loss_in)

    grads = lax.all_gather(
        low.reshape(tokens.shape), "ctx", axis=1, tiled=True
    ).reshape(all_rows, width)
    cut = (width // n_dp) % 128 == 0 and unit_rows % 128 == 0

    def blocks_of(rows_out, columns):
        if not cut:
            return [(LOCAL, shape_of((rows_out, columns), BF16))]
        block = (rows_out // n_dp, columns)
        return [(LOCAL, shape_of(block, BF16 if k else F32)) for k in range(n_dp)]

    back, gain_sum, shift_sum, up_bsum, qkv_bsum, *col_terms = kernel_call(
        functools.partial(
            backward_kernel, first_len, heads, size, scale, length, STEP, cut, len(w_split)
        ),
        "backward_kernel",
        [SCALAR, LOCAL] + [HBM] * (12 + len(w_split)),
        [
            store(width),
            *[(LOCAL, shape_of((1, a), F32)) for a in (width, width, units, 3 * part)],
            *blocks_of(width, 3 * part + units),
        ],
        [
            *w_scratch, wide(width), wide(units), wide(part), wide(part), wide(part),
            wide(part, F32), wide(part, F32), wide(part, F32), wide(width), wide(width),
            *weights, wide(part), wide(units), wide(3 * part), wide(part, F32),
            wide(part, F32), sems,
        ],
        flops=12 * 10**9, moved=2 * 10**7,
    )(
        order, segments, grads, slope, query, key, value, stat, cosine, sine, x_rows, normed,
        w_down, w_proj, *w_split,
    )
    normed_grad = lax.psum_scatter(
        back.reshape(seqs, length, width), "ctx", scatter_dimension=1, tiled=True
    ).reshape(rows, width)

    col_wgrad, act = reduce_blocks(col_terms, cut, n_dp, me_dp, act)
    col_wgrad = col_wgrad.astype(BF16)

    if paired:
        qkv_bsum = lax.dynamic_update_slice(
            jnp.zeros((3, 2, heads, n_ctx // 2, size), F32),
            qkv_bsum.reshape(3, 1, heads, 1, size), (0, me_core, 0, me_chip, 0),
        )
    else:
        qkv_bsum = lax.dynamic_update_slice(
            jnp.zeros((3, n_ctx, part), F32), qkv_bsum.reshape(3, 1, part), (0, me_ctx, 0)
        )
    up_bsum = lax.dynamic_update_slice(
        jnp.zeros((n_dp, n_ctx, unit_rows), F32), up_bsum.reshape(n_dp, 1, unit_rows),
        (0, me_ctx, 0),
    )
    parts = [
        gain_sum.reshape(n_all, own), shift_sum.reshape(n_all, own),
        column.reshape(n_all, own), qkv_bsum[2].reshape(n_all, own),
        qkv_bsum[:2].reshape(n_all, 2 * own), up_bsum.reshape(n_all, unit_rows),
        jnp.broadcast_to(square, (n_all, 1)),
    ]
    sums = jnp.concatenate(parts, axis=1)
    sums = jnp.pad(sums, ((0, 0), (0, -sums.shape[1] % 128)))
    sums, act = lax.optimization_barrier((sums, act))
    sums = lax.all_to_all(sums, both, 0, 0, tiled=True)
    col_wgrad, sums = lax.optimization_barrier((col_wgrad, sums))
    col_wgrad = lax.all_to_all(
        col_wgrad.reshape(n_ctx, own, 3 * part + units), "ctx", 0, 0, tiled=True
    )
    sums = jnp.sum(sums, axis=0)
    gain_grad, shift_grad, bias_grad, value_bgrad = (
        sums[k * own : (k + 1) * own] for k in range(4)
    )
    qk_bgrad = sums[4 * own : 6 * own]
    up_bgrad = sums[6 * own : 6 * own + unit_rows]
    loss = sums[6 * own + unit_rows] / (valid_count * width)

    proj_wgrad, *down_terms = kernel_call(
        functools.partial(down_kernel, cut), "down_kernel", [SCALAR] + [LOCAL] * 3,
        [(LOCAL, shape_of((part, width), BF16)), *blocks_of(units, width)],
        flops=10**6, moved=10**5,
    )(order, act, mixed, grads)
    down_wgrad, _ = reduce_blocks(down_terms, cut, n_dp, me_dp)
    if paired:
        halves = proj_wgrad.reshape(heads, 2, own, width)
        keep = lax.dynamic_index_in_dim(halves, me_core, 1, keepdims=False)
        got = lax.ppermute(
            lax.dynamic_index_in_dim(halves, 1 - me_core, 1, keepdims=False), "ctx", swap
        )
        proj_wgrad = jnp.concatenate(
            [jnp.where(me_core == 0, keep, got), jnp.where(me_core == 0, got, keep)], axis=0
        ).reshape(n_dp * own, width)
        proj_wgrad = reduce_dp(proj_wgrad, n_dp, me_dp)
    else:
        proj_wgrad = reduce_dp(proj_wgrad, n_dp, me_dp)
        proj_wgrad = lax.ppermute(proj_wgrad.astype(BF16), both, from_plan).astype(F32)

    (input_grad,) = kernel_call(
        norm_back_kernel, "norm_back_kernel", [LOCAL] * 4, [(LOCAL, shape_of(own_block, BF16))],
        flops=10**6, moved=3 * 10**6,
    )(normed_grad, tokens_rows, out_grad, gain)
    if aligned:
        qkv_wgrad, up_wgrad = pl.pallas_call(
            functools.partial(unpack_columns, heads, size, paired, units, n_dp, n_ctx),
            out_shape=[shape_of((own, 3 * width), F32), shape_of((own, hidden), F32)],
            compiler_params=PARAMS,
            name="unpack_columns",
        )(col_wgrad)
    else:
        qkv_wgrad = (
            col_wgrad[:, :, : 3 * part].reshape(n_ctx, own, 3, part).transpose(1, 2, 0, 3)
        ).reshape(own, 3 * width).astype(F32)
        up_wgrad = (
            col_wgrad[:, :, 3 * part :].reshape(n_ctx, own, n_dp, unit_rows).transpose(1, 2, 0, 3)
        ).reshape(own, hidden).astype(F32)

    return (
        layer_out.reshape(tokens.shape), loss, input_grad.reshape(tokens.shape), gain_grad,
        shift_grad, qkv_wgrad, qk_bgrad, value_bgrad, proj_wgrad, bias_grad, up_wgrad, up_bgrad,
        down_wgrad, bias_grad,
    )


def solution(mesh):
    n_dp, n_ctx = mesh.shape["dp"], mesh.shape["ctx"]
    seq, flat = P("dp", "ctx", None), P(("dp", "ctx"))
    mat = P(("dp", "ctx"), None)
    in_specs = (
        seq, seq, P("dp", None), P("dp", "ctx"), P("dp", "ctx"),
        flat, flat, mat, flat, mat, flat, mat, flat, mat, flat,
    )
    out_specs = (seq, P(), seq, flat, flat, mat, flat, flat, mat, flat, mat, flat, mat, flat)
    return jax.shard_map(
        functools.partial(body, n_dp, n_ctx),
        mesh=mesh, in_specs=in_specs, out_specs=out_specs, check_vma=False,
    )
```

```python
import functools
import math

import jax
import jax.numpy as jnp
from jax import lax
from jax.experimental import pallas as pl
from jax.experimental.pallas import tpu as pltpu
from jax.sharding import PartitionSpec as P

HEADS = 16
ROT = 16
BLK = 128
NEG_FILL = -1000000000.0
F32 = jnp.float32
BF16 = jnp.bfloat16
PARAMS = pltpu.CompilerParams(vmem_limit_bytes=56 * 1024 * 1024)
COPIES = 128
STEP = 512
TOGETHER = 4
LAST = ((1,), (1,))
FIRST = ((0,), (0,))


def mm(a, b, dims=((1,), (0,))):
    return lax.dot_general(a, b, (dims, ((), ())), preferred_element_type=F32)


def block_spans(length, first_len):
    return [(at, 0 if at < first_len else first_len) for at in range(0, length, BLK)]


def head_stack(rows, heads, size):
    lane = lax.broadcasted_iota(jnp.int32, rows.shape, 1) // size
    parts = [jnp.where(lane == h, rows, jnp.zeros_like(rows)) for h in range(heads)]
    return parts[0] if heads == 1 else jnp.concatenate(parts, axis=0)


def head_pick(stacked, heads, size):
    rows = stacked.shape[0] // heads
    out = stacked[:rows]
    lane = lax.broadcasted_iota(jnp.int32, out.shape, 1) // size
    for h in range(1, heads):
        out = jnp.where(lane == h, stacked[h * rows : (h + 1) * rows], out)
    return out


def turn(values, cosine, sine, size):
    half = ROT // 2
    width = values.shape[1]
    place = lax.broadcasted_iota(jnp.int32, values.shape, 1) % size
    partner = jnp.where(
        place < half,
        pltpu.roll(values, width - half, 1),
        pltpu.roll(values, half, 1),
    )
    return values * cosine + partner * sine


def mask_scores(scores, start, low, first_len, seg_row, heads):
    shape = (heads * BLK, BLK)
    row = lax.rem(lax.broadcasted_iota(jnp.int32, shape, 0), BLK)
    causal = lax.broadcasted_iota(jnp.int32, shape, 1) <= row
    if low < first_len:
        last = jnp.where(causal, scores[:, start - low :], NEG_FILL)
        return last if start == low else jnp.concatenate([scores[:, : start - low], last], axis=1)
    own = jnp.transpose(jnp.broadcast_to(seg_row[:, start : start + BLK], (BLK, BLK)))
    own = jnp.concatenate([own] * heads, axis=0)
    parts = []
    for at in range(low, start + BLK, BLK):
        allowed = own == seg_row[:, at : at + BLK]
        if at == start:
            allowed = allowed & causal
        parts.append(jnp.where(allowed, scores[:, at - low : at - low + BLK], NEG_FILL))
    return jnp.concatenate(parts, axis=1)


def in_step(chains):
    chains = list(chains)
    while chains:
        chains = [chain for chain in chains if next(chain, "over") != "over"]


def grouped(items, count):
    return [items[at : at + count] for at in range(0, len(items), count)]


def standardize(rows):
    centered = rows - jnp.mean(rows, axis=-1, keepdims=True)
    variance = jnp.mean(centered * centered, axis=-1, keepdims=True)
    root = lax.rsqrt(variance + 1e-05)
    return centered * root, root


class Copier:
    def __init__(self, sems):
        self.sems, self.used = sems, 0

    def start(self, source, target):
        copy = pltpu.make_async_copy(source, target, self.sems.at[self.used])
        self.used += 1
        copy.start()
        return copy

    def rows(self, pairs, at, step):
        return [self.start(a.at[at : at + step], b.at[at : at + step]) for a, b in pairs]


def fetch_columns(copier, order, sources, targets):
    if len(targets) == 2:
        return [copier.start(a, b) for a, b in zip(sources, targets)]
    rows = sources[0].shape[0]
    return [
        copier.start(a, targets[0].at[pl.ds(pl.multiple_of(order[k] * rows, rows), rows)])
        for k, a in enumerate(sources)
    ]


def view_columns(refs, part, units):
    if len(refs) == 2:
        return refs
    return refs[0].at[:, pl.ds(0, 3 * part)], refs[0].at[:, pl.ds(3 * part, units)]


def wait_all(copies):
    for copy in copies:
        copy.wait()


def forward_kernel(
    first_len, heads, size, scale, length, step, split,
    order, gain, shift, bqkv, bup, seg_row, x_in, cos_in, sin_in, wdown_in, wproj_in, *refs,
):
    (x, cosine, sine, wdown, wproj,
     normed, q, k, v, act, slope, mixed, stat, terms, sems) = refs[-15:]
    w_in, w = refs[:split], refs[split + 9 : -15]
    (n_out, q_out, k_out, v_out, act_out, slope_out, mixed_out, stat_out, terms_out) = refs[
        split : split + 9
    ]
    copier = Copier(sems)
    part = heads * size
    wqkv, wup = view_columns(w, part, act.shape[1])
    total = x.shape[0]
    starts = range(0, total, step)
    tables = ((cos_in, cosine), (sin_in, sine))
    x_copies = {0: copier.rows([(x_in, x)], 0, step)}
    w_copies = fetch_columns(copier, order, w_in, w)
    t_copies = {0: copier.rows(tables, 0, step)}
    for at in starts[1:]:
        x_copies[at] = copier.rows([(x_in, x)], at, step)
        t_copies[at] = copier.rows(tables, at, step)
    w_copies += [copier.start(wdown_in, wdown), copier.start(wproj_in, wproj)]
    out = []
    seqs = total // length
    for origin in range(0, total, length):
        for at in range(origin, origin + length, step):
            rows = slice(at, at + step)
            wait_all(x_copies[at])
            standard, _ = standardize(x[rows, :].astype(F32))
            low = (standard * gain[...] + shift[...]).astype(BF16)
            normed[rows, :] = low
            out += copier.rows([(normed, n_out)], at, step)
            if at == 0:
                wait_all(w_copies[:split])
            full = mm(low, wqkv[...]) + bqkv[...]
            wait_all(t_copies[at])
            cos_rows, sin_rows = cosine[rows, :], sine[rows, :]
            q[rows, :] = turn(full[:, :part], cos_rows, sin_rows, size).astype(
                BF16
            ) * jnp.asarray(scale, BF16)
            k[rows, :] = turn(full[:, part : 2 * part], cos_rows, sin_rows, size).astype(BF16)
            v[rows, :] = full[:, 2 * part :].astype(BF16)
            out += copier.rows(((q, q_out), (k, k_out), (v, v_out)), at, step)
            up = mm(low, wup[...]) + bup[...]
            cdf = 0.5 * (1.0 + lax.erf(up * math.sqrt(0.5)))
            act[rows, :] = (up * cdf).astype(BF16)
            slope[rows, :] = (
                cdf + up * jnp.exp(-0.5 * up * up) * (1.0 / math.sqrt(2.0 * math.pi))
            ).astype(BF16)
            out += copier.rows(((act, act_out), (slope, slope_out)), at, step)

    def attend(seq, start, low):
        origin = seq * length
        rows = slice(origin + start, origin + start + BLK)
        cols = slice(origin + low, origin + start + BLK)
        query = head_stack(q[rows, :], heads, size)
        yield
        scores = mm(query, k[cols, :], LAST)
        yield
        scores = mask_scores(scores, start, low, first_len, seg_row[seq : seq + 1, :], heads)
        peak = jnp.max(scores, axis=1, keepdims=True)
        yield
        grown = jnp.exp(scores - peak)
        summed = jnp.sum(grown, axis=1, keepdims=True)
        yield
        probs = (grown * (1.0 / summed)).astype(BF16)
        yield
        result = mm(probs, v[cols, :])
        yield
        mixed[rows, :] = head_pick(result, heads, size).astype(BF16)
        stat[rows, :] = head_pick(
            jnp.broadcast_to(peak + jnp.log(summed), result.shape), heads, size
        )

    for spans in grouped(block_spans(length, first_len), TOGETHER):
        in_step(attend(seq, start, low) for start, low in spans for seq in range(seqs))
    out += copier.rows(((mixed, mixed_out), (stat, stat_out)), 0, total)
    wait_all(w_copies[split:])
    for at in range(0, total, step):
        rows = slice(at, at + step)
        terms[rows, :] = (mm(act[rows, :], wdown[...]) + mm(mixed[rows, :], wproj[...])).astype(
            BF16
        )
        out += copier.rows([(terms, terms_out)], at, step)
    wait_all(out)


def backward_kernel(
    first_len, heads, size, scale, length, step, cut, split,
    order, seg_row, g_in, slope_in, q_in, k_in, v_in, stat_in, cos_in, sin_in, x_in, n_in,
    wdown_in, wproj_in, *refs,
):
    (g, slope, q, k, v, stat, cosine, sine, x, normed, wdown, wproj,
     mg, ug, qg, dk, dv, sems) = refs[-18:]
    w_in, refs = refs[:split], refs[split:-18]
    back_out, gain_sum, shift_sum, up_sum, qkv_sum = refs[:5]
    held = 2 if split == 2 else 1
    col_out, w = refs[5 : len(refs) - held], refs[len(refs) - held :]
    for ref in (gain_sum, shift_sum, up_sum, qkv_sum):
        ref[...] = jnp.zeros_like(ref)
    copier = Copier(sems)
    width = heads * size
    wqkv, wup = view_columns(w, width, ug.shape[1])
    total = g.shape[0]
    loads = ((g_in, g), (slope_in, slope))
    saved = (
        (q_in, q), (k_in, k), (v_in, v), (stat_in, stat), (cos_in, cosine), (sin_in, sine)
    )
    g_copies, s_copies, x_copies = {}, {}, {}
    for at in range(0, total, step):
        g_copies[at] = copier.rows(loads[:1], at, step)
        if at == 0:
            w_copies = [copier.start(wdown_in, wdown)]
        g_copies[at] += copier.rows(loads[1:], at, step)
        if at == 0:
            w_copies.append(copier.start(wproj_in, wproj))
        if (at + step) % length == 0:
            origin = at + step - length
            s_copies[origin] = copier.rows(saved, origin, length)
            if origin == 0:
                w_copies += fetch_columns(copier, order, w_in, w)
            x_copies[origin] = copier.rows([(x_in, x)], origin, length)
    late = [copier.start(n_in, normed)]
    out = []
    for seq in range(total // length):
        origin = seq * length
        for at in range(origin, origin + length, step):
            rows = slice(at, at + step)
            wait_all(g_copies[at])
            if at == 0:
                wait_all(w_copies[:2])
            grad = g[rows, :]
            up_grad = (mm(grad, wdown[...], LAST) * slope[rows, :].astype(F32)).astype(BF16)
            ug[rows, :] = up_grad
            up_sum[...] += jnp.sum(up_grad.astype(F32), axis=0, keepdims=True)
            mg[rows, :] = mm(grad, wproj[...], LAST).astype(BF16)
    dk[...] = jnp.zeros_like(dk)
    dv[...] = jnp.zeros_like(dv)
    for origin in s_copies:
        wait_all(s_copies[origin])

    def attend(seq, start, low):
        origin = seq * length
        stop = start + BLK
        rows, cols = slice(origin + start, origin + stop), slice(origin + low, origin + stop)
        query = head_stack(q[rows, :], heads, size)
        grad = head_stack(mg[rows, :], heads, size)
        key, value = k[cols, :], v[cols, :]
        yield
        scores = mm(query, key, LAST)
        yield
        prob_grad = mm(grad, value, LAST)
        yield
        peak = stat[rows, :]
        peak = jnp.concatenate([peak[:, h * size : h * size + 1] for h in range(heads)], axis=0)
        scores = mask_scores(scores, start, low, first_len, seg_row[seq : seq + 1, :], heads)
        probs = jnp.exp(scores - peak)
        yield
        delta = jnp.sum(probs * prob_grad, axis=1, keepdims=True)
        yield
        score_grad = (probs * (prob_grad - delta)).astype(BF16)
        yield
        dq = mm(score_grad, key)
        yield
        dk[cols, :] += mm(score_grad, query, FIRST)
        yield
        dv[cols, :] += mm(probs.astype(BF16), grad, FIRST)
        yield
        dq = head_pick(dq, heads, size) * scale
        qg[rows, :width] = turn(dq, cosine[rows, :], -sine[rows, :], size).astype(BF16)

    for spans in grouped(block_spans(length, first_len), 1):
        in_step(
            attend(seq, start, low) for start, low in spans for seq in range(total // length)
        )
    for at in range(0, total, step):
        rows = slice(at, at + step)
        qg[rows, width : 2 * width] = turn(
            dk[rows, :], cosine[rows, :], -sine[rows, :], size
        ).astype(BF16)
        qg[rows, 2 * width :] = dv[rows, :].astype(BF16)
    for origin in x_copies:
        wait_all(x_copies[origin])
    wait_all(w_copies[2:])
    for at in range(0, total, step):
        rows = slice(at, at + step)
        terms = mm(ug[rows, :], wup[...], LAST) + mm(qg[rows, :], wqkv[...], LAST)
        standard, _ = standardize(x[rows, :].astype(F32))
        x[rows, :] = terms.astype(BF16)
        out += copier.rows([(x, back_out)], at, step)
        gain_sum[...] += jnp.sum(terms * standard, axis=0, keepdims=True)
        shift_sum[...] += jnp.sum(terms, axis=0, keepdims=True)
        qkv_sum[...] += jnp.sum(qg[rows, :].astype(F32), axis=0, keepdims=True)
    wait_all(late)
    weight_blocks(cut, order, normed, (qg, ug), col_out)
    wait_all(out)


def weight_blocks(cut, order, left, rights, outs):
    rows = outs[0].shape[0]
    for i, part in enumerate(outs):
        block = left[...]
        if cut:
            block = left[:, pl.ds(pl.multiple_of(order[i] * rows, rows), rows)]
        column = 0
        for right in rights:
            stop = column + right.shape[1]
            part[:, column:stop] = mm(block, right[...], FIRST).astype(part.dtype)
            column = stop


def down_kernel(cut, order, act, mixed, g, pw, *outs):
    weight_blocks(cut, order, act, (g,), outs)
    pw[...] = mm(mixed[...], g[...], FIRST).astype(BF16)


def loss_terms(branch, x, teacher, valid, bias, factor):
    full = x[...].astype(F32) + (branch[...].astype(F32) + bias[...])
    error = valid[...] * (full - teacher[...].astype(F32))
    return full, error, factor[...] * error


def loss_kernel(branch, x, teacher, valid, bias, factor, low):
    low[...] = loss_terms(branch, x, teacher, valid, bias, factor)[2].astype(BF16)


def output_kernel(branch, x, teacher, valid, bias, factor, out, grad, column, square):
    full, error, scaled = loss_terms(branch, x, teacher, valid, bias, factor)
    out[...] = full.astype(BF16)
    grad[...] = scaled
    square[...] = jnp.sum(jnp.sum(error * error, axis=0, keepdims=True), axis=1, keepdims=True)
    column[...] = jnp.sum(scaled.astype(BF16).astype(F32), axis=0, keepdims=True)


def norm_back_kernel(ng, x, og, gain, out):
    standard, root = standardize(x[...].astype(F32))
    inner = ng[...].astype(F32) * gain[...]
    out[...] = (
        og[...]
        + root
        * (
            inner
            - jnp.mean(inner, axis=-1, keepdims=True)
            - standard * jnp.mean(inner * standard, axis=-1, keepdims=True)
        )
    ).astype(BF16)


def head_of(local, ctx, heads, n_ctx, paired):
    if not paired:
        return ctx * heads + local
    return (heads * (ctx % 2) + local) * (n_ctx // 2) + ctx // 2


def pack_columns(heads, size, paired, units, n_dp, n_ctx, qkv_ref, up_ref, valid_ref, *refs):
    vectors, out_ref, small_ref = refs[:-2], refs[-2], refs[-1]
    part = heads * size
    width, unit_rows = n_ctx * part, units // n_dp
    count = jnp.sum(jnp.sum(valid_ref[...].astype(F32), axis=1, keepdims=True), axis=0, keepdims=True)
    high = jnp.floor(count * (1.0 / 128.0))
    small = [
        jnp.pad(ref[...].astype(F32).reshape(1, ref.shape[0]), ((0, 0), (0, 128 - ref.shape[0])))
        for ref in vectors
    ]
    small += [jnp.broadcast_to(a, (1, 128)) for a in (high, count - 128.0 * high)]
    small = jnp.concatenate(small, axis=0).astype(BF16)
    for j in range(small_ref.shape[0]):
        small_ref[j] = small
    for j in range(n_ctx):
        for p in range(3):
            at = [p * width + head_of(h, j, heads, n_ctx, paired) * size for h in range(heads)]
            out_ref[j, :, p * part : (p + 1) * part] = jnp.concatenate(
                [qkv_ref[:, a : a + size] for a in at], axis=1
            )
        for i in range(n_dp):
            at = (i * n_ctx + j) * unit_rows
            out_ref[j, :, 3 * part + i * unit_rows : 3 * part + (i + 1) * unit_rows] = up_ref[
                :, at : at + unit_rows
            ]


def vector_kernel(own, heads, size, n_dp, n_ctx, place, small, gain, shift, qkv_b, up_b, full):
    rows = [small[d].astype(F32) for d in range(n_dp * n_ctx)]
    gain[...] = jnp.concatenate([row[0:1, :own] for row in rows], axis=1)
    shift[...] = jnp.concatenate([row[1:2, :own] for row in rows], axis=1)
    full[...] = jnp.concatenate([row[4:5, : 3 * own] for row in rows], axis=1)
    core, chip = place[0], place[1]
    part, third = heads * size, full.shape[1] // 3
    for p in range(3):
        pairs = []
        for h in range(heads):
            head = (heads * core + h) * (n_ctx // 2) + chip
            at = pl.multiple_of(p * third + (head // 2) * 2 * size, 2 * size)
            pairs.append(full[:, pl.ds(at, 2 * size)])
        low = jnp.concatenate([pair[:, :size] for pair in pairs], axis=1)
        high = jnp.concatenate([pair[:, size:] for pair in pairs], axis=1)
        qkv_b[:, p * part : (p + 1) * part] = jnp.where(lax.rem(chip, 2) == 0, low, high)
    me = 2 * chip + core
    block = up_b.shape[1] // n_dp
    for i in range(n_dp):
        up_b[:, i * block : (i + 1) * block] = small[i * n_ctx + me].astype(F32)[5:6, :block]


def unpack_columns(heads, size, paired, units, n_dp, n_ctx, in_ref, qkv_ref, up_ref):
    part = heads * size
    width, unit_rows = n_ctx * part, units // n_dp
    held = {
        head_of(h, j, heads, n_ctx, paired): (j, h) for j in range(n_ctx) for h in range(heads)
    }
    for p in range(3):
        for first in range(0, n_ctx * heads, heads):
            pieces = []
            for head in range(first, first + heads):
                j, h = held[head]
                pieces.append(in_ref[j, :, p * part : (p + 1) * part][:, h * size : (h + 1) * size])
            qkv_ref[:, p * width + first * size : p * width + (first + heads) * size] = (
                jnp.concatenate(pieces, axis=1).astype(F32)
            )
    for j in range(n_ctx):
        for i in range(n_dp):
            at = (i * n_ctx + j) * unit_rows
            up_ref[:, at : at + unit_rows] = in_ref[
                j, :, 3 * part + i * unit_rows : 3 * part + (i + 1) * unit_rows
            ].astype(F32)


def shape_of(dims, dtype):
    return jax.ShapeDtypeStruct(dims, dtype)


def row_spec(rows, *dims):
    return pl.BlockSpec((rows,) + dims, lambda s: (s,) + (0,) * len(dims))


def whole_spec(*dims):
    return pl.BlockSpec(dims, lambda s: (0,) * len(dims))


HBM = pl.BlockSpec(memory_space=pl.ANY)
LOCAL = pl.BlockSpec(memory_space=pltpu.VMEM)
SCALAR = pl.BlockSpec(memory_space=pltpu.SMEM)


def kernel_call(kernel, name, in_specs, out, scratch=(), flops=0, moved=0, grid=None):
    return pl.pallas_call(
        kernel,
        in_specs=in_specs,
        out_specs=[spec for spec, _ in out],
        out_shape=[shape for _, shape in out],
        scratch_shapes=list(scratch),
        compiler_params=PARAMS,
        cost_estimate=pl.CostEstimate(flops=flops, bytes_accessed=moved, transcendentals=0),
        name=name,
        **({"grid": grid} if grid else {}),
    )


def gather_dp(block, n_dp, me_dp):
    out = jnp.zeros((n_dp,) + block.shape, block.dtype)
    out = lax.dynamic_update_index_in_dim(out, block, me_dp, 0)
    for k in range(1, n_dp):
        pairs = [(i, i ^ k) for i in range(n_dp)]
        other = lax.ppermute(block, "dp", pairs)
        out = lax.dynamic_update_index_in_dim(out, other, me_dp ^ k, 0)
    return out.reshape((n_dp * block.shape[0],) + block.shape[1:])


def reduce_blocks(terms, cut, n_dp, me_dp, later=None):
    if not cut:
        return reduce_dp(terms[0], n_dp, me_dp), later
    parts = [
        lax.ppermute(terms[k], "dp", [(i, i ^ k) for i in range(n_dp)]) for k in range(1, n_dp)
    ]
    if later is not None:
        parts[0], later = lax.optimization_barrier((parts[0], later))
    total = terms[0]
    for part in parts:
        total = total + part.astype(F32)
    return total, later


def reduce_dp(terms, n_dp, me_dp):
    rows = terms.shape[0] // n_dp
    blocks = terms.reshape((n_dp, rows) + terms.shape[1:])
    total = lax.dynamic_index_in_dim(blocks, me_dp, 0, keepdims=False).astype(F32)
    for k in range(1, n_dp):
        pairs = [(i, i ^ k) for i in range(n_dp)]
        block = lax.dynamic_index_in_dim(blocks, me_dp ^ k, 0, keepdims=False)
        total = total + lax.ppermute(block, "dp", pairs).astype(F32)
    return total


def own_vectors(
    small, own, part, units, unit_rows, n_dp, n_ctx, me_ctx, paired, heads, size, me_core, me_chip
):
    width = n_dp * n_ctx * own
    gain = small[:, 0, :own].reshape(1, width)
    shift = small[:, 1, :own].reshape(1, width)
    qkv_b = small[:, 4, : 3 * own]
    if paired:
        qkv_b = lax.dynamic_slice(
            qkv_b.reshape(3, 2, heads, n_ctx // 2, size), (0, me_core, 0, me_chip, 0),
            (3, 1, heads, 1, size),
        )
    else:
        qkv_b = lax.dynamic_index_in_dim(qkv_b.reshape(3, n_ctx, part), me_ctx, 1)
    qkv_b = qkv_b.reshape(1, 3 * part)
    up_b = small[:, 5, :unit_rows].reshape(n_dp, n_ctx, unit_rows)
    up_b = lax.dynamic_index_in_dim(up_b, me_ctx, 1, keepdims=False).reshape(1, units)
    return gain, shift, qkv_b, up_b


def body(
    n_dp, n_ctx,
    tokens, teacher, segments, positions, valid_mask,
    norm_gain, norm_bias, qkv_weight, qkv_bias, proj_weight, proj_bias,
    up_weight, up_bias, down_weight, down_bias,
):
    seqs, local_len, width = tokens.shape
    length = segments.shape[1]
    rows = seqs * local_len
    all_rows = seqs * length
    n_all = n_dp * n_ctx
    first_len = length // 2 + local_len
    heads = HEADS // n_ctx
    size = width // HEADS
    part = heads * size
    hidden = up_weight.shape[1]
    units = hidden // n_ctx
    unit_rows = down_weight.shape[0]
    own = width // n_all
    scale = 1.0 / math.sqrt(size)
    me_dp = lax.axis_index("dp")
    me_ctx = lax.axis_index("ctx")
    both = ("dp", "ctx")
    aligned = part % 128 == 0 and unit_rows % 128 == 0 and own % 16 == 0
    paired = aligned and 2 * own == size and 2 * heads == n_dp
    me_core, me_chip = me_ctx % 2, me_ctx // 2
    swap = [(j, j ^ 1) for j in range(n_ctx)]

    to_plan = [(n_dp * j + i, i * n_ctx + j) for i in range(n_dp) for j in range(n_ctx)]
    from_plan = [(b, a) for a, b in to_plan]
    valid = valid_mask.astype(F32).reshape(rows, 1)
    vectors = [norm_gain, norm_bias, proj_bias, down_bias, qkv_bias, up_bias]
    total_cols = 3 * part + units
    if aligned:
        cols, small = pl.pallas_call(
            functools.partial(pack_columns, heads, size, paired, units, n_dp, n_ctx),
            out_shape=[
                shape_of((n_ctx, own, total_cols), BF16), shape_of((n_all, 8, 128), BF16)
            ],
            compiler_params=PARAMS,
            name="pack_columns",
        )(qkv_weight, up_weight, valid_mask, *vectors)
    else:
        count = jnp.sum(valid_mask)
        small = jnp.stack(
            [jnp.pad(a, (0, 128 - a.shape[0])) for a in vectors]
            + [jnp.broadcast_to(a.astype(BF16), (128,)) for a in (count // 128, count % 128)]
        )
        small = jnp.broadcast_to(small[None], (n_all, 8, 128))
        qkv_cols = qkv_weight.reshape(own, 3, n_ctx, part).transpose(2, 0, 1, 3)
        up_cols = up_weight.reshape(own, n_dp, n_ctx, unit_rows).transpose(2, 0, 1, 3)
        cols = jnp.concatenate(
            [
                qkv_cols.reshape(n_ctx, own, 3 * part), up_cols.reshape(n_ctx, own, units),
            ],
            axis=2,
        )
    tied = jnp.concatenate([down_weight, proj_weight], axis=0) if paired else down_weight
    cols, tied = lax.optimization_barrier((cols, tied))
    x_rows = lax.all_gather(tokens, "ctx", axis=1, tiled=True).reshape(all_rows, width)
    cols = lax.all_to_all(cols, "ctx", 0, 0, tiled=True).reshape(n_ctx * own, total_cols)
    cols, segments, small = lax.optimization_barrier((cols, segments, small))
    small = lax.all_to_all(small, both, 0, 0, tiled=True)
    if paired and 2 * size == 128 and (n_ctx // 2) % 2 == 0:
        gain, shift, qkv_b, up_b = kernel_call(
            functools.partial(vector_kernel, own, heads, size, n_dp, n_ctx), "vector_kernel",
            [SCALAR, LOCAL],
            [(LOCAL, shape_of((1, a), F32)) for a in (width, width, 3 * part, units)],
            [pltpu.VMEM((1, 3 * width), F32)], flops=10**6, moved=10**5,
        )(jnp.stack([me_core, me_chip]).astype(jnp.int32), small)
    else:
        gain, shift, qkv_b, up_b = own_vectors(
            small.astype(F32), own, part, units, unit_rows, n_dp, n_ctx, me_ctx, paired, heads,
            size, me_core, me_chip,
        )
    small = small.astype(F32)
    out_bias = (small[:, 2, :own] + small[:, 3, :own]).reshape(1, width)
    valid_count = 128.0 * jnp.sum(small[:, 6, 0]) + jnp.sum(small[:, 7, 0])
    sliced = (3 * part) % 128 == 0 and units % 128 == 0
    order = jnp.stack([me_dp ^ k for k in range(n_dp)]).astype(jnp.int32)
    if sliced and n_dp > 2:
        w_split = [cols] + [
            lax.ppermute(cols, "dp", [(i, i ^ k) for i in range(n_dp)]) for k in range(1, n_dp)
        ]
        w_scratch = [pltpu.VMEM((width, total_cols), BF16)]
    else:
        w_cols = gather_dp(cols, n_dp, me_dp)
        w_split = [w_cols[:, : 3 * part], w_cols[:, 3 * part : 3 * part + units]]
        w_scratch = [pltpu.VMEM(a.shape, BF16) for a in w_split]
    token = jnp.arange(length, dtype=jnp.int32)
    half = ROT // 2
    lane = jnp.arange(part, dtype=jnp.int32) % size
    steps = jnp.arange(half, dtype=F32)
    inverse = jnp.power(10000.0, -2.0 * steps / ROT)
    lane_inverse = jnp.where(lane < ROT, inverse[lane % half], 0.0)
    same = segments[:, :, None] == segments[:, None, :]
    before = token[None, None, :] < token[None, :, None]
    in_doc = jnp.sum((same & before).astype(F32), axis=2)
    angles = in_doc.reshape(all_rows, 1) * lane_inverse[None, :]
    cosine = jnp.cos(angles)
    sine = jnp.sin(angles) * jnp.where(lane < half, -1.0, 1.0)

    tied = gather_dp(tied, n_dp, me_dp).reshape(n_dp, -1, width)
    w_down = tied[:, :unit_rows].reshape(units, width)
    if paired:
        halves = tied[:, unit_rows:].reshape(2, heads, own, width)
        keep = lax.dynamic_index_in_dim(halves, me_core, 0, keepdims=False)
        got = lax.ppermute(
            lax.dynamic_index_in_dim(halves, 1 - me_core, 0, keepdims=False), "ctx", swap
        )
        w_proj = jnp.stack(
            [jnp.where(me_core == 0, keep, got), jnp.where(me_core == 0, got, keep)], axis=1
        ).reshape(part, width)
    else:
        w_proj = gather_dp(lax.ppermute(proj_weight, both, to_plan), n_dp, me_dp)

    def wide(columns, dtype=BF16):
        return pltpu.VMEM((all_rows, columns), dtype)

    def store(columns, dtype=BF16):
        return (HBM, shape_of((all_rows, columns), dtype))

    weights = [pltpu.VMEM((units, width), BF16), pltpu.VMEM((part, width), BF16)]
    sems = pltpu.SemaphoreType.DMA((COPIES,))
    normed, query, key, value, act, slope, mixed, stat, terms = kernel_call(
        functools.partial(
            forward_kernel, first_len, heads, size, scale, length, STEP, len(w_split)
        ),
        "forward_kernel",
        [SCALAR] + [LOCAL] * 5 + [HBM] * (5 + len(w_split)),
        [
            store(width), store(part), store(part), store(part), store(units), store(units),
            store(part), store(part, F32), store(width),
        ],
        [
            *w_scratch, wide(width), wide(part, F32), wide(part, F32), *weights,
            wide(width), wide(part), wide(part), wide(part), wide(units), wide(units),
            wide(part), wide(part, F32), wide(width), sems,
        ],
        flops=10 * 10**9, moved=2 * 10**7,
    )(
        order, gain, shift, qkv_b, up_b, segments, x_rows, cosine, sine, w_down, w_proj, *w_split
    )
    branch = lax.psum_scatter(
        terms.reshape(seqs, length, width), "ctx", scatter_dimension=1, tiled=True
    ).reshape(rows, width)

    total_tokens = seqs * n_dp * length
    factor = (total_tokens / valid_count).reshape(1, 1)
    tokens_rows = tokens.reshape(rows, width)
    own_block = (rows, width)
    loss_in = (branch, tokens_rows, teacher.reshape(rows, width), valid, out_bias, factor)
    (low,) = kernel_call(
        loss_kernel, "loss_kernel", [LOCAL] * 6, [(LOCAL, shape_of(own_block, BF16))],
        flops=10**6, moved=2 * 10**6,
    )(*loss_in)
    low, *loss_in = lax.optimization_barrier((low, *loss_in))
    layer_out, out_grad, column, square = kernel_call(
        output_kernel, "output_kernel", [LOCAL] * 6,
        [
            (LOCAL, shape_of(own_block, BF16)), (LOCAL, shape_of(own_block, F32)),
            (LOCAL, shape_of((1, width), F32)), (LOCAL, shape_of((1, 1), F32)),
        ],
        flops=10**6, moved=3 * 10**6,
    )(*loss_in)

    grads = lax.all_gather(
        low.reshape(tokens.shape), "ctx", axis=1, tiled=True
    ).reshape(all_rows, width)
    cut = (width // n_dp) % 128 == 0 and unit_rows % 128 == 0

    def blocks_of(rows_out, columns):
        if not cut:
            return [(LOCAL, shape_of((rows_out, columns), BF16))]
        block = (rows_out // n_dp, columns)
        return [(LOCAL, shape_of(block, BF16 if k else F32)) for k in range(n_dp)]

    back, gain_sum, shift_sum, up_bsum, qkv_bsum, *col_terms = kernel_call(
        functools.partial(
            backward_kernel, first_len, heads, size, scale, length, STEP, cut, len(w_split)
        ),
        "backward_kernel",
        [SCALAR, LOCAL] + [HBM] * (12 + len(w_split)),
        [
            store(width),
            *[(LOCAL, shape_of((1, a), F32)) for a in (width, width, units, 3 * part)],
            *blocks_of(width, 3 * part + units),
        ],
        [
            *w_scratch, wide(width), wide(units), wide(part), wide(part), wide(part),
            wide(part, F32), wide(part, F32), wide(part, F32), wide(width), wide(width),
            *weights, wide(part), wide(units), wide(3 * part), wide(part, F32),
            wide(part, F32), sems,
        ],
        flops=12 * 10**9, moved=2 * 10**7,
    )(
        order, segments, grads, slope, query, key, value, stat, cosine, sine, x_rows, normed,
        w_down, w_proj, *w_split,
    )
    normed_grad = lax.psum_scatter(
        back.reshape(seqs, length, width), "ctx", scatter_dimension=1, tiled=True
    ).reshape(rows, width)

    col_wgrad, act = reduce_blocks(col_terms, cut, n_dp, me_dp, act)
    col_wgrad = col_wgrad.astype(BF16)

    if paired:
        qkv_bsum = lax.dynamic_update_slice(
            jnp.zeros((3, 2, heads, n_ctx // 2, size), F32),
            qkv_bsum.reshape(3, 1, heads, 1, size), (0, me_core, 0, me_chip, 0),
        )
    else:
        qkv_bsum = lax.dynamic_update_slice(
            jnp.zeros((3, n_ctx, part), F32), qkv_bsum.reshape(3, 1, part), (0, me_ctx, 0)
        )
    up_bsum = lax.dynamic_update_slice(
        jnp.zeros((n_dp, n_ctx, unit_rows), F32), up_bsum.reshape(n_dp, 1, unit_rows),
        (0, me_ctx, 0),
    )
    parts = [
        gain_sum.reshape(n_all, own), shift_sum.reshape(n_all, own),
        column.reshape(n_all, own), qkv_bsum[2].reshape(n_all, own),
        qkv_bsum[:2].reshape(n_all, 2 * own), up_bsum.reshape(n_all, unit_rows),
        jnp.broadcast_to(square, (n_all, 1)),
    ]
    sums = jnp.concatenate(parts, axis=1)
    sums = jnp.pad(sums, ((0, 0), (0, -sums.shape[1] % 128)))
    sums, act = lax.optimization_barrier((sums, act))
    sums = lax.all_to_all(sums, both, 0, 0, tiled=True)
    col_wgrad, sums = lax.optimization_barrier((col_wgrad, sums))
    col_wgrad = lax.all_to_all(
        col_wgrad.reshape(n_ctx, own, 3 * part + units), "ctx", 0, 0, tiled=True
    )
    sums = jnp.sum(sums, axis=0)
    gain_grad, shift_grad, bias_grad, value_bgrad = (
        sums[k * own : (k + 1) * own] for k in range(4)
    )
    qk_bgrad = sums[4 * own : 6 * own]
    up_bgrad = sums[6 * own : 6 * own + unit_rows]
    loss = sums[6 * own + unit_rows] / (valid_count * width)

    proj_wgrad, *down_terms = kernel_call(
        functools.partial(down_kernel, cut), "down_kernel", [SCALAR] + [LOCAL] * 3,
        [(LOCAL, shape_of((part, width), BF16)), *blocks_of(units, width)],
        flops=10**6, moved=10**5,
    )(order, act, mixed, grads)
    down_wgrad, _ = reduce_blocks(down_terms, cut, n_dp, me_dp)
    if paired:
        halves = proj_wgrad.reshape(heads, 2, own, width)
        keep = lax.dynamic_index_in_dim(halves, me_core, 1, keepdims=False)
        got = lax.ppermute(
            lax.dynamic_index_in_dim(halves, 1 - me_core, 1, keepdims=False), "ctx", swap
        )
        proj_wgrad = jnp.concatenate(
            [jnp.where(me_core == 0, keep, got), jnp.where(me_core == 0, got, keep)], axis=0
        ).reshape(n_dp * own, width)
        proj_wgrad = reduce_dp(proj_wgrad, n_dp, me_dp)
    else:
        proj_wgrad = reduce_dp(proj_wgrad, n_dp, me_dp)
        proj_wgrad = lax.ppermute(proj_wgrad.astype(BF16), both, from_plan).astype(F32)

    (input_grad,) = kernel_call(
        norm_back_kernel, "norm_back_kernel", [LOCAL] * 4, [(LOCAL, shape_of(own_block, BF16))],
        flops=10**6, moved=3 * 10**6,
    )(normed_grad, tokens_rows, out_grad, gain)
    if aligned:
        qkv_wgrad, up_wgrad = pl.pallas_call(
            functools.partial(unpack_columns, heads, size, paired, units, n_dp, n_ctx),
            out_shape=[shape_of((own, 3 * width), F32), shape_of((own, hidden), F32)],
            compiler_params=PARAMS,
            name="unpack_columns",
        )(col_wgrad)
    else:
        qkv_wgrad = (
            col_wgrad[:, :, : 3 * part].reshape(n_ctx, own, 3, part).transpose(1, 2, 0, 3)
        ).reshape(own, 3 * width).astype(F32)
        up_wgrad = (
            col_wgrad[:, :, 3 * part :].reshape(n_ctx, own, n_dp, unit_rows).transpose(1, 2, 0, 3)
        ).reshape(own, hidden).astype(F32)

    return (
        layer_out.reshape(tokens.shape), loss, input_grad.reshape(tokens.shape), gain_grad,
        shift_grad, qkv_wgrad, qk_bgrad, value_bgrad, proj_wgrad, bias_grad, up_wgrad, up_bgrad,
        down_wgrad, bias_grad,
    )


def solution(mesh):
    n_dp, n_ctx = mesh.shape["dp"], mesh.shape["ctx"]
    seq, flat = P("dp", "ctx", None), P(("dp", "ctx"))
    mat = P(("dp", "ctx"), None)
    in_specs = (
        seq, seq, P("dp", None), P("dp", "ctx"), P("dp", "ctx"),
        flat, flat, mat, flat, mat, flat, mat, flat, mat, flat,
    )
    out_specs = (seq, P(), seq, flat, flat, mat, flat, flat, mat, flat, mat, flat, mat, flat)
    return jax.shard_map(
        functools.partial(body, n_dp, n_ctx),
        mesh=mesh, in_specs=in_specs, out_specs=out_specs, check_vma=False,
    )
```
